32 devices in a mesh: rep: 2 (over y), dp: 16 (over z, x, core).
Axes of the slice: x: 2, y: 2, z: 4, core: 2. Of those that a mesh axis runs over, the one named last changes fastest.
Arguments:
- images: bfloat16 [256, 2, 1280], P(('rep', 'dp')), may hold values from -6 to 6
- weight: bfloat16 [1280, 8192], P(None, 'dp'), may hold values from -0.3354102 to 0.3354102, as said below
Outputs:
- image_grad: float32 [256, 2, 1280], P(('rep', 'dp'))
- weight_grad: float32 [1280, 8192], P(None, 'dp')
The draws below stay inside these ranges and needn't reach their ends.
Inputs may be any that keep to these rules, and one draw needn't show every extreme that they name: `weight`: a projection whose columns have different scales.
All inputs are finite; a program needn't handle non-finite values.
Results may differ from the reference program's by a relative error of at most 0.0021.
Values may be sent and summed in bfloat16 or wider, within the bound.
No kernel may reach another device: no remote copies, remote signals or barrier semaphores. Data moves between devices by JAX's collectives and lax.ppermute only.
A program may use at most 64 MiB of HBM per device.

```python
import jax
import jax.numpy as jnp
from jax import lax

D_IN = 1280
EMB = 8192
IMG_DEV = 8
IMAGES = 256
N_REP = 2
N_DP = 16


def draw_weight(key, part):
    key_values = jax.random.fold_in(key, 11)
    key_scales = jax.random.fold_in(key, 23)
    values = jnp.clip(jax.random.normal(key_values, (D_IN, EMB), jnp.float32), -4.0, 4.0)
    scales = jnp.exp(jax.random.uniform(key_scales, (1, EMB), jnp.float32, jnp.log(0.3), jnp.log(3.0)))
    return (values * scales / jnp.sqrt(jnp.float32(D_IN))).astype(jnp.bfloat16)


def levels(key, dims, shards, smallest, largest):
    level, own = 1.0, jax.random.fold_in(key, 6)
    for dim, parts in shards:
        draws = jnp.exp(jax.random.uniform(jax.random.fold_in(own, dim), (parts,), jnp.float32, smallest / len(shards), largest / len(shards)))
        level = level * jnp.repeat(draws, dims[dim] // parts).reshape([-1 if axis == dim else 1 for axis in range(len(dims))])
    return level


def scatter_about(rng, dims, scale, limit, shards=(), kind=jnp.bfloat16):
    array = scale * jax.random.normal(rng, dims, jnp.float32)
    if shards:
        array = array * levels(rng, dims, shards, -0.22, 0.18)
    return jnp.clip(array, -limit, limit).astype(kind)


def setup_inputs(seed: int = 0) -> dict:
    splits = jax.random.split(jax.random.key(seed), 3)
    images = scatter_about(splits[0], (IMAGES, 2, D_IN), 1.0, 6.0, ((0, 32),))
    weight = draw_weight(jax.random.fold_in(splits[2], 71), 0)
    return dict(images=images, weight=weight)


invariance_weight = 25.0
variance_weight = 25.0
covariance_weight = 1.0
loss_scale = 8192.0
epsilon_var = 0.0001

def group_grads(weight, rows):
    embed = jnp.einsum('mvk,ki->mvi', rows.astype(jnp.float32), weight.astype(jnp.float32))
    count = rows.shape[0]
    grad_scale = loss_scale / N_REP
    column_mean = lax.optimization_barrier(jnp.mean(embed, axis=0))
    centred = embed - column_mean
    centred_bf = centred.astype(jnp.bfloat16)
    variance = lax.optimization_barrier(jnp.sum(centred * centred, axis=0)) / (count - 1)
    spread = jnp.sqrt(variance + epsilon_var)
    coeff = grad_scale * 4.0 * covariance_weight / (EMB * (count - 1))
    block_width = EMB // N_DP

    def block_terms(index):
        begin = index * block_width
        own_cols = lax.dynamic_slice_in_dim(centred_bf, begin, block_width, 2)
        covariance = jnp.einsum('mvi,mvj->vij', own_cols.astype(jnp.float32), centred_bf.astype(jnp.float32))
        rowpos = lax.broadcasted_iota(jnp.int32, (1, block_width, EMB), 1) + begin
        colpos = lax.broadcasted_iota(jnp.int32, (1, block_width, EMB), 2)
        cov_grad = jnp.where(rowpos == colpos, 0.0, covariance / (count - 1)) * coeff
        return jnp.einsum('mvj,vij->mvi', centred_bf.astype(jnp.float32), cov_grad, precision=lax.Precision.HIGHEST)
    blocks = lax.map(block_terms, jnp.arange(N_DP, dtype=jnp.int32))
    cov_term = jnp.transpose(blocks, (1, 2, 0, 3)).reshape(count, 2, EMB)
    view_gap = embed[:, 0] - embed[:, 1]
    inv_term = jnp.stack([view_gap, -view_gap], axis=1) * (grad_scale * 2.0 * invariance_weight / (count * EMB))
    var_term = jnp.where(spread < 1.0, -grad_scale * variance_weight / (EMB * (count - 1)) / spread, 0.0) * centred
    feature_grad = (inv_term + var_term + cov_term).astype(jnp.bfloat16)
    local_grad = jnp.einsum('mvk,mvi->ki', rows.astype(jnp.float32), feature_grad.astype(jnp.float32))
    image_part = jnp.einsum('mvi,ki->mvk', feature_grad.astype(jnp.float32), weight.astype(jnp.float32))
    return (local_grad, image_part)

def reference(images, weight):
    grouped = images.reshape(N_REP, IMG_DEV * N_DP, 2, D_IN)

    def advance(running, rows):
        local_grad, image_part = group_grads(weight, rows)
        return (running + local_grad, image_part)
    weight_grad, image_parts = lax.scan(advance, jnp.zeros((D_IN, EMB), jnp.float32), grouped)
    return (image_parts.reshape(IMAGES, 2, D_IN), weight_grad)
```

```python
import jax
import jax.numpy as jnp
from jax import lax
from jax.sharding import PartitionSpec as P

invariance_weight = 25.0
variance_weight = 25.0
covariance_weight = 1.0
loss_scale = 8192.0
epsilon_var = 0.0001


def spread_copies(block, axis):
    copies = jnp.broadcast_to(block, (lax.axis_size(axis),) + block.shape)
    return lax.all_to_all(copies, axis, 0, 0, tiled=True)


def others(block, axis):
    size = lax.axis_size(axis)
    return [
        lax.ppermute(block, axis, [(i, (i + shift) % size) for i in range(size)])
        for shift in range(1, size)
    ]


def shards(images, weight):
    groups = lax.axis_size("rep")
    owners = lax.axis_size("dp")
    own_images, views, depth = images.shape
    block_width = weight.shape[1]
    features = block_width * owners
    count = own_images * owners
    grad_scale = loss_scale / groups

    rows = spread_copies(jnp.swapaxes(images, 0, 1), "dp")
    rows = jnp.swapaxes(rows, 0, 1).reshape(views, count, depth)
    z = jnp.einsum("vmk,ki->vmi", rows, weight, preferred_element_type=jnp.float32)
    centred = z - jnp.mean(z, axis=1, keepdims=True)
    centred_bf = centred.astype(jnp.bfloat16)
    gram_part = jnp.einsum(
        "vmi,vni->mvn", centred_bf, centred_bf, preferred_element_type=jnp.float32
    )
    gram_part = gram_part.reshape(owners, own_images, views, count)
    gram_own = jnp.sum(lax.all_to_all(gram_part, "dp", 0, 0, tiled=True), axis=0)
    gram = spread_copies(gram_own, "dp").reshape(count, views, count)

    rows_others = others(rows, "rep")

    variance = jnp.sum(centred * centred, axis=1, keepdims=True) / (count - 1)
    spread = jnp.sqrt(variance + epsilon_var)
    coeff = grad_scale * 4.0 * covariance_weight / (features * (count - 1))
    centred_wide = centred_bf.astype(jnp.float32)
    diag_cov = jnp.sum(centred_wide * centred_wide, axis=1, keepdims=True) / (count - 1)
    through = jnp.einsum("mvn,vni->vmi", gram, centred_wide, precision=lax.Precision.HIGHEST)
    cov_term = through * (coeff / (count - 1)) - coeff * diag_cov * centred_wide
    inv_term = (z - z[::-1]) * (grad_scale * 2.0 * invariance_weight / (count * features))
    var_term = (
        jnp.where(
            spread < 1.0, -grad_scale * variance_weight / (features * (count - 1)) / spread, 0.0
        )
        * centred
    )
    feature_grad = (inv_term + var_term + cov_term).astype(jnp.bfloat16)

    grad_others = others(feature_grad, "rep")
    image_part = jnp.einsum("vmi,ki->mvk", feature_grad, weight, preferred_element_type=jnp.float32)
    image_part = image_part.astype(jnp.bfloat16).reshape(owners, own_images, views, depth)
    image_parts = lax.all_to_all(image_part, "dp", 0, 0, tiled=True)
    image_grad = jnp.sum(image_parts.astype(jnp.float32), axis=0)

    all_rows = jnp.concatenate([rows] + rows_others, axis=1)
    all_grads = jnp.concatenate([feature_grad] + grad_others, axis=1)
    weight_grad = jnp.einsum(
        "vmk,vmi->ki", all_rows, all_grads, preferred_element_type=jnp.float32
    )
    return (image_grad, weight_grad)


def solution(mesh):
    return jax.shard_map(
        shards,
        mesh=mesh,
        in_specs=(P(("rep", "dp"), None, None), P(None, "dp")),
        out_specs=(P(("rep", "dp"), None, None), P(None, "dp")),
        check_vma=False,
    )
```

```python
import functools

import jax
import jax.numpy as jnp
from jax import lax
from jax.experimental import pallas as pl
from jax.experimental.pallas import tpu as pltpu
from jax.sharding import PartitionSpec as P

invariance_weight = 25.0
variance_weight = 25.0
covariance_weight = 1.0
loss_scale = 8192.0
epsilon_var = 0.0001

F32 = jnp.float32
BF16 = jnp.bfloat16
VMEM = pl.BlockSpec(memory_space=pltpu.VMEM)
SMEM = pl.BlockSpec(memory_space=pltpu.SMEM)
QUAD = 4


def swap(block, axis, bits):
    return lax.ppermute(block, axis, [(i, i ^ bits) for i in range(lax.axis_size(axis))])


def moments(z, views):
    return [z[v] - jnp.mean(z[v], axis=0, keepdims=True) for v in range(views)]


def nt_dot(a, b):
    return lax.dot_general(a, b, (((1,), (1,)), ((), ())), preferred_element_type=F32)


def embed_kernel(me_ref, a_ref, b_ref, ca_ref, cb_ref, w_ref, rows_ref, z_ref, gram_ref):
    me = me_ref[0]
    outer, lot, depth = a_ref.shape
    views, count, width = z_ref.shape
    own = lot // views
    for low, ref in enumerate((a_ref, ca_ref, b_ref, cb_ref)):
        for high in range(outer):
            device = (high * QUAD + low) ^ me
            rows_ref[pl.ds(pl.multiple_of(device * lot, lot), lot), :] = ref[high]
    z = jnp.dot(rows_ref[...], w_ref[...], preferred_element_type=F32)
    z = jnp.swapaxes(z.reshape(count // own, views, own, width), 0, 1)
    z = z.reshape(views, count, width)
    z_ref[...] = z
    quarter = views * count // QUAD
    per_view = count // quarter
    for v, c in enumerate(moments(z, views)):
        c = c.astype(BF16)
        gram = nt_dot(c, c)
        for part in range(per_view):
            gram_ref[(v * per_view + part) ^ (me % QUAD)] = gram[part * quarter:(part + 1) * quarter]


def grads_kernel(scale, features, me_ref, g0_ref, g1_ref, g2_ref, g3_ref, z_ref, w_ref,
                 grad_ref, keep_ref, send_ref, gram_ref):
    me = me_ref[0]
    views, count, width = z_ref.shape
    for part, ref in enumerate((g0_ref, g1_ref, g2_ref, g3_ref)):
        gram_ref[part ^ (me % QUAD)] = ref[...]
    gram = gram_ref[...].reshape(views, count, count)
    z = z_ref[...]
    coeff = scale * 4.0 * covariance_weight / (features * (count - 1))
    grads = []
    for v, centred in enumerate(moments(z, views)):
        variance = jnp.sum(centred * centred, axis=0, keepdims=True) / (count - 1)
        spread = jnp.sqrt(variance + epsilon_var)
        centred_bf = centred.astype(BF16)
        wide = centred_bf.astype(F32)
        diag_cov = jnp.sum(wide * wide, axis=0, keepdims=True) / (count - 1)
        rest = gram[v]
        through = 0.0
        for _ in range(3):
            piece = rest.astype(BF16)
            rest = rest - piece.astype(F32)
            through = through + jnp.dot(piece, centred_bf, preferred_element_type=F32)
        cov_term = through * (coeff / (count - 1)) - coeff * diag_cov * wide
        inv_term = (z[v] - z[1 - v]) * (scale * 2.0 * invariance_weight / (count * features))
        var_coeff = jnp.where(
            spread < 1.0, -scale * variance_weight / (features * (count - 1)) / spread, 0.0
        )
        grads.append(inv_term + var_coeff * centred + cov_term)
    lot = keep_ref.shape[1]
    own = lot // views
    devices = count // own
    grad = jnp.stack(grads).reshape(views, devices, own, width)
    grad = jnp.swapaxes(grad, 0, 1).reshape(devices * lot, width).astype(BF16)
    grad_ref[...] = grad
    part = nt_dot(grad, w_ref[...]).reshape(devices, lot, w_ref.shape[0])
    outer = devices // QUAD
    for device in range(devices):
        rel = device ^ me
        low, high = rel % QUAD, rel // QUAD
        slot = (low // 2) * outer + high
        piece = part[device]

        @pl.when(low % 2 == 0)
        def _():
            keep_ref[slot] = piece

        @pl.when(low % 2 == 1)
        def _():
            send_ref[slot] = piece.astype(BF16)


def weight_kernel(*refs):
    out_ref = refs[-1]
    pairs = len(refs) // 2
    total = None
    for rows_ref, grad_ref in zip(refs[:pairs], refs[pairs:2 * pairs]):
        part = lax.dot_general(
            rows_ref[...], grad_ref[...], (((0,), (0,)), ((), ())), preferred_element_type=F32
        )
        total = part if total is None else total + part
    out_ref[...] = total


def call(kernel, out_shape, specs, scratch=()):
    return pl.pallas_call(
        kernel,
        out_shape=out_shape,
        in_specs=specs,
        out_specs=jax.tree.map(lambda _: VMEM, out_shape),
        scratch_shapes=list(scratch),
        compiler_params=pltpu.CompilerParams(vmem_limit_bytes=40 * 1024 * 1024),
    )


def shards(images, weight):
    groups = lax.axis_size("rep")
    owners = lax.axis_size("dp")
    own, views, depth = images.shape
    width = weight.shape[1]
    features = width * owners
    count = own * owners
    lot = own * views
    outer = owners // QUAD
    scale = loss_scale / groups
    me = lax.axis_index("dp").reshape(1)
    struct = jax.ShapeDtypeStruct

    mine = jnp.swapaxes(images, 0, 1).reshape(1, lot, depth)
    column = jnp.concatenate(
        [mine] + [swap(mine, "dp", high * QUAD) for high in range(1, outer)], axis=0
    )
    across = swap(column, "dp", 2)
    column_core = swap(column, "dp", 1)
    across_core = swap(across, "dp", 1)
    quarter = views * count // QUAD
    rows, z, gram_parts = call(
        embed_kernel,
        (
            struct((owners * lot, depth), BF16),
            struct((views, count, width), F32),
            struct((QUAD, quarter, count), F32),
        ),
        [SMEM] + [VMEM] * 5,
    )(me, column, across, column_core, across_core, weight)

    rows_others = [
        lax.ppermute(rows, "rep", [(i, (i + shift) % groups) for i in range(groups)])
        for shift in range(1, groups)
    ]

    gram = gram_parts[0]
    for low in range(1, QUAD):
        gram = gram + swap(gram_parts[low], "dp", low)
    received = [swap(gram, "dp", high * QUAD) for high in range(1, outer)]
    gram = functools.reduce(jnp.add, received, gram)
    gram_all = [gram] + [swap(gram, "dp", low) for low in range(1, QUAD)]

    grad, keep, send = call(
        functools.partial(grads_kernel, scale, features),
        (
            struct((owners * lot, width), BF16),
            struct((owners // 2, lot, depth), F32),
            struct((owners // 2, lot, depth), BF16),
        ),
        [SMEM] + [VMEM] * 6,
        [pltpu.VMEM((QUAD, quarter, count), F32)],
    )(me, *gram_all, z, weight)

    grad_others = [
        lax.ppermute(grad, "rep", [(i, (i + shift) % groups) for i in range(groups)])
        for shift in range(1, groups)
    ]

    keep = keep + swap(send, "dp", 1).astype(F32)
    keep = keep[:outer] + swap(keep[outer:].astype(BF16), "dp", 2).astype(F32)
    total = keep[0]
    for high in range(1, outer):
        total = total + swap(keep[high].astype(BF16), "dp", high * QUAD).astype(F32)
    image_grad = jnp.swapaxes(total.reshape(views, own, depth), 0, 1)

    weight_grad = call(weight_kernel, struct((depth, width), F32), [VMEM] * (2 * groups))(
        rows, *rows_others, grad, *grad_others
    )
    return (image_grad, weight_grad)


def solution(mesh):
    return jax.shard_map(
        shards,
        mesh=mesh,
        in_specs=(P(("rep", "dp"), None, None), P(None, "dp")),
        out_specs=(P(("rep", "dp"), None, None), P(None, "dp")),
        check_vma=False,
    )
```

```python
import functools

import jax
import jax.numpy as jnp
from jax import lax
from jax.experimental import pallas as pl
from jax.experimental.pallas import tpu as pltpu
from jax.sharding import PartitionSpec as P

invariance_weight = 25.0
variance_weight = 25.0
covariance_weight = 1.0
loss_scale = 8192.0
epsilon_var = 0.0001

F32 = jnp.float32
BF16 = jnp.bfloat16
VMEM = pl.BlockSpec(memory_space=pltpu.VMEM)
SMEM = pl.BlockSpec(memory_space=pltpu.SMEM)
CORE, ACROSS, QUAD = 1, 2, 4


def swap(block, axis, bits):
    return lax.ppermute(block, axis, [(i, i ^ bits) for i in range(lax.axis_size(axis))])


def slot_of(device, me, outer):
    rel = device ^ me
    low, high = rel % QUAD, rel // QUAD
    return ((low % 2) * 2 + low // 2) * outer + high


def part_of(index, me):
    return index ^ ((me % 2) * 2 + (me // 2) % 2)


def centre(z):
    return z - jnp.mean(z, axis=0, keepdims=True)


def nt_dot(a, b):
    return lax.dot_general(a, b, (((1,), (1,)), ((), ())), preferred_element_type=F32)


def gram_kernel(me_ref, z0_ref, z1_ref, z_ref, gram_ref):
    me = me_ref[0]
    views, count, width = z_ref.shape
    slots, lot, _ = z0_ref.shape
    own = lot // views
    for device in range(2 * slots):
        slot = slot_of(device, me, slots // 2)

        @pl.when(slot < slots)
        def _():
            for v in range(views):
                z_ref[v, device * own:(device + 1) * own] = z0_ref[slot, v * own:(v + 1) * own]

        @pl.when(slot >= slots)
        def _():
            for v in range(views):
                z_ref[v, device * own:(device + 1) * own] = z1_ref[
                    slot - slots, v * own:(v + 1) * own
                ]

    half = count // 2
    for v in range(views):
        c = centre(z_ref[v]).astype(BF16)
        gram = nt_dot(c, c)
        for h in range(2):
            gram_ref[part_of(2 * v + h, me)] = gram[h * half:(h + 1) * half]


def grads_kernel(scale, features, me_ref, g0_ref, g1_ref, g2_ref, z_ref, w_ref,
                 grad_ref, keep_ref, send_ref, gram_ref, rel_ref):
    me = me_ref[0]
    views, count, width = z_ref.shape
    parts = [g0_ref[...], g1_ref[...], g2_ref[0], g2_ref[1]]
    for index, part in enumerate(parts):
        gram_ref[part_of(index, me)] = part
    z = z_ref[...]
    coeff = scale * 4.0 * covariance_weight / (features * (count - 1))
    slots, lot, depth = keep_ref.shape
    own = lot // views
    for v in range(views):
        centred = centre(z[v])
        variance = jnp.sum(centred * centred, axis=0, keepdims=True) / (count - 1)
        spread = jnp.sqrt(variance + epsilon_var)
        centred_bf = centred.astype(BF16)
        wide = centred_bf.astype(F32)
        diag_cov = jnp.sum(wide * wide, axis=0, keepdims=True) / (count - 1)
        rest = jnp.concatenate([gram_ref[2 * v], gram_ref[2 * v + 1]], axis=0)
        through = 0.0
        for _ in range(3):
            piece = rest.astype(BF16)
            rest = rest - piece.astype(F32)
            through = through + jnp.dot(piece, centred_bf, preferred_element_type=F32)
        cov_term = through * (coeff / (count - 1)) - coeff * diag_cov * wide
        inv_term = (z[v] - z[1 - v]) * (scale * 2.0 * invariance_weight / (count * features))
        var_coeff = jnp.where(
            spread < 1.0, -scale * variance_weight / (features * (count - 1)) / spread, 0.0
        )
        grad = inv_term + var_coeff * centred + cov_term
        for device in range(2 * slots):
            rel_ref[slot_of(device, me, slots // 2), v * own:(v + 1) * own] = grad[
                device * own:(device + 1) * own
            ]
    grad = rel_ref[...].reshape(2 * slots * lot, width).astype(BF16)
    grad_ref[...] = grad
    part = nt_dot(grad, w_ref[...])
    keep_ref[...] = part[:slots * lot].reshape(slots, lot, depth)
    send_ref[...] = part[slots * lot:].reshape(slots, lot, depth).astype(BF16)


def weight_kernel(*refs):
    out_ref = refs[-1]
    total = None
    for i in range(0, len(refs) - 1, 3):
        rows = jnp.concatenate([ref[...].reshape(-1, ref.shape[2]) for ref in refs[i:i + 2]], axis=0)
        part = lax.dot_general(
            rows, refs[i + 2][...], (((0,), (0,)), ((), ())), preferred_element_type=F32
        )
        total = part if total is None else total + part
    out_ref[...] = total


def call(kernel, out_shape, specs, scratch=()):
    return pl.pallas_call(
        kernel,
        out_shape=out_shape,
        in_specs=specs,
        out_specs=jax.tree.map(lambda _: VMEM, out_shape),
        scratch_shapes=list(scratch),
        compiler_params=pltpu.CompilerParams(vmem_limit_bytes=32 * 1024 * 1024),
    )


def shards(images, weight):
    groups = lax.axis_size("rep")
    owners = lax.axis_size("dp")
    own, views, depth = images.shape
    width = weight.shape[1]
    features = width * owners
    count = own * owners
    lot = own * views
    outer = owners // QUAD
    slots = owners // 2
    scale = loss_scale / groups
    me = lax.axis_index("dp").reshape(1)
    struct = jax.ShapeDtypeStruct

    def over_rep(block):
        return [
            lax.ppermute(block, "rep", [(i, (i + shift) % groups) for i in range(groups)])
            for shift in range(1, groups)
        ]

    mine = jnp.swapaxes(images, 0, 1).reshape(1, lot, depth)
    column = jnp.concatenate(
        [mine] + [swap(mine, "dp", high * QUAD) for high in range(1, outer)], axis=0
    )
    near = jnp.concatenate([column, swap(column, "dp", ACROSS)], axis=0)
    far = swap(near, "dp", CORE)
    near_others = over_rep(near)

    z0 = jnp.dot(near.reshape(-1, depth), weight, preferred_element_type=F32)
    z1 = jnp.dot(far.reshape(-1, depth), weight, preferred_element_type=F32)
    half = count // 2
    z, parts = call(
        gram_kernel,
        (struct((views, count, width), F32), struct((4, half, count), F32)),
        [SMEM] + [VMEM] * 2,
    )(me, z0.reshape(slots, lot, width), z1.reshape(slots, lot, width))

    gram = parts[:2] + swap(parts[2:], "dp", CORE)
    gram = gram[0] + swap(gram[1], "dp", ACROSS)
    bit = QUAD
    while bit < owners:
        if bit * 2 >= owners:
            gram, near_others = lax.optimization_barrier((gram, near_others))
        gram = gram + swap(gram, "dp", bit)
        bit *= 2
    far_others = [swap(block, "dp", CORE) for block in near_others]
    gram_across = swap(gram, "dp", ACROSS)
    gram_core = swap(jnp.stack([gram, gram_across]), "dp", CORE)
    gram_core, far_others = lax.optimization_barrier((gram_core, far_others))

    grad, keep, send = call(
        functools.partial(grads_kernel, scale, features),
        (
            struct((owners * lot, width), BF16),
            struct((slots, lot, depth), F32),
            struct((slots, lot, depth), BF16),
        ),
        [SMEM] + [VMEM] * 5,
        [pltpu.VMEM((4, half, count), F32), pltpu.VMEM((owners, lot, width), F32)],
    )(me, gram, gram_across, gram_core, z, weight)

    grad_others = over_rep(grad)

    keep = keep + swap(send, "dp", CORE).astype(F32)
    keep = keep[:outer] + swap(keep[outer:].astype(BF16), "dp", ACROSS).astype(F32)
    received = [
        swap(keep[high].astype(BF16), "dp", high * QUAD) for high in range(1, outer)
    ]

    operands = [near, far, grad]
    for trio in zip(near_others, far_others, grad_others):
        operands += trio
    weight_grad = call(weight_kernel, struct((depth, width), F32), [VMEM] * len(operands))(*operands)
    received, weight_grad = lax.optimization_barrier((received, weight_grad))

    total = keep[0]
    for block in received:
        total = total + block.astype(F32)
    image_grad = jnp.swapaxes(total.reshape(views, own, depth), 0, 1)
    return (image_grad, weight_grad)


def solution(mesh):
    return jax.shard_map(
        shards,
        mesh=mesh,
        in_specs=(P(("rep", "dp"), None, None), P(None, "dp")),
        out_specs=(P(("rep", "dp"), None, None), P(None, "dp")),
        check_vma=False,
    )
```

```python
import functools

import jax
import jax.numpy as jnp
from jax import lax
from jax.experimental import pallas as pl
from jax.experimental.pallas import tpu as pltpu
from jax.sharding import PartitionSpec as P

invariance_weight = 25.0
variance_weight = 25.0
covariance_weight = 1.0
loss_scale = 8192.0
epsilon_var = 0.0001

F32 = jnp.float32
BF16 = jnp.bfloat16
VMEM = pl.BlockSpec(memory_space=pltpu.VMEM)
SMEM = pl.BlockSpec(memory_space=pltpu.SMEM)
CORE, ACROSS, QUAD = 1, 2, 4


def swap(block, axis, bits):
    return lax.ppermute(block, axis, [(i, i ^ bits) for i in range(lax.axis_size(axis))])


def slot_of(device, me, outer):
    rel = (device ^ me) % QUAD
    return ((rel % 2) * 2 + rel // 2) * outer + device // QUAD


def centre(z):
    return z - jnp.mean(z, axis=0, keepdims=True)


def nt_dot(a, b):
    return lax.dot_general(a, b, (((1,), (1,)), ((), ())), preferred_element_type=F32)


def gram_kernel(me_ref, z0_ref, z1_ref, z_ref, gram_ref):
    me = me_ref[0]
    views, count, width = z_ref.shape
    slots, lot, _ = z0_ref.shape
    own = lot // views
    for device in range(2 * slots):
        slot = slot_of(device, me, slots // 2)

        @pl.when(slot < slots)
        def _():
            for v in range(views):
                z_ref[v, device * own:(device + 1) * own] = z0_ref[slot, v * own:(v + 1) * own]

        @pl.when(slot >= slots)
        def _():
            for v in range(views):
                z_ref[v, device * own:(device + 1) * own] = z1_ref[
                    slot - slots, v * own:(v + 1) * own
                ]

    for v in range(views):
        c = centre(z_ref[v]).astype(BF16)
        gram_ref[v] = nt_dot(c, c)


def grads_kernel(scale, features, me_ref, gram_ref, z_ref, grad_ref, rel_ref):
    me = me_ref[0]
    views, count, width = z_ref.shape
    z = z_ref[...]
    coeff = scale * 4.0 * covariance_weight / (features * (count - 1))
    devices, lot, _ = rel_ref.shape
    own = lot // views
    for v in range(views):
        centred = centre(z[v])
        variance = jnp.sum(centred * centred, axis=0, keepdims=True) / (count - 1)
        spread = jnp.sqrt(variance + epsilon_var)
        centred_bf = centred.astype(BF16)
        wide = centred_bf.astype(F32)
        diag_cov = jnp.sum(wide * wide, axis=0, keepdims=True) / (count - 1)
        rest = gram_ref[v]
        through = 0.0
        for _ in range(3):
            piece = rest.astype(BF16)
            rest = rest - piece.astype(F32)
            through = through + jnp.dot(piece, centred_bf, preferred_element_type=F32)
        cov_term = through * (coeff / (count - 1)) - coeff * diag_cov * wide
        inv_term = (z[v] - z[1 - v]) * (scale * 2.0 * invariance_weight / (count * features))
        var_coeff = jnp.where(
            spread < 1.0, -scale * variance_weight / (features * (count - 1)) / spread, 0.0
        )
        grad = inv_term + var_coeff * centred + cov_term
        for device in range(devices):
            rel_ref[slot_of(device, me, devices // QUAD), v * own:(v + 1) * own] = grad[
                device * own:(device + 1) * own
            ]
    grad_ref[...] = rel_ref[...].reshape(devices * lot, width).astype(BF16)


def weight_kernel(*refs):
    out_ref = refs[-1]
    total = None
    for i in range(0, len(refs) - 1, 3):
        rows = jnp.concatenate([ref[...].reshape(-1, ref.shape[2]) for ref in refs[i:i + 2]], axis=0)
        part = lax.dot_general(
            rows, refs[i + 2][...], (((0,), (0,)), ((), ())), preferred_element_type=F32
        )
        total = part if total is None else total + part
    out_ref[...] = total


def call(kernel, out_shape, specs, scratch=()):
    return pl.pallas_call(
        kernel,
        out_shape=out_shape,
        in_specs=specs,
        out_specs=jax.tree.map(lambda _: VMEM, out_shape),
        scratch_shapes=list(scratch),
        compiler_params=pltpu.CompilerParams(vmem_limit_bytes=32 * 1024 * 1024),
    )


def shards(images, weight):
    groups = lax.axis_size("rep")
    owners = lax.axis_size("dp")
    own, views, depth = images.shape
    width = weight.shape[1]
    features = width * owners
    count = own * owners
    lot = own * views
    outer = owners // QUAD
    slots = owners // 2
    scale = loss_scale / groups
    me = lax.axis_index("dp").reshape(1)
    struct = jax.ShapeDtypeStruct

    def over_rep(block):
        return [
            lax.ppermute(block, "rep", [(i, (i + shift) % groups) for i in range(groups)])
            for shift in range(1, groups)
        ]

    columns = [[high * QUAD + low for high in range(outer)] for low in range(QUAD)]
    quads = [[high * QUAD + low for low in range(QUAD)] for high in range(outer)]

    def trade(blocks, lists):
        return lax.all_to_all(blocks, "dp", 0, 0, axis_index_groups=lists, tiled=True)

    def gather(block, lists):
        return trade(jnp.broadcast_to(block, (len(lists[0]),) + block.shape), lists)

    column = gather(jnp.swapaxes(images, 0, 1).reshape(lot, depth), columns)
    across = swap(column, "dp", ACROSS)
    column, across = lax.optimization_barrier((column, across))
    near = jnp.concatenate([column, across], axis=0)
    far = swap(near, "dp", CORE)
    near_others = over_rep(near)

    z0 = jnp.dot(near.reshape(-1, depth), weight, preferred_element_type=F32)
    z1 = jnp.dot(far.reshape(-1, depth), weight, preferred_element_type=F32)
    z, parts = call(
        gram_kernel,
        (struct((views, count, width), F32), struct((views, count, count), F32)),
        [SMEM] + [VMEM] * 2,
    )(me, z0.reshape(slots, lot, width), z1.reshape(slots, lot, width))

    quarter = jnp.sum(trade(parts.reshape(QUAD, -1, count), quads), axis=0)
    quarter = jnp.sum(gather(quarter, columns), axis=0)
    quarter, near_others = lax.optimization_barrier((quarter, near_others))
    gram = gather(quarter, quads).reshape(views, count, count)

    grad = call(
        functools.partial(grads_kernel, scale, features),
        struct((owners * lot, width), BF16),
        [SMEM] + [VMEM] * 2,
        [pltpu.VMEM((owners, lot, width), F32)],
    )(me, gram, z)

    grad_keep, grad_send = grad[:slots * lot], grad[slots * lot:]
    send = nt_dot(grad_send, weight).astype(BF16)
    received = swap(send, "dp", CORE)
    grad_others = over_rep(grad)
    keep = (nt_dot(grad_keep, weight) + received.astype(F32)).reshape(slots, lot, depth)
    keep, near_others = lax.optimization_barrier((keep, near_others))
    far_others = [swap(block, "dp", CORE) for block in near_others]
    received = swap(keep[outer:].astype(BF16), "dp", ACROSS)
    keep = keep[:outer] + received.astype(F32)
    received = trade(keep.astype(BF16), columns)

    operands = [near, far, grad]
    for trio in zip(near_others, far_others, grad_others):
        operands += trio
    weight_grad = call(weight_kernel, struct((depth, width), F32), [VMEM] * len(operands))(*operands)
    received, weight_grad = lax.optimization_barrier((received, weight_grad))

    total = jnp.sum(received.astype(F32), axis=0)
    image_grad = jnp.swapaxes(total.reshape(views, own, depth), 0, 1)
    return (image_grad, weight_grad)


def solution(mesh):
    return jax.shard_map(
        shards,
        mesh=mesh,
        in_specs=(P(("rep", "dp"), None, None), P(None, "dp")),
        out_specs=(P(("rep", "dp"), None, None), P(None, "dp")),
        check_vma=False,
    )
```

```python
import functools

import jax
import jax.numpy as jnp
from jax import lax
from jax.experimental import pallas as pl
from jax.experimental.pallas import tpu as pltpu
from jax.sharding import PartitionSpec as P

invariance_weight = 25.0
variance_weight = 25.0
covariance_weight = 1.0
loss_scale = 8192.0
epsilon_var = 0.0001

F32 = jnp.float32
BF16 = jnp.bfloat16
VMEM = pl.BlockSpec(memory_space=pltpu.VMEM)
SMEM = pl.BlockSpec(memory_space=pltpu.SMEM)
CORE, ACROSS, QUAD = 1, 2, 4
EXTRA = 8


def swap(block, axis, bits):
    return lax.ppermute(block, axis, [(i, i ^ bits) for i in range(lax.axis_size(axis))])


def slot_of(device, me, outer):
    rel = device ^ me
    low, high = rel % QUAD, rel // QUAD
    return ((low // 2) * outer + high) * 2 + low % 2


def centre(z):
    return z - jnp.mean(z, axis=0, keepdims=True)


def nt_dot(a, b):
    return lax.dot_general(a, b, (((1,), (1,)), ((), ())), preferred_element_type=F32)


def half_masks(half, count):
    row = lax.broadcasted_iota(jnp.int32, (half, count), 0)
    lane = lax.broadcasted_iota(jnp.int32, (half, count), 1)
    return (lane < half) & (row < lane), row == lane, lane < half


def gram_kernel(own, me_ref, z0_ref, z1_ref, c_ref, packed_ref, sorted_ref):
    me = me_ref[0]
    count, width = z0_ref.shape
    devices = count // own
    half = count // 2
    for block, ref in enumerate((z0_ref, z1_ref)):
        centred = centre(ref[...]).reshape(devices, own, width)
        for slot in range(devices):
            core, outer = slot % 2, devices // QUAD
            rel = (slot // 2 % outer) * QUAD + (slot // 2 // outer) * 2 + core
            sorted_ref[rel ^ me, :, block * width:(block + 1) * width] = centred[slot]
    c = sorted_ref[...].reshape(count, 2 * width).astype(BF16)
    c_ref[...] = c
    gram = nt_dot(c, c)
    upper, diagonal, _ = half_masks(half, count)
    turned = pltpu.roll(gram[half:], half, 1)
    packed_ref[:half] = jnp.where(upper, turned, gram[:half])
    second = jnp.sum(jnp.where(diagonal, turned, 0.0), axis=0, keepdims=True)
    packed_ref[half:] = jnp.broadcast_to(second, (EXTRA, count))


def unpack(packed_ref):
    count = packed_ref.shape[1]
    half = count // 2
    upper, diagonal, left = half_masks(half, count)
    top = packed_ref[:half]
    second = packed_ref[half:half + 1]
    mirror = jnp.swapaxes(jnp.concatenate([top, jnp.zeros_like(top)], axis=0), 0, 1)
    first = jnp.where(upper, mirror[:half], top)
    last = jnp.where(diagonal, second, jnp.where(upper, top, mirror[:half]))
    last = jnp.where(left, mirror[half:], pltpu.roll(last, half, 1))
    return jnp.concatenate([first, last], axis=0)


def grads_kernel(own, scale, features, me_ref, packed_ref, c_ref, z0_ref, z1_ref, o0_ref, o1_ref,
                 grad0_ref, grad1_ref, rel_ref):
    me = me_ref[0]
    count, width = z0_ref.shape
    devices = count // own
    gram = unpack(packed_ref)
    pieces = []
    for _ in range(3):
        pieces.append(gram.astype(BF16))
        gram = gram - pieces[-1].astype(F32)
    coeff = scale * 4.0 * covariance_weight / (features * (count - 1))
    blocks = ((z0_ref, o0_ref, grad0_ref), (z1_ref, o1_ref, grad1_ref))
    for block, (z_ref, o_ref, grad_ref) in enumerate(blocks):
        c = c_ref[:, block * width:(block + 1) * width]
        through = functools.reduce(
            jnp.add, [jnp.dot(piece, c, preferred_element_type=F32) for piece in pieces]
        )
        for device in range(devices):
            rel_ref[slot_of(device, me, devices // QUAD)] = through[device * own:(device + 1) * own]
        through = rel_ref[...].reshape(count, width)
        z = z_ref[...]
        other = o_ref[...].reshape(devices // 2, 2, own, width)
        other = jnp.concatenate([other[:, 1:], other[:, :1]], axis=1).reshape(count, width)
        centred = centre(z)
        variance = jnp.sum(centred * centred, axis=0, keepdims=True) / (count - 1)
        spread = jnp.sqrt(variance + epsilon_var)
        wide = centred.astype(BF16).astype(F32)
        diag_cov = jnp.sum(wide * wide, axis=0, keepdims=True) / (count - 1)
        cov_term = through * (coeff / (count - 1)) - coeff * diag_cov * wide
        inv_term = (z - other) * (scale * 2.0 * invariance_weight / (count * features))
        var_coeff = jnp.where(
            spread < 1.0, -scale * variance_weight / (features * (count - 1)) / spread, 0.0
        )
        grad_ref[...] = (inv_term + var_coeff * centred + cov_term).astype(BF16)


def weight_kernel(*refs):
    out_ref = refs[-1]
    total = None
    for i in range(0, len(refs) - 1, 4):
        rows, grads = (
            jnp.concatenate([refs[i + j][...], refs[i + j + 1][...]], axis=0) for j in (0, 2)
        )
        part = lax.dot_general(
            rows, grads, (((0,), (0,)), ((), ())), preferred_element_type=F32
        )
        total = part if total is None else total + part
    out_ref[...] = total


def call(kernel, out_shape, specs, scratch=()):
    return pl.pallas_call(
        kernel,
        out_shape=out_shape,
        in_specs=specs,
        out_specs=jax.tree.map(lambda _: VMEM, out_shape),
        scratch_shapes=list(scratch),
        compiler_params=pltpu.CompilerParams(vmem_limit_bytes=32 * 1024 * 1024),
    )


def shards(images, weight):
    groups = lax.axis_size("rep")
    owners = lax.axis_size("dp")
    own, views, depth = images.shape
    width = weight.shape[1]
    features = width * owners
    count = own * owners
    lot = 2 * own
    outer = owners // QUAD
    scale = loss_scale / groups
    position = lax.axis_index("dp")
    me = position.reshape(1)
    second = position % 2 == 1
    struct = jax.ShapeDtypeStruct

    def over_rep(block):
        return [
            lax.ppermute(block, "rep", [(i, (i + shift) % groups) for i in range(groups)])
            for shift in range(1, groups)
        ]

    def matmul(rows, matrix):
        return jnp.dot(rows, matrix, preferred_element_type=F32)

    weight_core = swap(weight, "dp", CORE)
    view0, view1 = images[:, 0], images[:, 1]
    given = swap(jnp.where(second, view0, view1), "dp", CORE)
    mine = jnp.concatenate([jnp.where(second, view1, view0), given], axis=0)
    column = jnp.concatenate(
        [mine] + [swap(mine, "dp", high * QUAD) for high in range(1, outer)], axis=0
    )
    across = swap(column, "dp", ACROSS)
    column, across = lax.optimization_barrier((column, across))
    rows = jnp.concatenate([column, across], axis=0)

    z0, z1 = matmul(rows, weight), matmul(rows, weight_core)
    half = count // 2
    c, packed = call(
        functools.partial(gram_kernel, own),
        (struct((count, 2 * width), BF16), struct((half + EXTRA, count), F32)),
        [SMEM] + [VMEM] * 2,
        [pltpu.VMEM((owners, own, 2 * width), F32)],
    )(me, z0, z1)

    rows_others = over_rep(rows)
    rows_core = swap(rows, "dp", CORE)
    o0, o1 = matmul(rows_core, weight), matmul(rows_core, weight_core)

    packed = packed + swap(packed, "dp", ACROSS)
    bit = QUAD
    while bit < owners:
        if bit * 2 >= owners:
            packed, rows_others = lax.optimization_barrier((packed, rows_others))
        packed = packed + swap(packed, "dp", bit)
        bit *= 2

    grad0, grad1 = call(
        functools.partial(grads_kernel, own, scale, features),
        (struct((count, width), BF16), struct((count, width), BF16)),
        [SMEM] + [VMEM] * 6,
        [pltpu.VMEM((owners, own, width), F32)],
    )(me, packed, c, z0, z1, o0, o1)

    send = (nt_dot(grad0[half:], weight) + nt_dot(grad1[half:], weight_core)).astype(BF16)
    received = swap(send, "dp", ACROSS)
    grad_core = swap(grad1, "dp", CORE)
    grad_others = [over_rep(grad0), over_rep(grad_core)]
    keep = nt_dot(grad0[:half], weight) + nt_dot(grad1[:half], weight_core)
    keep, rows_others = lax.optimization_barrier((keep, rows_others))
    rows_core_others = [swap(block, "dp", CORE) for block in rows_others]
    keep = (keep + received.astype(F32)).reshape(outer, lot, depth)
    received = [
        swap(keep[high].astype(BF16), "dp", high * QUAD) for high in range(1, outer)
    ]

    operands = [rows, rows_core, grad0, grad_core]
    for four in zip(rows_others, rows_core_others, *grad_others):
        operands += four
    weight_grad = call(weight_kernel, struct((depth, width), F32), [VMEM] * len(operands))(*operands)
    received, weight_grad = lax.optimization_barrier((received, weight_grad))

    total = keep[0]
    for block in received:
        total = total + block.astype(F32)
    view_own, view_other = total[:own], swap(total[own:], "dp", CORE)
    image_grad = jnp.stack(
        [jnp.where(second, view_other, view_own), jnp.where(second, view_own, view_other)], axis=1
    )
    return (image_grad, weight_grad)


def solution(mesh):
    return jax.shard_map(
        shards,
        mesh=mesh,
        in_specs=(P(("rep", "dp"), None, None), P(None, "dp")),
        out_specs=(P(("rep", "dp"), None, None), P(None, "dp")),
        check_vma=False,
    )
```

```python
import functools

import jax
import jax.numpy as jnp
from jax import lax
from jax.experimental import pallas as pl
from jax.experimental.pallas import tpu as pltpu
from jax.sharding import PartitionSpec as P

invariance_weight = 25.0
variance_weight = 25.0
covariance_weight = 1.0
loss_scale = 8192.0
epsilon_var = 0.0001

F32 = jnp.float32
BF16 = jnp.bfloat16
VMEM = pl.BlockSpec(memory_space=pltpu.VMEM)
SMEM = pl.BlockSpec(memory_space=pltpu.SMEM)
CORE, ACROSS, QUAD = 1, 2, 4
EXTRA = 8


def swap(block, axis, bits):
    return lax.ppermute(block, axis, [(i, i ^ bits) for i in range(lax.axis_size(axis))])


def slot_of(device, me, outer):
    rel = device ^ me
    low, high = rel % QUAD, rel // QUAD
    return ((low // 2) * outer + high) * 2 + low % 2


def centre(z):
    return z - jnp.mean(z, axis=0, keepdims=True)


def nt_dot(a, b):
    return lax.dot_general(a, b, (((1,), (1,)), ((), ())), preferred_element_type=F32)


def half_masks(half, count):
    row = lax.broadcasted_iota(jnp.int32, (half, count), 0)
    lane = lax.broadcasted_iota(jnp.int32, (half, count), 1)
    return (lane < half) & (row < lane), row == lane, lane < half


def whole(near_ref, far_ref):
    return jnp.concatenate([near_ref[...], far_ref[...]], axis=0)


def gram_kernel(own, me_ref, near_ref, far_ref, c_ref, packed_ref, sorted_ref):
    me = me_ref[0]
    count, width = c_ref.shape
    devices = count // own
    outer = devices // QUAD
    half = count // 2
    centred = centre(whole(near_ref, far_ref)).reshape(devices, own, width)
    for slot in range(devices):
        rel = (slot // 2 % outer) * QUAD + (slot // 2 // outer) * 2 + slot % 2
        sorted_ref[rel ^ me] = centred[slot]
    c = sorted_ref[...].reshape(count, width).astype(BF16)
    c_ref[...] = c
    gram = nt_dot(c, c)
    upper, diagonal, _ = half_masks(half, count)
    turned = pltpu.roll(gram[half:], half, 1)
    packed_ref[:half] = jnp.where(upper, turned, gram[:half])
    second = jnp.sum(jnp.where(diagonal, turned, 0.0), axis=0, keepdims=True)
    packed_ref[half:] = jnp.broadcast_to(second, (EXTRA, count))


def unpack(packed_ref):
    count = packed_ref.shape[1]
    half = count // 2
    upper, diagonal, left = half_masks(half, count)
    top = packed_ref[:half]
    second = packed_ref[half:half + 1]
    mirror = jnp.swapaxes(jnp.concatenate([top, jnp.zeros_like(top)], axis=0), 0, 1)
    first = jnp.where(upper, mirror[:half], top)
    last = jnp.where(diagonal, second, jnp.where(upper, top, mirror[:half]))
    last = jnp.where(left, mirror[half:], pltpu.roll(last, half, 1))
    return jnp.concatenate([first, last], axis=0)


def base_kernel(scale, features, near_ref, far_ref, base_ref):
    count = base_ref.shape[0]
    coeff = scale * 4.0 * covariance_weight / (features * (count - 1))
    centred = centre(whole(near_ref, far_ref))
    variance = jnp.sum(centred * centred, axis=0, keepdims=True) / (count - 1)
    spread = jnp.sqrt(variance + epsilon_var)
    wide = centred.astype(BF16).astype(F32)
    diag_cov = jnp.sum(wide * wide, axis=0, keepdims=True) / (count - 1)
    var_coeff = jnp.where(
        spread < 1.0, -scale * variance_weight / (features * (count - 1)) / spread, 0.0
    )
    base_ref[...] = var_coeff * centred - coeff * diag_cov * wide


def grads_kernel(own, scale, features, me_ref, packed_ref, c_ref, near_ref, far_ref, other_ref,
                 base_ref, w_ref, grad0_ref, grad1_ref, send_ref, rel_ref):
    me = me_ref[0]
    count, width = c_ref.shape
    devices = count // own
    rest = unpack(packed_ref)
    through = 0.0
    for _ in range(3):
        piece = rest.astype(BF16)
        rest = rest - piece.astype(F32)
        through = through + jnp.dot(piece, c_ref[...], preferred_element_type=F32)
    for device in range(devices):
        rel_ref[slot_of(device, me, devices // QUAD)] = through[device * own:(device + 1) * own]
    coeff = scale * 4.0 * covariance_weight / (features * (count - 1))
    other = other_ref[...].reshape(devices // 2, 2, own, width)
    other = jnp.concatenate([other[:, 1:], other[:, :1]], axis=1).reshape(count, width)
    gap = whole(near_ref, far_ref) - other
    inv_term = gap * (scale * 2.0 * invariance_weight / (count * features))
    through = rel_ref[...].reshape(count, width)
    grad = (inv_term + base_ref[...] + through * (coeff / (count - 1))).astype(BF16)
    grad0_ref[...] = grad[:, :width // 2]
    grad1_ref[...] = grad[:, width // 2:]
    send_ref[...] = nt_dot(grad[count // 2:], w_ref[...]).astype(BF16)


def weight_kernel(*refs):
    out_ref = refs[-1]
    total = None
    for i in range(0, len(refs) - 1, 4):
        rows, grads = (
            jnp.concatenate([refs[i + j][...], refs[i + j + 1][...]], axis=0) for j in (0, 2)
        )
        part = lax.dot_general(
            rows, grads, (((0,), (0,)), ((), ())), preferred_element_type=F32
        )
        total = part if total is None else total + part
    out_ref[...] = total


def call(kernel, out_shape, specs, scratch=()):
    return pl.pallas_call(
        kernel,
        out_shape=out_shape,
        in_specs=specs,
        out_specs=jax.tree.map(lambda _: VMEM, out_shape),
        scratch_shapes=list(scratch),
        compiler_params=pltpu.CompilerParams(vmem_limit_bytes=32 * 1024 * 1024),
    )


def shards(images, weight):
    groups = lax.axis_size("rep")
    owners = lax.axis_size("dp")
    own, views, depth = images.shape
    block = weight.shape[1]
    width = 2 * block
    features = block * owners
    count = own * owners
    half = count // 2
    lot = 2 * own
    outer = owners // QUAD
    scale = loss_scale / groups
    position = lax.axis_index("dp")
    me = position.reshape(1)
    second = position % 2 == 1
    struct = jax.ShapeDtypeStruct

    def over_rep(array):
        return [
            lax.ppermute(array, "rep", [(i, (i + shift) % groups) for i in range(groups)])
            for shift in range(1, groups)
        ]

    def matmul(rows, matrix):
        return jnp.dot(rows, matrix, preferred_element_type=F32)

    def own_view(array):
        return jnp.where(second, array[:, 1], array[:, 0])

    given = swap(images, "dp", CORE)
    weight_core = swap(weight, "dp", CORE)
    mine = jnp.concatenate([own_view(images), own_view(given)], axis=0)
    column = [swap(mine, "dp", high * QUAD) for high in range(1, outer)]
    wide = jnp.concatenate([weight, weight_core], axis=1)
    column, wide = lax.optimization_barrier((column, wide))
    column = jnp.concatenate([mine] + column, axis=0)
    across = swap(column, "dp", ACROSS)
    near = matmul(column, wide)
    near, across = lax.optimization_barrier((near, across))
    far = matmul(across, wide)

    c, packed = call(
        functools.partial(gram_kernel, own),
        (struct((count, width), BF16), struct((half + EXTRA, count), F32)),
        [SMEM] + [VMEM] * 2,
        [pltpu.VMEM((owners, own, width), F32)],
    )(me, near, far)

    along, beside, corner = (swap(packed, "dp", bits) for bits in (ACROSS, QUAD, ACROSS | QUAD))
    packed = (packed + along) + (beside + corner)
    packed, near_late, far_late, rows = lax.optimization_barrier(
        (packed, near, far, jnp.concatenate([column, across], axis=0))
    )
    rows_core = swap(rows, "dp", CORE)
    base = call(
        functools.partial(base_kernel, scale, features), struct((count, width), F32), [VMEM] * 2
    )(near_late, far_late)
    base, sent = lax.optimization_barrier((base, rows))
    rows_others = over_rep(sent)
    other = matmul(rows_core, wide)
    bit = 2 * QUAD
    while bit < owners:
        received = swap(packed, "dp", bit)
        received, other, base = lax.optimization_barrier((received, other, base))
        packed = packed + received
        bit *= 2

    grad0, grad1, send = call(
        functools.partial(grads_kernel, own, scale, features),
        (
            struct((count, block), BF16),
            struct((count, block), BF16),
            struct((half, depth), BF16),
        ),
        [SMEM] + [VMEM] * 7,
        [pltpu.VMEM((owners, own, width), F32)],
    )(me, packed, c, near, far, other, base, wide)

    received = swap(send, "dp", ACROSS)
    grad = jnp.concatenate([grad0[:half], grad1[:half]], axis=1)
    keep = nt_dot(grad, wide)
    keep, grad0, grad1 = lax.optimization_barrier((keep, grad0, grad1))
    grad_core = swap(grad1, "dp", CORE)
    grad_others = [over_rep(grad0), over_rep(grad_core)]
    rows_core_others = [swap(array, "dp", CORE) for array in rows_others]
    keep = (keep + received.astype(F32)).reshape(outer, lot, depth)
    received = [
        swap(keep[high].astype(BF16), "dp", high * QUAD) for high in range(1, outer)
    ]

    operands = [rows, rows_core, grad0, grad_core]
    for four in zip(rows_others, rows_core_others, *grad_others):
        operands += four
    weight_grad = call(weight_kernel, struct((depth, block), F32), [VMEM] * len(operands))(*operands)
    received, weight_grad = lax.optimization_barrier((received, weight_grad))

    total = keep[0]
    for array in received:
        total = total + array.astype(F32)
    view_own, view_other = total[:own], swap(total[own:], "dp", CORE)
    image_grad = jnp.stack(
        [jnp.where(second, view_other, view_own), jnp.where(second, view_own, view_other)], axis=1
    )
    return (image_grad, weight_grad)


def solution(mesh):
    return jax.shard_map(
        shards,
        mesh=mesh,
        in_specs=(P(("rep", "dp"), None, None), P(None, "dp")),
        out_specs=(P(("rep", "dp"), None, None), P(None, "dp")),
        check_vma=False,
    )
```

```python
import functools

import jax
import jax.numpy as jnp
from jax import lax
from jax.experimental import pallas as pl
from jax.experimental.pallas import tpu as pltpu
from jax.sharding import PartitionSpec as P

invariance_weight = 25.0
variance_weight = 25.0
covariance_weight = 1.0
loss_scale = 8192.0
epsilon_var = 0.0001

F32 = jnp.float32
BF16 = jnp.bfloat16
VMEM = pl.BlockSpec(memory_space=pltpu.VMEM)
SMEM = pl.BlockSpec(memory_space=pltpu.SMEM)
CORE, ACROSS, QUAD = 1, 2, 4
EXTRA = 8


def swap(block, axis, bits):
    return lax.ppermute(block, axis, [(i, i ^ bits) for i in range(lax.axis_size(axis))])


def slot_of(device, me, outer):
    rel = device ^ me
    low, high = rel % QUAD, rel // QUAD
    return ((low // 2) * outer + high) * 2 + low % 2


def centre(z):
    return z - jnp.mean(z, axis=0, keepdims=True)


def nt_dot(a, b):
    return lax.dot_general(a, b, (((1,), (1,)), ((), ())), preferred_element_type=F32)


def half_masks(half, count):
    row = lax.broadcasted_iota(jnp.int32, (half, count), 0)
    lane = lax.broadcasted_iota(jnp.int32, (half, count), 1)
    return (lane < half) & (row < lane), row == lane, lane < half


def whole(near_ref, far_ref):
    return jnp.concatenate([near_ref[...], far_ref[...]], axis=0)


def gram_kernel(own, me_ref, near_ref, far_ref, c_ref, packed_ref, sorted_ref):
    me = me_ref[0]
    count, width = c_ref.shape
    devices = count // own
    outer = devices // QUAD
    half = count // 2
    centred = centre(whole(near_ref, far_ref)).reshape(devices, own, width)
    for slot in range(devices):
        rel = (slot // 2 % outer) * QUAD + (slot // 2 // outer) * 2 + slot % 2
        sorted_ref[rel ^ me] = centred[slot]
    c = sorted_ref[...].reshape(count, width).astype(BF16)
    c_ref[...] = c
    gram = nt_dot(c, c)
    upper, diagonal, _ = half_masks(half, count)
    turned = pltpu.roll(gram[half:], half, 1)
    packed_ref[:half] = jnp.where(upper, turned, gram[:half])
    second = jnp.sum(jnp.where(diagonal, turned, 0.0), axis=0, keepdims=True)
    packed_ref[half:] = jnp.broadcast_to(second, (EXTRA, count))


def unpack(packed_ref):
    count = packed_ref.shape[1]
    half = count // 2
    upper, diagonal, left = half_masks(half, count)
    top = packed_ref[:half]
    second = packed_ref[half:half + 1]
    mirror = jnp.swapaxes(jnp.concatenate([top, jnp.zeros_like(top)], axis=0), 0, 1)
    first = jnp.where(upper, mirror[:half], top)
    last = jnp.where(diagonal, second, jnp.where(upper, top, mirror[:half]))
    last = jnp.where(left, mirror[half:], pltpu.roll(last, half, 1))
    return jnp.concatenate([first, last], axis=0)


def base_kernel(scale, features, near_ref, far_ref, base_ref):
    count = base_ref.shape[0]
    coeff = scale * 4.0 * covariance_weight / (features * (count - 1))
    centred = centre(whole(near_ref, far_ref))
    variance = jnp.sum(centred * centred, axis=0, keepdims=True) / (count - 1)
    spread = jnp.sqrt(variance + epsilon_var)
    wide = centred.astype(BF16).astype(F32)
    diag_cov = jnp.sum(wide * wide, axis=0, keepdims=True) / (count - 1)
    var_coeff = jnp.where(
        spread < 1.0, -scale * variance_weight / (features * (count - 1)) / spread, 0.0
    )
    base_ref[...] = var_coeff * centred - coeff * diag_cov * wide


def grads_kernel(own, scale, features, me_ref, packed_ref, c_ref, near_ref, far_ref, other_ref,
                 base_ref, w_ref, grad_ref, send_ref, rel_ref):
    me = me_ref[0]
    count, width = c_ref.shape
    devices = count // own
    rest = unpack(packed_ref)
    through = 0.0
    for _ in range(3):
        piece = rest.astype(BF16)
        rest = rest - piece.astype(F32)
        through = through + jnp.dot(piece, c_ref[...], preferred_element_type=F32)
    for device in range(devices):
        rel_ref[slot_of(device, me, devices // QUAD)] = through[device * own:(device + 1) * own]
    coeff = scale * 4.0 * covariance_weight / (features * (count - 1))
    other = other_ref[...].reshape(devices // 2, 2, own, width)
    other = jnp.concatenate([other[:, 1:], other[:, :1]], axis=1).reshape(count, width)
    gap = whole(near_ref, far_ref) - other
    inv_term = gap * (scale * 2.0 * invariance_weight / (count * features))
    through = rel_ref[...].reshape(count, width)
    grad = (inv_term + base_ref[...] + through * (coeff / (count - 1))).astype(BF16)
    grad_ref[...] = grad
    send_ref[...] = nt_dot(grad[count // 2:], w_ref[...]).astype(BF16)


def weight_kernel(*refs):
    rows_ref, rows_core_ref, grad_ref, grad_core_ref = refs[:4]
    block = grad_core_ref.shape[1]
    rows = jnp.concatenate([rows_ref[...], rows_core_ref[...]], axis=0)
    grads = jnp.concatenate([grad_ref[:, :block], grad_core_ref[...]], axis=0)
    part = lax.dot_general(rows, grads, (((0,), (0,)), ((), ())), preferred_element_type=F32)
    refs[-1][...] = part + refs[4][...] if len(refs) > 5 else part


def call(kernel, out_shape, specs, scratch=()):
    return pl.pallas_call(
        kernel,
        out_shape=out_shape,
        in_specs=specs,
        out_specs=jax.tree.map(lambda _: VMEM, out_shape),
        scratch_shapes=list(scratch),
        compiler_params=pltpu.CompilerParams(vmem_limit_bytes=32 * 1024 * 1024),
    )


def shards(images, weight):
    groups = lax.axis_size("rep")
    owners = lax.axis_size("dp")
    own, views, depth = images.shape
    block = weight.shape[1]
    width = 2 * block
    features = block * owners
    count = own * owners
    half = count // 2
    lot = 2 * own
    outer = owners // QUAD
    scale = loss_scale / groups
    position = lax.axis_index("dp")
    me = position.reshape(1)
    second = position % 2 == 1
    struct = jax.ShapeDtypeStruct

    def over_rep(array):
        return [
            lax.ppermute(array, "rep", [(i, (i + shift) % groups) for i in range(groups)])
            for shift in range(1, groups)
        ]

    def matmul(rows, matrix):
        return jnp.dot(rows, matrix, preferred_element_type=F32)

    def own_view(array):
        return jnp.where(second, array[:, 1], array[:, 0])

    given = swap(images, "dp", CORE)
    weight_core = swap(weight, "dp", CORE)
    mine = jnp.concatenate([own_view(images), own_view(given)], axis=0)
    column = [swap(mine, "dp", high * QUAD) for high in range(1, outer)]
    wide = jnp.concatenate([weight, weight_core], axis=1)
    column, wide = lax.optimization_barrier((column, wide))
    column = jnp.concatenate([mine] + column, axis=0)
    across = swap(column, "dp", ACROSS)
    near = matmul(column, wide)
    near, across = lax.optimization_barrier((near, across))
    far = matmul(across, wide)

    c, packed = call(
        functools.partial(gram_kernel, own),
        (struct((count, width), BF16), struct((half + EXTRA, count), F32)),
        [SMEM] + [VMEM] * 2,
        [pltpu.VMEM((owners, own, width), F32)],
    )(me, near, far)

    along, beside, corner = (swap(packed, "dp", bits) for bits in (ACROSS, QUAD, ACROSS | QUAD))
    packed = (packed + along) + (beside + corner)
    packed, near_late, far_late, rows = lax.optimization_barrier(
        (packed, near, far, jnp.concatenate([column, across], axis=0))
    )
    rows_core = swap(rows, "dp", CORE)
    base = call(
        functools.partial(base_kernel, scale, features), struct((count, width), F32), [VMEM] * 2
    )(near_late, far_late)
    base, sent = lax.optimization_barrier((base, rows))
    rows_others = over_rep(sent)
    other = matmul(rows_core, wide)
    bit = 2 * QUAD
    while bit < owners:
        received = swap(packed, "dp", bit)
        received, other, base = lax.optimization_barrier((received, other, base))
        packed = packed + received
        bit *= 2

    grad, send = call(
        functools.partial(grads_kernel, own, scale, features),
        (struct((count, width), BF16), struct((half, depth), BF16)),
        [SMEM] + [VMEM] * 7,
        [pltpu.VMEM((owners, own, width), F32)],
    )(me, packed, c, near, far, other, base, wide)

    def weight_part(*operands):
        return call(weight_kernel, struct((depth, block), F32), [VMEM] * len(operands))(*operands)

    received = swap(send, "dp", ACROSS)
    keep = nt_dot(grad[:half], wide)
    keep, grad = lax.optimization_barrier((keep, grad))
    grad_others = over_rep(grad)
    grad_core = swap(grad[:, block:], "dp", CORE)
    keep = (keep + received.astype(F32)).reshape(outer, lot, depth)
    received = [
        swap(keep[high].astype(BF16), "dp", high * QUAD) for high in range(1, outer)
    ]
    weight_grad = weight_part(rows, rows_core, grad, grad_core)
    received, weight_grad = lax.optimization_barrier((received, weight_grad))

    total = keep[0]
    for array in received:
        total = total + array.astype(F32)
    view_other = swap(total[own:], "dp", CORE)
    for theirs, theirs_grad in zip(rows_others, grad_others):
        weight_grad = weight_part(
            theirs, swap(theirs, "dp", CORE),
            theirs_grad, swap(theirs_grad[:, block:], "dp", CORE), weight_grad,
        )
    view_other, weight_grad = lax.optimization_barrier((view_other, weight_grad))
    view_own = total[:own]
    image_grad = jnp.stack(
        [jnp.where(second, view_other, view_own), jnp.where(second, view_own, view_other)], axis=1
    )
    return (image_grad, weight_grad)


def solution(mesh):
    return jax.shard_map(
        shards,
        mesh=mesh,
        in_specs=(P(("rep", "dp"), None, None), P(None, "dp")),
        out_specs=(P(("rep", "dp"), None, None), P(None, "dp")),
        check_vma=False,
    )
```

```python
import functools

import jax
import jax.numpy as jnp
from jax import lax
from jax.experimental import pallas as pl
from jax.experimental.pallas import tpu as pltpu
from jax.sharding import PartitionSpec as P

invariance_weight = 25.0
variance_weight = 25.0
covariance_weight = 1.0
loss_scale = 8192.0
epsilon_var = 0.0001

F32 = jnp.float32
BF16 = jnp.bfloat16
VMEM = pl.BlockSpec(memory_space=pltpu.VMEM)
SMEM = pl.BlockSpec(memory_space=pltpu.SMEM)
CORE, ACROSS, QUAD = 1, 2, 4
EXTRA = 8


def swap(block, axis, bits):
    return lax.ppermute(block, axis, [(i, i ^ bits) for i in range(lax.axis_size(axis))])


def slot_of(device, me, outer):
    rel = device ^ me
    return rel % QUAD * outer + rel // QUAD


def centre(z):
    return z - jnp.mean(z, axis=0, keepdims=True)


def nt_dot(a, b):
    return lax.dot_general(a, b, (((1,), (1,)), ((), ())), preferred_element_type=F32)


def half_masks(half, count):
    row = lax.broadcasted_iota(jnp.int32, (half, count), 0)
    lane = lax.broadcasted_iota(jnp.int32, (half, count), 1)
    return (lane < half) & (row < lane), row == lane, lane < half


def whole(near_ref, far_ref):
    return jnp.concatenate([near_ref[...], far_ref[...]], axis=0)


def split_kernel(me_ref, *refs):
    second = me_ref[0] % 2 == 1
    *image_refs, own_ref, other_ref = refs
    own = image_refs[0].shape[0]
    for i, ref in enumerate(image_refs):
        images = ref[...]
        view0, view1 = images[:, 0, :], images[:, 1, :]
        own_ref[i * own:(i + 1) * own] = jnp.where(second, view1, view0)
        other_ref[i * own:(i + 1) * own] = jnp.where(second, view0, view1)


def gram_kernel(own, me_ref, near_ref, far_ref, c_ref, packed_ref, sorted_ref):
    me = me_ref[0]
    count, width = c_ref.shape
    devices = count // own
    outer = devices // QUAD
    half = count // 2
    centred = centre(whole(near_ref, far_ref)).reshape(devices, own, width)
    for slot in range(devices):
        sorted_ref[(slot % outer * QUAD + slot // outer) ^ me] = centred[slot]
    c = sorted_ref[...].reshape(count, width).astype(BF16)
    c_ref[...] = c
    gram = nt_dot(c, c)
    upper, diagonal, _ = half_masks(half, count)
    turned = pltpu.roll(gram[half:], half, 1)
    packed_ref[:half] = jnp.where(upper, turned, gram[:half])
    second = jnp.sum(jnp.where(diagonal, turned, 0.0), axis=0, keepdims=True)
    packed_ref[half:] = jnp.broadcast_to(second, (EXTRA, count))


def unpack(packed_ref):
    count = packed_ref.shape[1]
    half = count // 2
    upper, diagonal, left = half_masks(half, count)
    top = packed_ref[:half]
    second = packed_ref[half:half + 1]
    mirror = jnp.swapaxes(jnp.concatenate([top, jnp.zeros_like(top)], axis=0), 0, 1)
    first = jnp.where(upper, mirror[:half], top)
    last = jnp.where(diagonal, second, jnp.where(upper, top, mirror[:half]))
    last = jnp.where(left, mirror[half:], pltpu.roll(last, half, 1))
    return jnp.concatenate([first, last], axis=0)


def base_kernel(scale, features, near_ref, far_ref, base_ref):
    count = base_ref.shape[0]
    coeff = scale * 4.0 * covariance_weight / (features * (count - 1))
    centred = centre(whole(near_ref, far_ref))
    variance = jnp.sum(centred * centred, axis=0, keepdims=True) / (count - 1)
    spread = jnp.sqrt(variance + epsilon_var)
    wide = centred.astype(BF16).astype(F32)
    diag_cov = jnp.sum(wide * wide, axis=0, keepdims=True) / (count - 1)
    var_coeff = jnp.where(
        spread < 1.0, -scale * variance_weight / (features * (count - 1)) / spread, 0.0
    )
    base_ref[...] = var_coeff * centred - coeff * diag_cov * wide


def grads_kernel(own, scale, features, me_ref, packed_ref, c_ref, near_ref, far_ref, other_ref,
                 base_ref, w_ref, grad_ref, send_ref, rel_ref):
    me = me_ref[0]
    count, width = c_ref.shape
    devices = count // own
    rest = unpack(packed_ref)
    through = 0.0
    for _ in range(3):
        piece = rest.astype(BF16)
        rest = rest - piece.astype(F32)
        through = through + jnp.dot(piece, c_ref[...], preferred_element_type=F32)
    for device in range(devices):
        rel_ref[slot_of(device, me, devices // QUAD)] = through[device * own:(device + 1) * own]
    coeff = scale * 4.0 * covariance_weight / (features * (count - 1))
    other = other_ref[...].reshape(2, 2, count // 4, width)
    other = jnp.concatenate([other[:, 1:], other[:, :1]], axis=1).reshape(count, width)
    gap = whole(near_ref, far_ref) - other
    inv_term = gap * (scale * 2.0 * invariance_weight / (count * features))
    through = rel_ref[...].reshape(count, width)
    grad = (inv_term + base_ref[...] + through * (coeff / (count - 1))).astype(BF16)
    grad_ref[...] = grad
    send_ref[...] = nt_dot(grad[count // 2:], w_ref[...]).astype(BF16)


def join_kernel(me_ref, own_ref, other_ref, out_ref):
    second = me_ref[0] % 2 == 1
    own, other = own_ref[...], other_ref[...]
    out_ref[:, 0, :] = jnp.where(second, other, own)
    out_ref[:, 1, :] = jnp.where(second, own, other)


def weight_operands(rows_ref, rows_core_ref, grad_ref, grad_core_ref):
    block = grad_core_ref.shape[1]
    rows = jnp.concatenate([rows_ref[...], rows_core_ref[...]], axis=0)
    return rows, jnp.concatenate([grad_ref[:, :block], grad_core_ref[...]], axis=0)


def tn_dot(a, b):
    return lax.dot_general(a, b, (((0,), (0,)), ((), ())), preferred_element_type=F32)


def weight_kernel(*refs):
    part = tn_dot(*weight_operands(*refs[:4]))
    refs[-1][...] = part + refs[4][...] if len(refs) > 5 else part


def last_weight_kernel(*refs):
    *operand_refs, earlier_ref, out_ref, sum_ref, sems = refs
    rows, grads = weight_operands(*operand_refs)
    bands, height, _ = sum_ref.shape
    copies = []
    for i in range(bands):
        band = slice(i * height, (i + 1) * height)
        sum_ref[i] = tn_dot(rows[:, band], grads) + earlier_ref[band]
        copies.append(pltpu.make_async_copy(sum_ref.at[i], out_ref.at[pl.ds(i * height, height)], sems.at[i]))
        copies[-1].start()
    for copy in copies:
        copy.wait()


def call(kernel, out_shape, specs, scratch=(), place=VMEM):
    return pl.pallas_call(
        kernel,
        out_shape=out_shape,
        in_specs=specs,
        out_specs=jax.tree.map(lambda _: place, out_shape),
        scratch_shapes=list(scratch),
        compiler_params=pltpu.CompilerParams(vmem_limit_bytes=32 * 1024 * 1024),
    )


def shards(images, weight):
    groups = lax.axis_size("rep")
    owners = lax.axis_size("dp")
    own, views, depth = images.shape
    block = weight.shape[1]
    width = 2 * block
    features = block * owners
    count = own * owners
    half = count // 2
    outer = owners // QUAD
    scale = loss_scale / groups
    position = lax.axis_index("dp")
    me = position.reshape(1)
    second = position % 2 == 1
    struct = jax.ShapeDtypeStruct

    def over_rep(array):
        return [
            lax.ppermute(array, "rep", [(i, (i + shift) % groups) for i in range(groups)])
            for shift in range(1, groups)
        ]

    def matmul(rows, matrix):
        return jnp.dot(rows, matrix, preferred_element_type=F32)

    weight_core = swap(weight, "dp", CORE)
    column = [swap(images, "dp", high * QUAD) for high in range(1, outer)]
    wide = jnp.concatenate([weight, weight_core], axis=1)
    column, wide = lax.optimization_barrier((column, wide))
    quarter = count // 4
    rows0, rows_other = call(
        split_kernel,
        (struct((quarter, depth), BF16), struct((quarter, depth), BF16)),
        [SMEM] + [VMEM] * outer,
    )(me, images, *column)
    rows1, rows2, rows3 = (
        swap(array, "dp", bits)
        for array, bits in ((rows_other, CORE), (rows0, ACROSS), (rows_other, ACROSS | CORE))
    )
    near = matmul(jnp.concatenate([rows0, rows1], axis=0), wide)
    near, rows2, rows3 = lax.optimization_barrier((near, rows2, rows3))
    far = matmul(jnp.concatenate([rows2, rows3], axis=0), wide)

    c, packed = call(
        functools.partial(gram_kernel, own),
        (struct((count, width), BF16), struct((half + EXTRA, count), F32)),
        [SMEM] + [VMEM] * 2,
        [pltpu.VMEM((owners, own, width), F32)],
    )(me, near, far)

    along, beside, corner = (swap(packed, "dp", bits) for bits in (ACROSS, QUAD, ACROSS | QUAD))
    packed = (packed + along) + (beside + corner)
    packed, near_late, far_late, rows = lax.optimization_barrier(
        (packed, near, far, jnp.concatenate([rows0, rows1, rows2, rows3], axis=0))
    )
    rows_core = swap(rows, "dp", CORE)
    base = call(
        functools.partial(base_kernel, scale, features), struct((count, width), F32), [VMEM] * 2
    )(near_late, far_late)
    base, sent = lax.optimization_barrier((base, rows))
    rows_others = over_rep(sent)
    other = matmul(rows_core, wide)
    bit = 2 * QUAD
    while bit < owners:
        received = swap(packed, "dp", bit)
        received, other, base = lax.optimization_barrier((received, other, base))
        packed = packed + received
        bit *= 2

    grad, send = call(
        functools.partial(grads_kernel, own, scale, features),
        (struct((count, width), BF16), struct((half, depth), BF16)),
        [SMEM] + [VMEM] * 7,
        [pltpu.VMEM((owners, own, width), F32)],
    )(me, packed, c, near, far, other, base, wide)

    received = swap(send, "dp", ACROSS)
    keep = nt_dot(grad[:half], wide)
    keep, grad = lax.optimization_barrier((keep, grad))
    grad_others = over_rep(grad)
    grad_core = swap(grad[:, block:], "dp", CORE)
    keep = (keep + received.astype(F32)).reshape(2, outer, own, depth)
    keep = [keep[:, high].reshape(2 * own, depth) for high in range(outer)]
    received = [swap(keep[high].astype(BF16), "dp", high * QUAD) for high in range(1, outer)]

    def weight_part(*operands):
        return call(weight_kernel, struct((depth, block), F32), [VMEM] * len(operands))(*operands)

    weight_grad = weight_part(rows, rows_core, grad, grad_core)
    received, weight_grad = lax.optimization_barrier((received, weight_grad))
    total = keep[0]
    for array in received:
        total = total + array.astype(F32)
    view_other = swap(total[own:], "dp", CORE)
    height = min(depth, 256)
    for left, (theirs, theirs_grad) in enumerate(zip(rows_others, grad_others), 2 - groups):
        operands = [
            theirs, swap(theirs, "dp", CORE),
            theirs_grad, swap(theirs_grad[:, block:], "dp", CORE), weight_grad,
        ]
        if left < 0:
            weight_grad = weight_part(*operands)
        else:
            weight_grad = call(
                last_weight_kernel, struct((depth, block), F32), [VMEM] * 5,
                [
                    pltpu.VMEM((depth // height, height, block), F32),
                    pltpu.SemaphoreType.DMA((depth // height,)),
                ],
                pl.BlockSpec(memory_space=pl.ANY),
            )(*operands)
    view_other, weight_grad = lax.optimization_barrier((view_other, weight_grad))
    image_grad = call(join_kernel, struct((own, views, depth), F32), [SMEM] + [VMEM] * 2)(
        me, total[:own], view_other
    )
    return (image_grad, weight_grad)


def solution(mesh):
    return jax.shard_map(
        shards,
        mesh=mesh,
        in_specs=(P(("rep", "dp"), None, None), P(None, "dp")),
        out_specs=(P(("rep", "dp"), None, None), P(None, "dp")),
        check_vma=False,
    )
```

```python
import functools

import jax
import jax.numpy as jnp
from jax import lax
from jax.experimental import pallas as pl
from jax.experimental.pallas import tpu as pltpu
from jax.sharding import PartitionSpec as P

invariance_weight = 25.0
variance_weight = 25.0
covariance_weight = 1.0
loss_scale = 8192.0
epsilon_var = 0.0001

F32 = jnp.float32
BF16 = jnp.bfloat16
VMEM = pl.BlockSpec(memory_space=pltpu.VMEM)
SMEM = pl.BlockSpec(memory_space=pltpu.SMEM)
CORE, ACROSS, QUAD = 1, 2, 4
EXTRA = 8


def swap(block, axis, bits):
    return lax.ppermute(block, axis, [(i, i ^ bits) for i in range(lax.axis_size(axis))])


def slot_of(device, me, outer):
    rel = device ^ me
    low, high = rel % QUAD, rel // QUAD
    return ((low // 2) * outer + high) * 2 + low % 2


def centre(z):
    return z - jnp.mean(z, axis=0, keepdims=True)


def nt_dot(a, b):
    return lax.dot_general(a, b, (((1,), (1,)), ((), ())), preferred_element_type=F32)


def half_masks(half, count):
    row = lax.broadcasted_iota(jnp.int32, (half, count), 0)
    lane = lax.broadcasted_iota(jnp.int32, (half, count), 1)
    return (lane < half) & (row < lane), row == lane, lane < half


def gram_kernel(own, me_ref, z0_ref, z1_ref, c_ref, packed_ref, sorted_ref):
    me = me_ref[0]
    count, width = c_ref.shape
    devices = count // own
    outer = devices // QUAD
    half = count // 2
    for block, ref in enumerate((z0_ref, z1_ref)):
        centred = centre(ref[...]).reshape(devices, own, width // 2)
        lanes = slice(block * width // 2, (block + 1) * width // 2)
        for slot in range(devices):
            rel = (slot // 2 % outer) * QUAD + (slot // 2 // outer) * 2 + slot % 2
            sorted_ref[rel ^ me, :, lanes] = centred[slot]
    c = sorted_ref[...].reshape(count, width).astype(BF16)
    c_ref[...] = c
    gram = nt_dot(c, c)
    upper, diagonal, _ = half_masks(half, count)
    turned = pltpu.roll(gram[half:], half, 1)
    packed_ref[:half] = jnp.where(upper, turned, gram[:half])
    second = jnp.sum(jnp.where(diagonal, turned, 0.0), axis=0, keepdims=True)
    packed_ref[half:] = jnp.broadcast_to(second, (EXTRA, count))


def unpack(packed_ref):
    count = packed_ref.shape[1]
    half = count // 2
    upper, diagonal, left = half_masks(half, count)
    top = packed_ref[:half]
    second = packed_ref[half:half + 1]
    mirror = jnp.swapaxes(jnp.concatenate([top, jnp.zeros_like(top)], axis=0), 0, 1)
    first = jnp.where(upper, mirror[:half], top)
    last = jnp.where(diagonal, second, jnp.where(upper, top, mirror[:half]))
    last = jnp.where(left, mirror[half:], pltpu.roll(last, half, 1))
    return jnp.concatenate([first, last], axis=0)


def base_kernel(scale, features, z0_ref, z1_ref, base_ref):
    count = base_ref.shape[0]
    coeff = scale * 4.0 * covariance_weight / (features * (count - 1))
    centred = centre(jnp.concatenate([z0_ref[...], z1_ref[...]], axis=1))
    variance = jnp.sum(centred * centred, axis=0, keepdims=True) / (count - 1)
    spread = jnp.sqrt(variance + epsilon_var)
    wide = centred.astype(BF16).astype(F32)
    diag_cov = jnp.sum(wide * wide, axis=0, keepdims=True) / (count - 1)
    var_coeff = jnp.where(
        spread < 1.0, -scale * variance_weight / (features * (count - 1)) / spread, 0.0
    )
    base_ref[...] = var_coeff * centred - coeff * diag_cov * wide


def grads_kernel(own, scale, features, me_ref, packed_ref, c_ref, z0_ref, z1_ref, other_ref,
                 base_ref, w_ref, grad_ref, send_ref, rel_ref):
    me = me_ref[0]
    count, width = c_ref.shape
    devices = count // own
    rest = unpack(packed_ref)
    through = 0.0
    for _ in range(3):
        piece = rest.astype(BF16)
        rest = rest - piece.astype(F32)
        through = through + jnp.dot(piece, c_ref[...], preferred_element_type=F32)
    for device in range(devices):
        rel_ref[slot_of(device, me, devices // QUAD)] = through[device * own:(device + 1) * own]
    coeff = scale * 4.0 * covariance_weight / (features * (count - 1))
    other = other_ref[...].reshape(devices // 2, 2, own, width)
    other = jnp.concatenate([other[:, 1:], other[:, :1]], axis=1).reshape(count, width)
    gap = jnp.concatenate([z0_ref[...], z1_ref[...]], axis=1) - other
    inv_term = gap * (scale * 2.0 * invariance_weight / (count * features))
    through = rel_ref[...].reshape(count, width)
    grad = (inv_term + base_ref[...] + through * (coeff / (count - 1))).astype(BF16)
    grad_ref[...] = grad
    send_ref[...] = nt_dot(grad[count // 2:], w_ref[...]).astype(BF16)


def join_kernel(me_ref, own_ref, other_ref, out_ref):
    second = me_ref[0] % 2 == 1
    own, other = own_ref[...], other_ref[...]
    out_ref[:, 0, :] = jnp.where(second, other, own)
    out_ref[:, 1, :] = jnp.where(second, own, other)


def weight_operands(rows_ref, rows_core_ref, grad_ref, grad_core_ref):
    block = grad_core_ref.shape[1]
    rows = jnp.concatenate([rows_ref[...], rows_core_ref[...]], axis=0)
    return rows, jnp.concatenate([grad_ref[:, :block], grad_core_ref[...]], axis=0)


def tn_dot(a, b):
    return lax.dot_general(a, b, (((0,), (0,)), ((), ())), preferred_element_type=F32)


def weight_kernel(*refs):
    part = tn_dot(*weight_operands(*refs[:4]))
    refs[-1][...] = part + refs[4][...] if len(refs) > 5 else part


def last_weight_kernel(*refs):
    *operand_refs, earlier_ref, out_ref, sum_ref, sems = refs
    rows, grads = weight_operands(*operand_refs)
    bands, height, _ = sum_ref.shape
    copies = []
    for i in range(bands):
        band = slice(i * height, (i + 1) * height)
        sum_ref[i] = tn_dot(rows[:, band], grads) + earlier_ref[band]
        copies.append(pltpu.make_async_copy(sum_ref.at[i], out_ref.at[pl.ds(i * height, height)], sems.at[i]))
        copies[-1].start()
    for copy in copies:
        copy.wait()


def call(kernel, out_shape, specs, scratch=(), place=VMEM):
    return pl.pallas_call(
        kernel,
        out_shape=out_shape,
        in_specs=specs,
        out_specs=jax.tree.map(lambda _: place, out_shape),
        scratch_shapes=list(scratch),
        compiler_params=pltpu.CompilerParams(vmem_limit_bytes=32 * 1024 * 1024),
    )


def shards(images, weight):
    groups = lax.axis_size("rep")
    owners = lax.axis_size("dp")
    own, views, depth = images.shape
    block = weight.shape[1]
    width = 2 * block
    features = block * owners
    count = own * owners
    half = count // 2
    lot = 2 * own
    outer = owners // QUAD
    scale = loss_scale / groups
    position = lax.axis_index("dp")
    me = position.reshape(1)
    second = position % 2 == 1
    struct = jax.ShapeDtypeStruct

    def over_rep(array):
        return [
            lax.ppermute(array, "rep", [(i, (i + shift) % groups) for i in range(groups)])
            for shift in range(1, groups)
        ]

    def matmul(rows, matrix):
        return jnp.dot(rows, matrix, preferred_element_type=F32)

    def own_view(array):
        return jnp.where(second, array[:, 1], array[:, 0])

    given = swap(images, "dp", CORE)
    weight_core = swap(weight, "dp", CORE)
    mine = jnp.concatenate([own_view(images), own_view(given)], axis=0)
    chips = [high * QUAD + across for across in (0, ACROSS) for high in range(outer)]
    rows = jnp.concatenate(
        [mine if bits == 0 else swap(mine, "dp", bits) for bits in chips], axis=0
    )
    z1, rows = lax.optimization_barrier((matmul(rows, weight_core), rows))
    z0 = matmul(rows, weight)

    c, packed = call(
        functools.partial(gram_kernel, own),
        (struct((count, width), BF16), struct((half + EXTRA, count), F32)),
        [SMEM] + [VMEM] * 2,
        [pltpu.VMEM((owners, own, width), F32)],
    )(me, z0, z1)

    along, beside, corner = (swap(packed, "dp", bits) for bits in (ACROSS, QUAD, ACROSS | QUAD))
    wide = jnp.concatenate([weight, weight_core], axis=1)
    along, beside, corner, wide = lax.optimization_barrier((along, beside, corner, wide))
    packed = (packed + along) + (beside + corner)
    packed, z0_late, z1_late, rows = lax.optimization_barrier((packed, z0, z1, rows))
    rows_core = swap(rows, "dp", CORE)
    base = call(
        functools.partial(base_kernel, scale, features), struct((count, width), F32), [VMEM] * 2
    )(z0_late, z1_late)
    base, sent = lax.optimization_barrier((base, rows))
    rows_others = over_rep(sent)
    other = matmul(rows_core, wide)
    bit = 2 * QUAD
    while bit < owners:
        received = swap(packed, "dp", bit)
        received, other, base = lax.optimization_barrier((received, other, base))
        packed = packed + received
        bit *= 2

    grad, send = call(
        functools.partial(grads_kernel, own, scale, features),
        (struct((count, width), BF16), struct((half, depth), BF16)),
        [SMEM] + [VMEM] * 7,
        [pltpu.VMEM((owners, own, width), F32)],
    )(me, packed, c, z0, z1, other, base, wide)

    def weight_part(*operands):
        return call(weight_kernel, struct((depth, block), F32), [VMEM] * len(operands))(*operands)

    received = swap(send, "dp", ACROSS)
    keep = nt_dot(grad[:half], wide)
    keep, grad = lax.optimization_barrier((keep, grad))
    grad_others = over_rep(grad)
    grad_core = swap(grad[:, block:], "dp", CORE)
    keep = (keep + received.astype(F32)).reshape(outer, lot, depth)
    received = [
        swap(keep[high].astype(BF16), "dp", high * QUAD) for high in range(1, outer)
    ]
    grad, grad_others = lax.optimization_barrier((grad, grad_others))
    weight_grad = weight_part(rows, rows_core, grad, grad_core)
    received, weight_grad = lax.optimization_barrier((received, weight_grad))
    total = keep[0]
    for array in received:
        total = total + array.astype(F32)
    view_other = swap(total[own:], "dp", CORE)
    height = min(depth, 256)
    for left, (theirs, theirs_grad) in enumerate(zip(rows_others, grad_others), 2 - groups):
        operands = [
            theirs, swap(theirs, "dp", CORE),
            theirs_grad, swap(theirs_grad[:, block:], "dp", CORE), weight_grad,
        ]
        if left < 0:
            weight_grad = weight_part(*operands)
        else:
            weight_grad = call(
                last_weight_kernel, struct((depth, block), F32), [VMEM] * 5,
                [
                    pltpu.VMEM((depth // height, height, block), F32),
                    pltpu.SemaphoreType.DMA((depth // height,)),
                ],
                pl.BlockSpec(memory_space=pl.ANY),
            )(*operands)
    view_other, weight_grad = lax.optimization_barrier((view_other, weight_grad))
    image_grad = call(join_kernel, struct((own, views, depth), F32), [SMEM] + [VMEM] * 2)(
        me, total[:own], view_other
    )
    return (image_grad, weight_grad)


def solution(mesh):
    return jax.shard_map(
        shards,
        mesh=mesh,
        in_specs=(P(("rep", "dp"), None, None), P(None, "dp")),
        out_specs=(P(("rep", "dp"), None, None), P(None, "dp")),
        check_vma=False,
    )
```

```python
import functools

import jax
import jax.numpy as jnp
from jax import lax
from jax.experimental import pallas as pl
from jax.experimental.pallas import tpu as pltpu
from jax.sharding import PartitionSpec as P

invariance_weight = 25.0
variance_weight = 25.0
covariance_weight = 1.0
loss_scale = 8192.0
epsilon_var = 0.0001

F32 = jnp.float32
BF16 = jnp.bfloat16
VMEM = pl.BlockSpec(memory_space=pltpu.VMEM)
SMEM = pl.BlockSpec(memory_space=pltpu.SMEM)
CORE, ACROSS, QUAD = 1, 2, 4
EXTRA = 8


def swap(block, axis, bits):
    return lax.ppermute(block, axis, [(i, i ^ bits) for i in range(lax.axis_size(axis))])


def slot_of(device, me, outer):
    rel = device ^ me
    low, high = rel % QUAD, rel // QUAD
    return ((low // 2) * outer + high) * 2 + low % 2


def centre(z):
    return z - jnp.mean(z, axis=0, keepdims=True)


def nt_dot(a, b):
    return lax.dot_general(a, b, (((1,), (1,)), ((), ())), preferred_element_type=F32)


def half_masks(half, count):
    row = lax.broadcasted_iota(jnp.int32, (half, count), 0)
    lane = lax.broadcasted_iota(jnp.int32, (half, count), 1)
    return (lane < half) & (row < lane), row == lane, lane < half


def whole(near_ref, far_ref):
    return jnp.concatenate([near_ref[...], far_ref[...]], axis=0)


def split_kernel(me_ref, *refs):
    second = me_ref[0] % 2 == 1
    *image_refs, rows_ref = refs
    own = image_refs[0].shape[0]
    parts = [jnp.where(second, ref[:, 1, :], ref[:, 0, :]) for ref in image_refs]
    rows_ref[...] = jnp.concatenate(parts, axis=0)


def gram_kernel(own, me_ref, near_ref, far_ref, c_ref, packed_ref, sorted_ref):
    me = me_ref[0]
    count, width = c_ref.shape
    devices = count // own
    outer = devices // QUAD
    half = count // 2
    centred = centre(whole(near_ref, far_ref)).reshape(devices, own, width)
    for slot in range(devices):
        rel = (slot // 2 % outer) * QUAD + (slot // 2 // outer) * 2 + slot % 2
        sorted_ref[rel ^ me] = centred[slot]
    c = sorted_ref[...].reshape(count, width).astype(BF16)
    c_ref[...] = c
    gram = nt_dot(c, c)
    upper, diagonal, _ = half_masks(half, count)
    turned = pltpu.roll(gram[half:], half, 1)
    packed_ref[:half] = jnp.where(upper, turned, gram[:half])
    second = jnp.sum(jnp.where(diagonal, turned, 0.0), axis=0, keepdims=True)
    packed_ref[half:] = jnp.broadcast_to(second, (EXTRA, count))


def unpack(packed_ref):
    count = packed_ref.shape[1]
    half = count // 2
    upper, diagonal, left = half_masks(half, count)
    top = packed_ref[:half]
    second = packed_ref[half:half + 1]
    mirror = jnp.swapaxes(jnp.concatenate([top, jnp.zeros_like(top)], axis=0), 0, 1)
    first = jnp.where(upper, mirror[:half], top)
    last = jnp.where(diagonal, second, jnp.where(upper, top, mirror[:half]))
    last = jnp.where(left, mirror[half:], pltpu.roll(last, half, 1))
    return jnp.concatenate([first, last], axis=0)


def base_kernel(scale, features, near_ref, far_ref, base_ref):
    count = base_ref.shape[0]
    coeff = scale * 4.0 * covariance_weight / (features * (count - 1))
    centred = centre(whole(near_ref, far_ref))
    variance = jnp.sum(centred * centred, axis=0, keepdims=True) / (count - 1)
    spread = jnp.sqrt(variance + epsilon_var)
    wide = centred.astype(BF16).astype(F32)
    diag_cov = jnp.sum(wide * wide, axis=0, keepdims=True) / (count - 1)
    var_coeff = jnp.where(
        spread < 1.0, -scale * variance_weight / (features * (count - 1)) / spread, 0.0
    )
    base_ref[...] = var_coeff * centred - coeff * diag_cov * wide


def grads_kernel(own, scale, features, me_ref, packed_ref, c_ref, near_ref, far_ref, other_ref,
                 base_ref, w_ref, grad_ref, send_ref, rel_ref):
    me = me_ref[0]
    count, width = c_ref.shape
    devices = count // own
    rest = unpack(packed_ref)
    through = 0.0
    for _ in range(2):
        piece = rest.astype(BF16)
        rest = rest - piece.astype(F32)
        through = through + jnp.dot(piece, c_ref[...], preferred_element_type=F32)
    for device in range(devices):
        rel_ref[slot_of(device, me, devices // QUAD)] = through[device * own:(device + 1) * own]
    coeff = scale * 4.0 * covariance_weight / (features * (count - 1))
    other = other_ref[...].reshape(devices // 2, 2, own, width)
    other = jnp.concatenate([other[:, 1:], other[:, :1]], axis=1).reshape(count, width)
    gap = whole(near_ref, far_ref) - other
    inv_term = gap * (scale * 2.0 * invariance_weight / (count * features))
    through = rel_ref[...].reshape(count, width)
    grad = (inv_term + base_ref[...] + through * (coeff / (count - 1))).astype(BF16)
    grad_ref[...] = grad
    send_ref[...] = nt_dot(grad[count // 2:], w_ref[...]).astype(BF16)


def join_kernel(me_ref, own_ref, other_ref, out_ref):
    second = me_ref[0] % 2 == 1
    own, other = own_ref[...], other_ref[...]
    out_ref[:, 0, :] = jnp.where(second, other, own)
    out_ref[:, 1, :] = jnp.where(second, own, other)


def weight_operands(rows_ref, rows_core_ref, grad_ref, grad_core_ref):
    block = grad_core_ref.shape[1]
    rows = jnp.concatenate([rows_ref[...], rows_core_ref[...]], axis=0)
    return rows, jnp.concatenate([grad_ref[:, :block], grad_core_ref[...]], axis=0)


def tn_dot(a, b):
    return lax.dot_general(a, b, (((0,), (0,)), ((), ())), preferred_element_type=F32)


def weight_kernel(*refs):
    part = tn_dot(*weight_operands(*refs[:4]))
    refs[-1][...] = part + refs[4][...] if len(refs) > 5 else part


def last_weight_kernel(*refs):
    *operand_refs, earlier_ref, out_ref, sum_ref, sems = refs
    rows, grads = weight_operands(*operand_refs)
    bands, height, _ = sum_ref.shape
    copies = []
    for i in range(bands):
        band = slice(i * height, (i + 1) * height)
        sum_ref[i] = tn_dot(rows[:, band], grads) + earlier_ref[band]
        copies.append(pltpu.make_async_copy(sum_ref.at[i], out_ref.at[pl.ds(i * height, height)], sems.at[i]))
        copies[-1].start()
    for copy in copies:
        copy.wait()


def call(kernel, out_shape, specs, scratch=(), place=VMEM):
    return pl.pallas_call(
        kernel,
        out_shape=out_shape,
        in_specs=specs,
        out_specs=jax.tree.map(lambda _: place, out_shape),
        scratch_shapes=list(scratch),
        compiler_params=pltpu.CompilerParams(vmem_limit_bytes=32 * 1024 * 1024),
    )


def shards(images, weight):
    groups = lax.axis_size("rep")
    owners = lax.axis_size("dp")
    own, views, depth = images.shape
    block = weight.shape[1]
    width = 2 * block
    features = block * owners
    count = own * owners
    half = count // 2
    lot = 2 * own
    outer = owners // QUAD
    scale = loss_scale / groups
    position = lax.axis_index("dp")
    me = position.reshape(1)
    struct = jax.ShapeDtypeStruct

    def over_rep(array):
        return [
            lax.ppermute(array, "rep", [(i, (i + shift) % groups) for i in range(groups)])
            for shift in range(1, groups)
        ]

    def matmul(rows, matrix):
        return jnp.dot(rows, matrix, preferred_element_type=F32)

    given = swap(images, "dp", CORE)
    weight_core = swap(weight, "dp", CORE)
    mine = call(split_kernel, struct((lot, depth), BF16), [SMEM] + [VMEM] * 2)(me, images, given)
    column = [swap(mine, "dp", high * QUAD) for high in range(1, outer)]
    wide = jnp.concatenate([weight, weight_core], axis=1)
    column, wide = lax.optimization_barrier((column, wide))
    column = jnp.concatenate([mine] + column, axis=0)
    across = swap(column, "dp", ACROSS)
    near = matmul(column, wide)
    near, across = lax.optimization_barrier((near, across))
    far = matmul(across, wide)

    c, packed = call(
        functools.partial(gram_kernel, own),
        (struct((count, width), BF16), struct((half + EXTRA, count), F32)),
        [SMEM] + [VMEM] * 2,
        [pltpu.VMEM((owners, own, width), F32)],
    )(me, near, far)

    along, beside, corner = (swap(packed, "dp", bits) for bits in (ACROSS, QUAD, ACROSS | QUAD))
    packed = (packed + along) + (beside + corner)
    packed, near_late, far_late, rows = lax.optimization_barrier(
        (packed, near, far, jnp.concatenate([column, across], axis=0))
    )
    rows_core = swap(rows, "dp", CORE)
    base = call(
        functools.partial(base_kernel, scale, features), struct((count, width), F32), [VMEM] * 2
    )(near_late, far_late)
    base, sent = lax.optimization_barrier((base, rows))
    rows_others = over_rep(sent)
    other = matmul(rows_core, wide)
    bit = 2 * QUAD
    while bit < owners:
        received = swap(packed, "dp", bit)
        received, other, base = lax.optimization_barrier((received, other, base))
        packed = packed + received
        bit *= 2

    grad, send = call(
        functools.partial(grads_kernel, own, scale, features),
        (struct((count, width), BF16), struct((half, depth), BF16)),
        [SMEM] + [VMEM] * 7,
        [pltpu.VMEM((owners, own, width), F32)],
    )(me, packed, c, near, far, other, base, wide)

    def weight_part(*operands):
        return call(weight_kernel, struct((depth, block), F32), [VMEM] * len(operands))(*operands)

    received = swap(send, "dp", ACROSS)
    keep = nt_dot(grad[:half], wide)
    keep, grad = lax.optimization_barrier((keep, grad))
    grad_others = over_rep(grad)
    grad_core = swap(grad[:, block:], "dp", CORE)
    keep = (keep + received.astype(F32)).reshape(outer, lot, depth)
    received = [
        swap(keep[high].astype(BF16), "dp", high * QUAD) for high in range(1, outer)
    ]
    grad, grad_others = lax.optimization_barrier((grad, grad_others))
    weight_grad = weight_part(rows, rows_core, grad, grad_core)
    received, weight_grad = lax.optimization_barrier((received, weight_grad))
    total = keep[0]
    for array in received:
        total = total + array.astype(F32)
    view_other = swap(total[own:], "dp", CORE)
    height = min(depth, 256)
    for left, (theirs, theirs_grad) in enumerate(zip(rows_others, grad_others), 2 - groups):
        operands = [
            theirs, swap(theirs, "dp", CORE),
            theirs_grad, swap(theirs_grad[:, block:], "dp", CORE), weight_grad,
        ]
        if left < 0:
            weight_grad = weight_part(*operands)
        else:
            weight_grad = call(
                last_weight_kernel, struct((depth, block), F32), [VMEM] * 5,
                [
                    pltpu.VMEM((depth // height, height, block), F32),
                    pltpu.SemaphoreType.DMA((depth // height,)),
                ],
                pl.BlockSpec(memory_space=pl.ANY),
            )(*operands)
    view_other, weight_grad = lax.optimization_barrier((view_other, weight_grad))
    image_grad = call(join_kernel, struct((own, views, depth), F32), [SMEM] + [VMEM] * 2)(
        me, total[:own], view_other
    )
    return (image_grad, weight_grad)


def solution(mesh):
    return jax.shard_map(
        shards,
        mesh=mesh,
        in_specs=(P(("rep", "dp"), None, None), P(None, "dp")),
        out_specs=(P(("rep", "dp"), None, None), P(None, "dp")),
        check_vma=False,
    )
```

```python
import functools

import jax
import jax.numpy as jnp
from jax import lax
from jax.experimental import pallas as pl
from jax.experimental.pallas import tpu as pltpu
from jax.sharding import PartitionSpec as P

invariance_weight = 25.0
variance_weight = 25.0
covariance_weight = 1.0
loss_scale = 8192.0
epsilon_var = 0.0001

F32 = jnp.float32
BF16 = jnp.bfloat16
VMEM = pl.BlockSpec(memory_space=pltpu.VMEM)
SMEM = pl.BlockSpec(memory_space=pltpu.SMEM)
CORE, ACROSS, QUAD = 1, 2, 4
EXTRA = 8


def swap(block, axis, bits):
    return lax.ppermute(block, axis, [(i, i ^ bits) for i in range(lax.axis_size(axis))])


def slot_of(device, me, outer):
    rel = device ^ me
    low, high = rel % QUAD, rel // QUAD
    return ((low // 2) * outer + high) * 2 + low % 2


def centre(z):
    return z - jnp.mean(z, axis=0, keepdims=True)


def nt_dot(a, b):
    return lax.dot_general(a, b, (((1,), (1,)), ((), ())), preferred_element_type=F32)


def half_masks(half, count):
    row = lax.broadcasted_iota(jnp.int32, (half, count), 0)
    lane = lax.broadcasted_iota(jnp.int32, (half, count), 1)
    return (lane < half) & (row < lane), row == lane, lane < half


def whole(near_ref, far_ref):
    return jnp.concatenate([near_ref[...], far_ref[...]], axis=0)


def pick_kernel(me_ref, images_ref, rows_ref):
    images = images_ref[...]
    rows_ref[...] = jnp.where(me_ref[0] % 2 == 1, images[:, 1, :], images[:, 0, :])


def pair_kernel(me_ref, rows_ref, images_ref, both_ref):
    images = images_ref[...]
    rows = jnp.where(me_ref[0] % 2 == 1, images[:, 1, :], images[:, 0, :])
    both_ref[...] = jnp.concatenate([rows_ref[...], rows], axis=0)


def gram_kernel(own, me_ref, near_ref, far_ref, c_ref, packed_ref, sorted_ref):
    me = me_ref[0]
    count, width = c_ref.shape
    devices = count // own
    outer = devices // QUAD
    half = count // 2
    centred = centre(whole(near_ref, far_ref)).reshape(devices, own, width)
    for slot in range(devices):
        rel = (slot // 2 % outer) * QUAD + (slot // 2 // outer) * 2 + slot % 2
        sorted_ref[rel ^ me] = centred[slot]
    c = sorted_ref[...].reshape(count, width).astype(BF16)
    c_ref[...] = c
    gram = nt_dot(c, c)
    upper, diagonal, _ = half_masks(half, count)
    turned = pltpu.roll(gram[half:], half, 1)
    packed_ref[:half] = jnp.where(upper, turned, gram[:half])
    second = jnp.sum(jnp.where(diagonal, turned, 0.0), axis=0, keepdims=True)
    packed_ref[half:] = jnp.broadcast_to(second, (EXTRA, count))


def unpack(packed_ref):
    count = packed_ref.shape[1]
    half = count // 2
    upper, diagonal, left = half_masks(half, count)
    top = packed_ref[:half]
    second = packed_ref[half:half + 1]
    mirror = jnp.swapaxes(jnp.concatenate([top, jnp.zeros_like(top)], axis=0), 0, 1)
    first = jnp.where(upper, mirror[:half], top)
    last = jnp.where(diagonal, second, jnp.where(upper, top, mirror[:half]))
    last = jnp.where(left, mirror[half:], pltpu.roll(last, half, 1))
    return jnp.concatenate([first, last], axis=0)


def base_kernel(scale, features, near_ref, far_ref, base_ref):
    count = base_ref.shape[0]
    coeff = scale * 4.0 * covariance_weight / (features * (count - 1))
    centred = centre(whole(near_ref, far_ref))
    variance = jnp.sum(centred * centred, axis=0, keepdims=True) / (count - 1)
    spread = jnp.sqrt(variance + epsilon_var)
    wide = centred.astype(BF16).astype(F32)
    diag_cov = jnp.sum(wide * wide, axis=0, keepdims=True) / (count - 1)
    var_coeff = jnp.where(
        spread < 1.0, -scale * variance_weight / (features * (count - 1)) / spread, 0.0
    )
    base_ref[...] = var_coeff * centred - coeff * diag_cov * wide


def grads_kernel(own, scale, features, me_ref, packed_ref, c_ref, near_ref, far_ref, other_ref,
                 base_ref, w_ref, grad_ref, send_ref, rel_ref):
    me = me_ref[0]
    count, width = c_ref.shape
    devices = count // own
    rest = unpack(packed_ref)
    through = 0.0
    for _ in range(2):
        piece = rest.astype(BF16)
        rest = rest - piece.astype(F32)
        through = through + jnp.dot(piece, c_ref[...], preferred_element_type=F32)
    for device in range(devices):
        rel_ref[slot_of(device, me, devices // QUAD)] = through[device * own:(device + 1) * own]
    coeff = scale * 4.0 * covariance_weight / (features * (count - 1))
    other = other_ref[...].reshape(devices // 2, 2, own, width)
    other = jnp.concatenate([other[:, 1:], other[:, :1]], axis=1).reshape(count, width)
    gap = whole(near_ref, far_ref) - other
    inv_term = gap * (scale * 2.0 * invariance_weight / (count * features))
    through = rel_ref[...].reshape(count, width)
    grad = (inv_term + base_ref[...] + through * (coeff / (count - 1))).astype(BF16)
    grad_ref[...] = grad
    send_ref[...] = nt_dot(grad[count // 2:], w_ref[...]).astype(BF16)


def join_kernel(me_ref, own_ref, other_ref, out_ref):
    second = me_ref[0] % 2 == 1
    own, other = own_ref[...], other_ref[...]
    out_ref[:, 0, :] = jnp.where(second, other, own)
    out_ref[:, 1, :] = jnp.where(second, own, other)


def weight_operands(rows_ref, rows_core_ref, grad_ref, grad_core_ref):
    block = grad_core_ref.shape[1]
    rows = jnp.concatenate([rows_ref[...], rows_core_ref[...]], axis=0)
    return rows, jnp.concatenate([grad_ref[:, :block], grad_core_ref[...]], axis=0)


def tn_dot(a, b):
    return lax.dot_general(a, b, (((0,), (0,)), ((), ())), preferred_element_type=F32)


def weight_kernel(*refs):
    part = tn_dot(*weight_operands(*refs[:4]))
    refs[-1][...] = part + refs[4][...] if len(refs) > 5 else part


def last_weight_kernel(*refs):
    *operand_refs, earlier_ref, out_ref, sum_ref, sems = refs
    rows, grads = weight_operands(*operand_refs)
    bands, height, _ = sum_ref.shape
    copies = []
    for i in range(bands):
        band = slice(i * height, (i + 1) * height)
        sum_ref[i] = tn_dot(rows[:, band], grads) + earlier_ref[band]
        copies.append(pltpu.make_async_copy(sum_ref.at[i], out_ref.at[pl.ds(i * height, height)], sems.at[i]))
        copies[-1].start()
    for copy in copies:
        copy.wait()


def call(kernel, out_shape, specs, scratch=(), place=VMEM):
    return pl.pallas_call(
        kernel,
        out_shape=out_shape,
        in_specs=specs,
        out_specs=jax.tree.map(lambda _: place, out_shape),
        scratch_shapes=list(scratch),
        compiler_params=pltpu.CompilerParams(vmem_limit_bytes=32 * 1024 * 1024),
    )


def shards(images, weight):
    groups = lax.axis_size("rep")
    owners = lax.axis_size("dp")
    own, views, depth = images.shape
    block = weight.shape[1]
    width = 2 * block
    features = block * owners
    count = own * owners
    half = count // 2
    lot = 2 * own
    outer = owners // QUAD
    scale = loss_scale / groups
    position = lax.axis_index("dp")
    me = position.reshape(1)
    struct = jax.ShapeDtypeStruct

    def over_rep(array):
        return [
            lax.ppermute(array, "rep", [(i, (i + shift) % groups) for i in range(groups)])
            for shift in range(1, groups)
        ]

    def matmul(rows, matrix):
        return jnp.dot(rows, matrix, preferred_element_type=F32)

    given = swap(images, "dp", CORE)
    mine = call(pick_kernel, struct((own, depth), BF16), [SMEM, VMEM])(me, images)
    given, mine, sent = lax.optimization_barrier((given, mine, weight))
    weight_core = swap(sent, "dp", CORE)
    mine = call(pair_kernel, struct((lot, depth), BF16), [SMEM] + [VMEM] * 2)(me, mine, given)
    column = [swap(mine, "dp", high * QUAD) for high in range(1, outer)]
    wide = jnp.concatenate([weight, weight_core], axis=1)
    column, wide = lax.optimization_barrier((column, wide))
    column = lax.optimization_barrier(jnp.concatenate([mine] + column, axis=0))
    across = swap(column, "dp", ACROSS)
    near = matmul(column, wide)
    near, across = lax.optimization_barrier((near, across))
    far = matmul(across, wide)

    c, packed = call(
        functools.partial(gram_kernel, own),
        (struct((count, width), BF16), struct((half + EXTRA, count), F32)),
        [SMEM] + [VMEM] * 2,
        [pltpu.VMEM((owners, own, width), F32)],
    )(me, near, far)

    along, beside, corner = (swap(packed, "dp", bits) for bits in (ACROSS, QUAD, ACROSS | QUAD))
    packed = (packed + along) + (beside + corner)
    packed, near_late, far_late, rows = lax.optimization_barrier(
        (packed, near, far, jnp.concatenate([column, across], axis=0))
    )
    rows_core = swap(rows, "dp", CORE)
    base = call(
        functools.partial(base_kernel, scale, features), struct((count, width), F32), [VMEM] * 2
    )(near_late, far_late)
    base, sent = lax.optimization_barrier((base, rows))
    rows_others = over_rep(sent)
    other = matmul(rows_core, wide)
    bit = 2 * QUAD
    while bit < owners:
        received = swap(packed, "dp", bit)
        received, other, base = lax.optimization_barrier((received, other, base))
        packed = packed + received
        bit *= 2

    grad, send = call(
        functools.partial(grads_kernel, own, scale, features),
        (struct((count, width), BF16), struct((half, depth), BF16)),
        [SMEM] + [VMEM] * 7,
        [pltpu.VMEM((owners, own, width), F32)],
    )(me, packed, c, near, far, other, base, wide)

    def weight_part(*operands):
        return call(weight_kernel, struct((depth, block), F32), [VMEM] * len(operands))(*operands)

    received = swap(send, "dp", ACROSS)
    keep = nt_dot(grad[:half], wide)
    keep, grad = lax.optimization_barrier((keep, grad))
    grad_others = over_rep(grad)
    grad_core = swap(grad[:, block:], "dp", CORE)
    keep = (keep + received.astype(F32)).reshape(outer, lot, depth)
    received = [
        swap(keep[high].astype(BF16), "dp", high * QUAD) for high in range(1, outer)
    ]
    grad, grad_others = lax.optimization_barrier((grad, grad_others))
    weight_grad = weight_part(rows, rows_core, grad, grad_core)
    received, weight_grad = lax.optimization_barrier((received, weight_grad))
    total = keep[0]
    for array in received:
        total = total + array.astype(F32)
    view_other = swap(total[own:], "dp", CORE)
    height = min(depth, 256)
    for left, (theirs, theirs_grad) in enumerate(zip(rows_others, grad_others), 2 - groups):
        operands = [
            theirs, swap(theirs, "dp", CORE),
            theirs_grad, swap(theirs_grad[:, block:], "dp", CORE), weight_grad,
        ]
        if left < 0:
            weight_grad = weight_part(*operands)
        else:
            weight_grad = call(
                last_weight_kernel, struct((depth, block), F32), [VMEM] * 5,
                [
                    pltpu.VMEM((depth // height, height, block), F32),
                    pltpu.SemaphoreType.DMA((depth // height,)),
                ],
                pl.BlockSpec(memory_space=pl.ANY),
            )(*operands)
    view_other, weight_grad = lax.optimization_barrier((view_other, weight_grad))
    image_grad = call(join_kernel, struct((own, views, depth), F32), [SMEM] + [VMEM] * 2)(
        me, total[:own], view_other
    )
    return (image_grad, weight_grad)


def solution(mesh):
    return jax.shard_map(
        shards,
        mesh=mesh,
        in_specs=(P(("rep", "dp"), None, None), P(None, "dp")),
        out_specs=(P(("rep", "dp"), None, None), P(None, "dp")),
        check_vma=False,
    )
```

```python
import functools

import jax
import jax.numpy as jnp
from jax import lax
from jax.experimental import pallas as pl
from jax.experimental.pallas import tpu as pltpu
from jax.sharding import PartitionSpec as P

invariance_weight = 25.0
variance_weight = 25.0
covariance_weight = 1.0
loss_scale = 8192.0
epsilon_var = 0.0001

F32 = jnp.float32
BF16 = jnp.bfloat16
VMEM = pl.BlockSpec(memory_space=pltpu.VMEM)
SMEM = pl.BlockSpec(memory_space=pltpu.SMEM)
CORE, ACROSS, QUAD = 1, 2, 4
EXTRA = 8


def swap(block, axis, bits):
    return lax.ppermute(block, axis, [(i, i ^ bits) for i in range(lax.axis_size(axis))])


def centre(z):
    return z - jnp.mean(z, axis=0, keepdims=True)


def nt_dot(a, b):
    return lax.dot_general(a, b, (((1,), (1,)), ((), ())), preferred_element_type=F32)


def half_masks(half, count):
    row = lax.broadcasted_iota(jnp.int32, (half, count), 0)
    lane = lax.broadcasted_iota(jnp.int32, (half, count), 1)
    return (lane < half) & (row < lane), row == lane, lane < half


def whole(near_ref, far_ref):
    return jnp.concatenate([near_ref[...], far_ref[...]], axis=0)


def pick_kernel(me_ref, images_ref, rows_ref):
    images = images_ref[...]
    rows_ref[...] = jnp.where(me_ref[0] % 2 == 1, images[:, 1, :], images[:, 0, :])


def pair_kernel(me_ref, rows_ref, images_ref, both_ref):
    images = images_ref[...]
    rows = jnp.where(me_ref[0] % 2 == 1, images[:, 1, :], images[:, 0, :])
    both_ref[...] = jnp.concatenate([rows_ref[...], rows], axis=0)


def gram_kernel(own, me_ref, near_ref, far_ref, c_ref, packed_ref, sorted_ref):
    me = me_ref[0]
    count, width = c_ref.shape
    devices = count // own
    outer = devices // QUAD
    half = count // 2
    centred = centre(whole(near_ref, far_ref)).reshape(devices, own, width)
    for slot in range(devices):
        rel = (slot // 2 % outer) * QUAD + (slot // 2 // outer) * 2 + slot % 2
        sorted_ref[rel ^ me] = centred[slot]
    c = sorted_ref[...].reshape(count, width).astype(BF16)
    c_ref[...] = c
    gram = nt_dot(c, c)
    upper, diagonal, _ = half_masks(half, count)
    turned = pltpu.roll(gram[half:], half, 1)
    packed_ref[:half] = jnp.where(upper, turned, gram[:half])
    second = jnp.sum(jnp.where(diagonal, turned, 0.0), axis=0, keepdims=True)
    packed_ref[half:] = jnp.broadcast_to(second, (EXTRA, count))


def unpack(packed_ref):
    count = packed_ref.shape[1]
    half = count // 2
    upper, diagonal, left = half_masks(half, count)
    top = packed_ref[:half]
    second = packed_ref[half:half + 1]
    mirror = jnp.swapaxes(jnp.concatenate([top, jnp.zeros_like(top)], axis=0), 0, 1)
    first = jnp.where(upper, mirror[:half], top)
    last = jnp.where(diagonal, second, jnp.where(upper, top, mirror[:half]))
    last = jnp.where(left, mirror[half:], pltpu.roll(last, half, 1))
    return first, last


def base_kernel(scale, features, near_ref, far_ref, base_ref):
    count = base_ref.shape[0]
    coeff = scale * 4.0 * covariance_weight / (features * (count - 1))
    centred = centre(whole(near_ref, far_ref))
    variance = jnp.sum(centred * centred, axis=0, keepdims=True) / (count - 1)
    spread = jnp.sqrt(variance + epsilon_var)
    wide = centred.astype(BF16).astype(F32)
    diag_cov = jnp.sum(wide * wide, axis=0, keepdims=True) / (count - 1)
    var_coeff = jnp.where(
        spread < 1.0, -scale * variance_weight / (features * (count - 1)) / spread, 0.0
    )
    base_ref[...] = var_coeff * centred - coeff * diag_cov * wide


def grads_kernel(own, scale, features, me_ref, packed_ref, c_ref, near_ref, far_ref, other_ref,
                 base_ref, w_ref, grad_ref, send_ref, gram_ref):
    me = me_ref[0]
    count, width = c_ref.shape
    devices = count // own
    half = count // 2
    first, last = unpack(packed_ref)
    gram_ref[:devices // 2] = first.reshape(devices // 2, own, count)
    gram_ref[devices // 2:] = last.reshape(devices // 2, own, count)
    order = [
        high * QUAD + across + core
        for across in (0, ACROSS) for high in range(devices // QUAD) for core in (0, CORE)
    ]
    rest = jnp.concatenate([gram_ref[rel ^ me] for rel in order], axis=0)
    through = 0.0
    for _ in range(2):
        piece = rest.astype(BF16)
        rest = rest - piece.astype(F32)
        through = through + jnp.dot(piece, c_ref[...], preferred_element_type=F32)
    coeff = scale * 4.0 * covariance_weight / (features * (count - 1))
    other = other_ref[...].reshape(devices // 2, 2, own, width)
    other = jnp.concatenate([other[:, 1:], other[:, :1]], axis=1).reshape(count, width)
    gap = whole(near_ref, far_ref) - other
    inv_term = gap * (scale * 2.0 * invariance_weight / (count * features))
    grad = (inv_term + base_ref[...] + through * (coeff / (count - 1))).astype(BF16)
    grad_ref[...] = grad
    send_ref[...] = nt_dot(grad[count // 2:], w_ref[...]).astype(BF16)


def join_kernel(me_ref, own_ref, other_ref, out_ref):
    second = me_ref[0] % 2 == 1
    own, other = own_ref[...], other_ref[...]
    out_ref[:, 0, :] = jnp.where(second, other, own)
    out_ref[:, 1, :] = jnp.where(second, own, other)


def weight_operands(rows_ref, rows_core_ref, grad_ref, grad_core_ref):
    block = grad_core_ref.shape[1]
    rows = jnp.concatenate([rows_ref[...], rows_core_ref[...]], axis=0)
    return rows, jnp.concatenate([grad_ref[:, :block], grad_core_ref[...]], axis=0)


def tn_dot(a, b):
    return lax.dot_general(a, b, (((0,), (0,)), ((), ())), preferred_element_type=F32)


def weight_kernel(*refs):
    part = tn_dot(*weight_operands(*refs[:4]))
    refs[-1][...] = part + refs[4][...] if len(refs) > 5 else part


def last_weight_kernel(*refs):
    *operand_refs, earlier_ref, out_ref, sum_ref, sems = refs
    rows, grads = weight_operands(*operand_refs)
    bands, height, _ = sum_ref.shape
    copies = []
    for i in range(bands):
        band = slice(i * height, (i + 1) * height)
        sum_ref[i] = tn_dot(rows[:, band], grads) + earlier_ref[band]
        copies.append(pltpu.make_async_copy(sum_ref.at[i], out_ref.at[pl.ds(i * height, height)], sems.at[i]))
        copies[-1].start()
    for copy in copies:
        copy.wait()


def call(kernel, out_shape, specs, scratch=(), place=VMEM):
    return pl.pallas_call(
        kernel,
        out_shape=out_shape,
        in_specs=specs,
        out_specs=jax.tree.map(lambda _: place, out_shape),
        scratch_shapes=list(scratch),
        compiler_params=pltpu.CompilerParams(vmem_limit_bytes=32 * 1024 * 1024),
    )


def shards(images, weight):
    groups = lax.axis_size("rep")
    owners = lax.axis_size("dp")
    own, views, depth = images.shape
    block = weight.shape[1]
    width = 2 * block
    features = block * owners
    count = own * owners
    half = count // 2
    lot = 2 * own
    outer = owners // QUAD
    scale = loss_scale / groups
    position = lax.axis_index("dp")
    me = position.reshape(1)
    struct = jax.ShapeDtypeStruct

    def over_rep(array):
        return [
            lax.ppermute(array, "rep", [(i, (i + shift) % groups) for i in range(groups)])
            for shift in range(1, groups)
        ]

    def matmul(rows, matrix):
        return jnp.dot(rows, matrix, preferred_element_type=F32)

    given = swap(images, "dp", CORE)
    mine = call(pick_kernel, struct((own, depth), BF16), [SMEM, VMEM])(me, images)
    given, mine, sent = lax.optimization_barrier((given, mine, weight))
    weight_core = swap(sent, "dp", CORE)
    mine = call(pair_kernel, struct((lot, depth), BF16), [SMEM] + [VMEM] * 2)(me, mine, given)
    column = [swap(mine, "dp", high * QUAD) for high in range(1, outer)]
    wide = jnp.concatenate([weight, weight_core], axis=1)
    column, wide = lax.optimization_barrier((column, wide))
    column = lax.optimization_barrier(jnp.concatenate([mine] + column, axis=0))
    across = swap(column, "dp", ACROSS)
    near = matmul(column, wide)
    near, across = lax.optimization_barrier((near, across))
    far = matmul(across, wide)

    c, packed = call(
        functools.partial(gram_kernel, own),
        (struct((count, width), BF16), struct((half + EXTRA, count), F32)),
        [SMEM] + [VMEM] * 2,
        [pltpu.VMEM((owners, own, width), F32)],
    )(me, near, far)

    top = owners // 2
    along, beside, corner = (swap(packed, "dp", bits) for bits in (ACROSS, top, ACROSS | top))
    packed = (packed + along) + (beside + corner)
    packed, near_late, far_late, rows = lax.optimization_barrier(
        (packed, near, far, jnp.concatenate([column, across], axis=0))
    )
    rows_core = swap(rows, "dp", CORE)
    base = call(
        functools.partial(base_kernel, scale, features), struct((count, width), F32), [VMEM] * 2
    )(near_late, far_late)
    base, sent = lax.optimization_barrier((base, rows))
    rows_others = over_rep(sent)
    other = matmul(rows_core, wide)
    bit = QUAD
    while bit < top:
        received = swap(packed, "dp", bit)
        received, other, base = lax.optimization_barrier((received, other, base))
        packed = packed + received
        bit *= 2

    grad, send = call(
        functools.partial(grads_kernel, own, scale, features),
        (struct((count, width), BF16), struct((half, depth), BF16)),
        [SMEM] + [VMEM] * 7,
        [pltpu.VMEM((owners, own, count), F32)],
    )(me, packed, c, near, far, other, base, wide)

    def weight_part(*operands):
        return call(weight_kernel, struct((depth, block), F32), [VMEM] * len(operands))(*operands)

    received = swap(send, "dp", ACROSS)
    keep = nt_dot(grad[:half], wide)
    keep, grad = lax.optimization_barrier((keep, grad))
    grad_others = over_rep(grad)
    grad_core = swap(grad[:, block:], "dp", CORE)
    keep = (keep + received.astype(F32)).reshape(outer, lot, depth)
    received = [
        swap(keep[high].astype(BF16), "dp", high * QUAD) for high in range(1, outer)
    ]
    grad, grad_others = lax.optimization_barrier((grad, grad_others))
    weight_grad = weight_part(rows, rows_core, grad, grad_core)
    received, weight_grad = lax.optimization_barrier((received, weight_grad))
    total = keep[0]
    for array in received:
        total = total + array.astype(F32)
    view_other = swap(total[own:], "dp", CORE)
    height = min(depth, 256)
    for left, (theirs, theirs_grad) in enumerate(zip(rows_others, grad_others), 2 - groups):
        operands = [
            theirs, swap(theirs, "dp", CORE),
            theirs_grad, swap(theirs_grad[:, block:], "dp", CORE), weight_grad,
        ]
        if left < 0:
            weight_grad = weight_part(*operands)
        else:
            weight_grad = call(
                last_weight_kernel, struct((depth, block), F32), [VMEM] * 5,
                [
                    pltpu.VMEM((depth // height, height, block), F32),
                    pltpu.SemaphoreType.DMA((depth // height,)),
                ],
                pl.BlockSpec(memory_space=pl.ANY),
            )(*operands)
    view_other, weight_grad = lax.optimization_barrier((view_other, weight_grad))
    image_grad = call(join_kernel, struct((own, views, depth), F32), [SMEM] + [VMEM] * 2)(
        me, total[:own], view_other
    )
    return (image_grad, weight_grad)


def solution(mesh):
    return jax.shard_map(
        shards,
        mesh=mesh,
        in_specs=(P(("rep", "dp"), None, None), P(None, "dp")),
        out_specs=(P(("rep", "dp"), None, None), P(None, "dp")),
        check_vma=False,
    )
```

```python
import functools

import jax
import jax.numpy as jnp
from jax import lax
from jax.experimental import pallas as pl
from jax.experimental.pallas import tpu as pltpu
from jax.sharding import PartitionSpec as P

invariance_weight = 25.0
variance_weight = 25.0
covariance_weight = 1.0
loss_scale = 8192.0
epsilon_var = 0.0001

F32 = jnp.float32
BF16 = jnp.bfloat16
VMEM = pl.BlockSpec(memory_space=pltpu.VMEM)
SMEM = pl.BlockSpec(memory_space=pltpu.SMEM)
CORE, ACROSS, QUAD = 1, 2, 4
EXTRA = 8


def swap(block, axis, bits):
    return lax.ppermute(block, axis, [(i, i ^ bits) for i in range(lax.axis_size(axis))])


def centre(z):
    return z - jnp.mean(z, axis=0, keepdims=True)


def nt_dot(a, b):
    return lax.dot_general(a, b, (((1,), (1,)), ((), ())), preferred_element_type=F32)


def half_masks(half, count):
    row = lax.broadcasted_iota(jnp.int32, (half, count), 0)
    lane = lax.broadcasted_iota(jnp.int32, (half, count), 1)
    return (lane < half) & (row < lane), row == lane, lane < half


def whole(near_ref, far_ref):
    return jnp.concatenate([near_ref[...], far_ref[...]], axis=0)


def pick_kernel(me_ref, images_ref, rows_ref):
    images = images_ref[...]
    rows_ref[...] = jnp.where(me_ref[0] % 2 == 1, images[:, 1, :], images[:, 0, :])


def pair_kernel(me_ref, rows_ref, images_ref, both_ref):
    images = images_ref[...]
    rows = jnp.where(me_ref[0] % 2 == 1, images[:, 1, :], images[:, 0, :])
    both_ref[...] = jnp.concatenate([rows_ref[...], rows], axis=0)


def gram_kernel(own, me_ref, near_ref, far_ref, c_ref, packed_ref, sorted_ref):
    me = me_ref[0]
    count, width = c_ref.shape
    devices = count // own
    outer = devices // QUAD
    half = count // 2
    centred = centre(whole(near_ref, far_ref)).reshape(devices, own, width)
    for slot in range(devices):
        rel = (slot // 2 % outer) * QUAD + (slot // 2 // outer) * 2 + slot % 2
        sorted_ref[rel ^ me] = centred[slot]
    c = sorted_ref[...].reshape(count, width).astype(BF16)
    c_ref[...] = c
    gram = nt_dot(c, c)
    upper, diagonal, _ = half_masks(half, count)
    turned = pltpu.roll(gram[half:], half, 1)
    packed_ref[:half] = jnp.where(upper, turned, gram[:half])
    second = jnp.sum(jnp.where(diagonal, turned, 0.0), axis=0, keepdims=True)
    packed_ref[half:] = jnp.broadcast_to(second, (EXTRA, count))


def unpack(packed_ref):
    count = packed_ref.shape[1]
    half = count // 2
    upper, diagonal, left = half_masks(half, count)
    top = packed_ref[:half]
    second = packed_ref[half:half + 1]
    mirror = jnp.swapaxes(jnp.concatenate([top, jnp.zeros_like(top)], axis=0), 0, 1)
    first = jnp.where(upper, mirror[:half], top)
    last = jnp.where(diagonal, second, jnp.where(upper, top, mirror[:half]))
    last = jnp.where(left, mirror[half:], pltpu.roll(last, half, 1))
    return first, last


def base_kernel(scale, features, near_ref, far_ref, base_ref):
    count = base_ref.shape[0]
    coeff = scale * 4.0 * covariance_weight / (features * (count - 1))
    centred = centre(whole(near_ref, far_ref))
    variance = jnp.sum(centred * centred, axis=0, keepdims=True) / (count - 1)
    spread = jnp.sqrt(variance + epsilon_var)
    wide = centred.astype(BF16).astype(F32)
    diag_cov = jnp.sum(wide * wide, axis=0, keepdims=True) / (count - 1)
    var_coeff = jnp.where(
        spread < 1.0, -scale * variance_weight / (features * (count - 1)) / spread, 0.0
    )
    base_ref[...] = var_coeff * centred - coeff * diag_cov * wide


def grads_kernel(own, scale, features, me_ref, packed_ref, c_ref, near_ref, far_ref, other_ref,
                 base_ref, w_ref, grad_ref, send_ref, gram_ref):
    me = me_ref[0]
    count, width = c_ref.shape
    devices = count // own
    half = count // 2
    first, last = unpack(packed_ref)
    gram_ref[:devices // 2] = first.reshape(devices // 2, own, count)
    gram_ref[devices // 2:] = last.reshape(devices // 2, own, count)
    order = [
        high * QUAD + across + core
        for across in (0, ACROSS) for high in range(devices // QUAD) for core in (0, CORE)
    ]
    rest = jnp.concatenate([gram_ref[rel ^ me] for rel in order], axis=0)
    through = 0.0
    for _ in range(2):
        piece = rest.astype(BF16)
        rest = rest - piece.astype(F32)
        through = through + jnp.dot(piece, c_ref[...], preferred_element_type=F32)
    coeff = scale * 4.0 * covariance_weight / (features * (count - 1))
    other = other_ref[...].reshape(devices // 2, 2, own, width)
    other = jnp.concatenate([other[:, 1:], other[:, :1]], axis=1).reshape(count, width)
    gap = whole(near_ref, far_ref) - other
    inv_term = gap * (scale * 2.0 * invariance_weight / (count * features))
    grad = (inv_term + base_ref[...] + through * (coeff / (count - 1))).astype(BF16)
    grad_ref[...] = grad
    send_ref[...] = nt_dot(grad[count // 2:], w_ref[...]).astype(BF16)


def join_kernel(me_ref, own_ref, other_ref, out_ref):
    second = me_ref[0] % 2 == 1
    own, other = own_ref[...], other_ref[...]
    out_ref[:, 0, :] = jnp.where(second, other, own)
    out_ref[:, 1, :] = jnp.where(second, own, other)


def weight_kernel(first, height, *refs):
    *operand_refs, out_ref, band_ref, sems = refs
    operands = [
        [jnp.concatenate([refs[i + j][...], refs[i + j + 1][...]], axis=0) for j in (0, 2)]
        for i in range(0, len(operand_refs) // 4 * 4, 4)
    ]
    copies = []
    for i in range(band_ref.shape[0]):
        start = (first + i) * height
        band = [
            lax.dot_general(
                rows[:, start:start + height], grads, (((0,), (0,)), ((), ())),
                preferred_element_type=F32,
            )
            for rows, grads in operands
        ]
        band_ref[i] = functools.reduce(jnp.add, band)
        copy = pltpu.make_async_copy(band_ref.at[i], out_ref.at[pl.ds(start, height)], sems.at[i])
        copy.start()
        copies.append(copy)
    for copy in copies:
        copy.wait()


def call(kernel, out_shape, specs, scratch=(), place=VMEM, aliases=()):
    return pl.pallas_call(
        kernel,
        out_shape=out_shape,
        in_specs=specs,
        out_specs=jax.tree.map(lambda _: place, out_shape),
        scratch_shapes=list(scratch),
        input_output_aliases=dict(aliases),
        compiler_params=pltpu.CompilerParams(vmem_limit_bytes=32 * 1024 * 1024),
    )


def shards(images, weight):
    groups = lax.axis_size("rep")
    owners = lax.axis_size("dp")
    own, views, depth = images.shape
    block = weight.shape[1]
    width = 2 * block
    features = block * owners
    count = own * owners
    half = count // 2
    lot = 2 * own
    outer = owners // QUAD
    scale = loss_scale / groups
    position = lax.axis_index("dp")
    me = position.reshape(1)
    struct = jax.ShapeDtypeStruct

    def over_rep(array):
        return [
            lax.ppermute(array, "rep", [(i, (i + shift) % groups) for i in range(groups)])
            for shift in range(1, groups)
        ]

    def matmul(rows, matrix):
        return jnp.dot(rows, matrix, preferred_element_type=F32)

    given = swap(images, "dp", CORE)
    mine = call(pick_kernel, struct((own, depth), BF16), [SMEM, VMEM])(me, images)
    given, mine, sent = lax.optimization_barrier((given, mine, weight))
    weight_core = swap(sent, "dp", CORE)
    mine = call(pair_kernel, struct((lot, depth), BF16), [SMEM] + [VMEM] * 2)(me, mine, given)
    column = [swap(mine, "dp", high * QUAD) for high in range(1, outer)]
    wide = jnp.concatenate([weight, weight_core], axis=1)
    column, wide = lax.optimization_barrier((column, wide))
    column = lax.optimization_barrier(jnp.concatenate([mine] + column, axis=0))
    across = swap(column, "dp", ACROSS)
    near = matmul(column, wide)
    near, across = lax.optimization_barrier((near, across))
    far = matmul(across, wide)

    c, packed = call(
        functools.partial(gram_kernel, own),
        (struct((count, width), BF16), struct((half + EXTRA, count), F32)),
        [SMEM] + [VMEM] * 2,
        [pltpu.VMEM((owners, own, width), F32)],
    )(me, near, far)

    top = owners // 2
    along, beside, corner = (swap(packed, "dp", bits) for bits in (ACROSS, top, ACROSS | top))
    packed = (packed + along) + (beside + corner)
    packed, near_late, far_late, rows = lax.optimization_barrier(
        (packed, near, far, jnp.concatenate([column, across], axis=0))
    )
    rows_core = swap(rows, "dp", CORE)
    base = call(
        functools.partial(base_kernel, scale, features), struct((count, width), F32), [VMEM] * 2
    )(near_late, far_late)
    base, sent = lax.optimization_barrier((base, rows))
    rows_others = over_rep(sent)
    other = matmul(rows_core, wide)
    bit = QUAD
    while bit < top:
        received = swap(packed, "dp", bit)
        received, other, base = lax.optimization_barrier((received, other, base))
        packed = packed + received
        bit *= 2

    grad, send = call(
        functools.partial(grads_kernel, own, scale, features),
        (struct((count, width), BF16), struct((half, depth), BF16)),
        [SMEM] + [VMEM] * 7,
        [pltpu.VMEM((owners, own, count), F32)],
    )(me, packed, c, near, far, other, base, wide)

    received = swap(send, "dp", ACROSS)
    keep = nt_dot(grad[:half], wide)
    keep, grad = lax.optimization_barrier((keep, grad))
    grad_core = swap(grad[:, block:], "dp", CORE)
    grad = grad[:, :block]
    grad_others, grad_core_others = over_rep(grad), over_rep(grad_core)
    keep = (keep + received.astype(F32)).reshape(outer, lot, depth)
    received = [
        swap(keep[high].astype(BF16), "dp", high * QUAD) for high in range(1, outer)
    ]
    operands = [rows, rows_core, grad, grad_core]
    for theirs, *theirs_grads in zip(rows_others, grad_others, grad_core_others):
        operands += [theirs, swap(theirs, "dp", CORE), *theirs_grads]
    height = min(depth, 256)
    bands = depth // height
    early = bands * 2 // 5

    def weight_bands(first, amount, *earlier):
        anywhere = pl.BlockSpec(memory_space=pl.ANY)
        return call(
            functools.partial(weight_kernel, first, height), struct((depth, block), F32),
            [VMEM] * len(operands) + [anywhere] * len(earlier),
            [pltpu.VMEM((amount, height, block), F32), pltpu.SemaphoreType.DMA((amount,))],
            anywhere, [(len(operands), 0)] if earlier else (),
        )(*operands, *earlier)

    weight_grad = weight_bands(0, early)
    received, weight_grad = lax.optimization_barrier((received, weight_grad))
    total = keep[0]
    for array in received:
        total = total + array.astype(F32)
    view_other = swap(total[own:], "dp", CORE)
    weight_grad = weight_bands(early, bands - early, weight_grad)
    view_other, weight_grad = lax.optimization_barrier((view_other, weight_grad))
    image_grad = call(join_kernel, struct((own, views, depth), F32), [SMEM] + [VMEM] * 2)(
        me, total[:own], view_other
    )
    return (image_grad, weight_grad)


def solution(mesh):
    return jax.shard_map(
        shards,
        mesh=mesh,
        in_specs=(P(("rep", "dp"), None, None), P(None, "dp")),
        out_specs=(P(("rep", "dp"), None, None), P(None, "dp")),
        check_vma=False,
    )
```

```python
import functools

import jax
import jax.numpy as jnp
from jax import lax
from jax.experimental import pallas as pl
from jax.experimental.pallas import tpu as pltpu
from jax.sharding import PartitionSpec as P

invariance_weight = 25.0
variance_weight = 25.0
covariance_weight = 1.0
loss_scale = 8192.0
epsilon_var = 0.0001

F32 = jnp.float32
BF16 = jnp.bfloat16
VMEM = pl.BlockSpec(memory_space=pltpu.VMEM)
SMEM = pl.BlockSpec(memory_space=pltpu.SMEM)
CORE, ACROSS, QUAD = 1, 2, 4
EXTRA = 8


def swap(block, axis, bits):
    return lax.ppermute(block, axis, [(i, i ^ bits) for i in range(lax.axis_size(axis))])


def centre(z):
    return z - jnp.mean(z, axis=0, keepdims=True)


def nt_dot(a, b):
    return lax.dot_general(a, b, (((1,), (1,)), ((), ())), preferred_element_type=F32)


def half_masks(half, count):
    row = lax.broadcasted_iota(jnp.int32, (half, count), 0)
    lane = lax.broadcasted_iota(jnp.int32, (half, count), 1)
    return (lane < half) & (row < lane), row == lane, lane < half


def whole(near_ref, far_ref):
    return jnp.concatenate([near_ref[...], far_ref[...]], axis=0)


def pick_kernel(me_ref, images_ref, rows_ref):
    images = images_ref[...]
    rows_ref[...] = jnp.where(me_ref[0] % 2 == 1, images[:, 1, :], images[:, 0, :])


def pair_kernel(me_ref, rows_ref, images_ref, both_ref):
    images = images_ref[...]
    rows = jnp.where(me_ref[0] % 2 == 1, images[:, 1, :], images[:, 0, :])
    both_ref[...] = jnp.concatenate([rows_ref[...], rows], axis=0)


def gram_kernel(own, me_ref, near_ref, across_ref, w_ref, c_ref, packed_ref, far_ref, sorted_ref):
    me = me_ref[0]
    count, width = c_ref.shape
    devices = count // own
    outer = devices // QUAD
    half = count // 2
    far = jnp.dot(across_ref[...], w_ref[...], preferred_element_type=F32)
    far_ref[...] = far
    near = near_ref[...]
    total = jnp.sum(near, axis=0, keepdims=True) + jnp.sum(far, axis=0, keepdims=True)
    mean = total / count
    for x, z in enumerate((near, far)):
        centred = (z - mean).reshape(devices // 2, own, width)
        for slot in range(devices // 2):
            rel = (slot // 2) * QUAD + x * ACROSS + slot % 2
            sorted_ref[rel ^ me] = centred[slot]
    c = sorted_ref[...].reshape(count, width).astype(BF16)
    c_ref[...] = c
    gram = nt_dot(c, c)
    upper, diagonal, _ = half_masks(half, count)
    turned = pltpu.roll(gram[half:], half, 1)
    packed_ref[:half] = jnp.where(upper, turned, gram[:half])
    second = jnp.sum(jnp.where(diagonal, turned, 0.0), axis=0, keepdims=True)
    packed_ref[half:] = jnp.broadcast_to(second, (EXTRA, count))


def unpack(packed_ref):
    count = packed_ref.shape[1]
    half = count // 2
    upper, diagonal, left = half_masks(half, count)
    top = packed_ref[:half]
    second = packed_ref[half:half + 1]
    mirror = jnp.swapaxes(jnp.concatenate([top, jnp.zeros_like(top)], axis=0), 0, 1)
    first = jnp.where(upper, mirror[:half], top)
    last = jnp.where(diagonal, second, jnp.where(upper, top, mirror[:half]))
    last = jnp.where(left, mirror[half:], pltpu.roll(last, half, 1))
    return first, last


def base_kernel(scale, features, near_ref, far_ref, base_ref):
    count = base_ref.shape[0]
    coeff = scale * 4.0 * covariance_weight / (features * (count - 1))
    centred = centre(whole(near_ref, far_ref))
    variance = jnp.sum(centred * centred, axis=0, keepdims=True) / (count - 1)
    spread = jnp.sqrt(variance + epsilon_var)
    wide = centred.astype(BF16).astype(F32)
    diag_cov = jnp.sum(wide * wide, axis=0, keepdims=True) / (count - 1)
    var_coeff = jnp.where(
        spread < 1.0, -scale * variance_weight / (features * (count - 1)) / spread, 0.0
    )
    base_ref[...] = var_coeff * centred - coeff * diag_cov * wide


def other_kernel(own, scale, features, rows_ref, w_ref, near_ref, far_ref, base_ref, out_ref):
    count, width = out_ref.shape
    other = jnp.dot(rows_ref[...], w_ref[...], preferred_element_type=F32)
    other = other.reshape(count // (2 * own), 2, own, width)
    other = jnp.concatenate([other[:, 1:], other[:, :1]], axis=1).reshape(count, width)
    inv_term = (whole(near_ref, far_ref) - other) * (
        scale * 2.0 * invariance_weight / (count * features)
    )
    out_ref[...] = inv_term + base_ref[...]


def grads_kernel(own, scale, features, me_ref, packed_ref, c_ref, base_ref, w_ref,
                 grad_ref, send_ref, gram_ref):
    me = me_ref[0]
    count, width = c_ref.shape
    devices = count // own
    half = count // 2
    first, last = unpack(packed_ref)
    gram_ref[:devices // 2] = first.reshape(devices // 2, own, count)
    gram_ref[devices // 2:] = last.reshape(devices // 2, own, count)
    order = [
        high * QUAD + across + core
        for across in (0, ACROSS) for high in range(devices // QUAD) for core in (0, CORE)
    ]
    rest = jnp.concatenate([gram_ref[rel ^ me] for rel in order], axis=0)
    through = 0.0
    for _ in range(2):
        piece = rest.astype(BF16)
        rest = rest - piece.astype(F32)
        through = through + jnp.dot(piece, c_ref[...], preferred_element_type=F32)
    coeff = scale * 4.0 * covariance_weight / (features * (count - 1))
    grad = (base_ref[...] + through * (coeff / (count - 1))).astype(BF16)
    grad_ref[...] = grad
    send_ref[...] = nt_dot(grad[count // 2:], w_ref[...]).astype(BF16)


def join_kernel(me_ref, own_ref, other_ref, out_ref):
    second = me_ref[0] % 2 == 1
    own, other = own_ref[...], other_ref[...]
    out_ref[:, 0, :] = jnp.where(second, other, own)
    out_ref[:, 1, :] = jnp.where(second, own, other)


def weight_operands(rows_ref, rows_core_ref, grad_ref, grad_core_ref):
    block = grad_core_ref.shape[1]
    rows = jnp.concatenate([rows_ref[...], rows_core_ref[...]], axis=0)
    return rows, jnp.concatenate([grad_ref[:, :block], grad_core_ref[...]], axis=0)


def tn_dot(a, b):
    return lax.dot_general(a, b, (((0,), (0,)), ((), ())), preferred_element_type=F32)


def weight_kernel(*refs):
    part = tn_dot(*weight_operands(*refs[:4]))
    refs[-1][...] = part + refs[4][...] if len(refs) > 5 else part


def last_weight_kernel(*refs):
    *operand_refs, earlier_ref, out_ref, sum_ref, sems = refs
    rows, grads = weight_operands(*operand_refs)
    bands, height, _ = sum_ref.shape
    copies = []
    for i in range(bands):
        band = slice(i * height, (i + 1) * height)
        sum_ref[i] = tn_dot(rows[:, band], grads) + earlier_ref[band]
        copies.append(pltpu.make_async_copy(sum_ref.at[i], out_ref.at[pl.ds(i * height, height)], sems.at[i]))
        copies[-1].start()
    for copy in copies:
        copy.wait()


def call(kernel, out_shape, specs, scratch=(), place=VMEM):
    return pl.pallas_call(
        kernel,
        out_shape=out_shape,
        in_specs=specs,
        out_specs=jax.tree.map(lambda _: place, out_shape),
        scratch_shapes=list(scratch),
        compiler_params=pltpu.CompilerParams(vmem_limit_bytes=32 * 1024 * 1024),
    )


def shards(images, weight):
    groups = lax.axis_size("rep")
    owners = lax.axis_size("dp")
    own, views, depth = images.shape
    block = weight.shape[1]
    width = 2 * block
    features = block * owners
    count = own * owners
    half = count // 2
    lot = 2 * own
    outer = owners // QUAD
    scale = loss_scale / groups
    position = lax.axis_index("dp")
    me = position.reshape(1)
    struct = jax.ShapeDtypeStruct

    def over_rep(array):
        return [
            lax.ppermute(array, "rep", [(i, (i + shift) % groups) for i in range(groups)])
            for shift in range(1, groups)
        ]

    def matmul(rows, matrix):
        return jnp.dot(rows, matrix, preferred_element_type=F32)

    given = swap(images, "dp", CORE)
    mine = call(pick_kernel, struct((own, depth), BF16), [SMEM, VMEM])(me, images)
    given, mine, sent = lax.optimization_barrier((given, mine, weight))
    weight_core = swap(sent, "dp", CORE)
    mine = call(pair_kernel, struct((lot, depth), BF16), [SMEM] + [VMEM] * 2)(me, mine, given)
    column = [swap(mine, "dp", high * QUAD) for high in range(1, outer)]
    wide = jnp.concatenate([weight, weight_core], axis=1)
    column, wide = lax.optimization_barrier((column, wide))
    column = lax.optimization_barrier(jnp.concatenate([mine] + column, axis=0))
    across = swap(column, "dp", ACROSS)
    near = matmul(column, wide)
    near, across = lax.optimization_barrier((near, across))

    c, packed, far = call(
        functools.partial(gram_kernel, own),
        (
            struct((count, width), BF16),
            struct((half + EXTRA, count), F32),
            struct((half, width), F32),
        ),
        [SMEM] + [VMEM] * 3,
        [pltpu.VMEM((owners, own, width), F32)],
    )(me, near, across, wide)

    top = owners // 2
    along, beside, corner = (swap(packed, "dp", bits) for bits in (ACROSS, top, ACROSS | top))
    packed = (packed + along) + (beside + corner)
    packed, near_late, far_late, rows = lax.optimization_barrier(
        (packed, near, far, jnp.concatenate([column, across], axis=0))
    )
    rows_core = swap(rows, "dp", CORE)
    base = call(
        functools.partial(base_kernel, scale, features), struct((count, width), F32), [VMEM] * 2
    )(near_late, far_late)
    base, sent = lax.optimization_barrier((base, rows))
    rows_others = over_rep(sent)
    base = call(
        functools.partial(other_kernel, own, scale, features), struct((count, width), F32),
        [VMEM] * 5,
    )(rows_core, wide, near, far, base)
    bit = QUAD
    while bit < top:
        received = swap(packed, "dp", bit)
        received, base = lax.optimization_barrier((received, base))
        packed = packed + received
        bit *= 2

    grad, send = call(
        functools.partial(grads_kernel, own, scale, features),
        (struct((count, width), BF16), struct((half, depth), BF16)),
        [SMEM] + [VMEM] * 4,
        [pltpu.VMEM((owners, own, count), F32)],
    )(me, packed, c, base, wide)

    def weight_part(*operands):
        return call(weight_kernel, struct((depth, block), F32), [VMEM] * len(operands))(*operands)

    received = swap(send, "dp", ACROSS)
    keep = nt_dot(grad[:half], wide)
    keep, grad = lax.optimization_barrier((keep, grad))
    grad_others = over_rep(grad)
    grad_core = swap(grad[:, block:], "dp", CORE)
    keep = (keep + received.astype(F32)).reshape(outer, lot, depth)
    received = [
        swap(keep[high].astype(BF16), "dp", high * QUAD) for high in range(1, outer)
    ]
    grad, grad_others = lax.optimization_barrier((grad, grad_others))
    weight_grad = weight_part(rows, rows_core, grad, grad_core)
    received, weight_grad = lax.optimization_barrier((received, weight_grad))
    total = keep[0]
    for array in received:
        total = total + array.astype(F32)
    view_other = swap(total[own:], "dp", CORE)
    height = min(depth, 256)
    for left, (theirs, theirs_grad) in enumerate(zip(rows_others, grad_others), 2 - groups):
        operands = [
            theirs, swap(theirs, "dp", CORE),
            theirs_grad, swap(theirs_grad[:, block:], "dp", CORE), weight_grad,
        ]
        if left < 0:
            weight_grad = weight_part(*operands)
        else:
            weight_grad = call(
                last_weight_kernel, struct((depth, block), F32), [VMEM] * 5,
                [
                    pltpu.VMEM((depth // height, height, block), F32),
                    pltpu.SemaphoreType.DMA((depth // height,)),
                ],
                pl.BlockSpec(memory_space=pl.ANY),
            )(*operands)
    view_other, weight_grad = lax.optimization_barrier((view_other, weight_grad))
    image_grad = call(join_kernel, struct((own, views, depth), F32), [SMEM] + [VMEM] * 2)(
        me, total[:own], view_other
    )
    return (image_grad, weight_grad)


def solution(mesh):
    return jax.shard_map(
        shards,
        mesh=mesh,
        in_specs=(P(("rep", "dp"), None, None), P(None, "dp")),
        out_specs=(P(("rep", "dp"), None, None), P(None, "dp")),
        check_vma=False,
    )
```

```python
import functools

import jax
import jax.numpy as jnp
from jax import lax
from jax.experimental import pallas as pl
from jax.experimental.pallas import tpu as pltpu
from jax.sharding import PartitionSpec as P

invariance_weight = 25.0
variance_weight = 25.0
covariance_weight = 1.0
loss_scale = 8192.0
epsilon_var = 0.0001

F32 = jnp.float32
BF16 = jnp.bfloat16
VMEM = pl.BlockSpec(memory_space=pltpu.VMEM)
SMEM = pl.BlockSpec(memory_space=pltpu.SMEM)
CORE, ACROSS, QUAD = 1, 2, 4
EXTRA = 8


def swap(block, axis, bits):
    return lax.ppermute(block, axis, [(i, i ^ bits) for i in range(lax.axis_size(axis))])


def centre(z):
    return z - jnp.mean(z, axis=0, keepdims=True)


def nt_dot(a, b):
    return lax.dot_general(a, b, (((1,), (1,)), ((), ())), preferred_element_type=F32)


def half_masks(half, count):
    row = lax.broadcasted_iota(jnp.int32, (half, count), 0)
    lane = lax.broadcasted_iota(jnp.int32, (half, count), 1)
    return (lane < half) & (row < lane), row == lane, lane < half


def whole(near_ref, far_ref):
    return jnp.concatenate([near_ref[...], far_ref[...]], axis=0)


def pick_kernel(me_ref, images_ref, rows_ref):
    images = images_ref[...]
    rows_ref[...] = jnp.where(me_ref[0] % 2 == 1, images[:, 1, :], images[:, 0, :])


def pair_kernel(me_ref, rows_ref, images_ref, both_ref):
    images = images_ref[...]
    rows = jnp.where(me_ref[0] % 2 == 1, images[:, 1, :], images[:, 0, :])
    both_ref[...] = jnp.concatenate([rows_ref[...], rows], axis=0)


def turn_kernel(wide_ref, turned_ref):
    turned_ref[...] = jnp.swapaxes(wide_ref[...], 0, 1)


def gram_kernel(own, me_ref, near_ref, far_ref, c_ref, packed_ref, sorted_ref):
    me = me_ref[0]
    count, width = c_ref.shape
    devices = count // own
    outer = devices // QUAD
    half = count // 2
    centred = centre(whole(near_ref, far_ref)).reshape(devices, own, width)
    for slot in range(devices):
        rel = (slot // 2 % outer) * QUAD + (slot // 2 // outer) * 2 + slot % 2
        sorted_ref[rel ^ me] = centred[slot]
    c = sorted_ref[...].reshape(count, width).astype(BF16)
    c_ref[...] = c
    gram = nt_dot(c, c)
    upper, diagonal, _ = half_masks(half, count)
    turned = pltpu.roll(gram[half:], half, 1)
    packed_ref[:half] = jnp.where(upper, turned, gram[:half])
    second = jnp.sum(jnp.where(diagonal, turned, 0.0), axis=0, keepdims=True)
    packed_ref[half:] = jnp.broadcast_to(second, (EXTRA, count))


def unpack(packed_ref):
    count = packed_ref.shape[1]
    half = count // 2
    upper, diagonal, left = half_masks(half, count)
    top = packed_ref[:half]
    second = packed_ref[half:half + 1]
    mirror = jnp.swapaxes(jnp.concatenate([top, jnp.zeros_like(top)], axis=0), 0, 1)
    first = jnp.where(upper, mirror[:half], top)
    last = jnp.where(diagonal, second, jnp.where(upper, top, mirror[:half]))
    last = jnp.where(left, mirror[half:], pltpu.roll(last, half, 1))
    return first, last


def base_kernel(scale, features, near_ref, far_ref, base_ref):
    count = base_ref.shape[0]
    coeff = scale * 4.0 * covariance_weight / (features * (count - 1))
    centred = centre(whole(near_ref, far_ref))
    variance = jnp.sum(centred * centred, axis=0, keepdims=True) / (count - 1)
    spread = jnp.sqrt(variance + epsilon_var)
    wide = centred.astype(BF16).astype(F32)
    diag_cov = jnp.sum(wide * wide, axis=0, keepdims=True) / (count - 1)
    var_coeff = jnp.where(
        spread < 1.0, -scale * variance_weight / (features * (count - 1)) / spread, 0.0
    )
    base_ref[...] = var_coeff * centred - coeff * diag_cov * wide


def grads_kernel(own, scale, features, me_ref, packed_ref, c_ref, near_ref, far_ref, other_ref,
                 base_ref, w_ref, grad_ref, send_ref, gram_ref):
    me = me_ref[0]
    count, width = c_ref.shape
    devices = count // own
    half = count // 2
    first, last = unpack(packed_ref)
    gram_ref[:devices // 2] = first.reshape(devices // 2, own, count)
    gram_ref[devices // 2:] = last.reshape(devices // 2, own, count)
    order = [
        high * QUAD + across + core
        for across in (0, ACROSS) for high in range(devices // QUAD) for core in (0, CORE)
    ]
    rest = jnp.concatenate([gram_ref[rel ^ me] for rel in order], axis=0)
    through = 0.0
    for _ in range(2):
        piece = rest.astype(BF16)
        rest = rest - piece.astype(F32)
        through = through + jnp.dot(piece, c_ref[...], preferred_element_type=F32)
    coeff = scale * 4.0 * covariance_weight / (features * (count - 1))
    other = other_ref[...].reshape(devices // 2, 2, own, width)
    other = jnp.concatenate([other[:, 1:], other[:, :1]], axis=1).reshape(count, width)
    gap = whole(near_ref, far_ref) - other
    inv_term = gap * (scale * 2.0 * invariance_weight / (count * features))
    grad = (inv_term + base_ref[...] + through * (coeff / (count - 1))).astype(BF16)
    grad_ref[...] = grad
    send_ref[...] = jnp.dot(grad[count // 2:], w_ref[...], preferred_element_type=F32).astype(BF16)


def join_kernel(me_ref, own_ref, other_ref, out_ref):
    second = me_ref[0] % 2 == 1
    own, other = own_ref[...], other_ref[...]
    out_ref[:, 0, :] = jnp.where(second, other, own)
    out_ref[:, 1, :] = jnp.where(second, own, other)


def weight_operands(rows_ref, rows_core_ref, grad_ref, grad_core_ref):
    block = grad_core_ref.shape[1]
    rows = jnp.concatenate([rows_ref[...], rows_core_ref[...]], axis=0)
    return rows, jnp.concatenate([grad_ref[:, :block], grad_core_ref[...]], axis=0)


def tn_dot(a, b):
    return lax.dot_general(a, b, (((0,), (0,)), ((), ())), preferred_element_type=F32)


def weight_kernel(*refs):
    part = tn_dot(*weight_operands(*refs[:4]))
    refs[-1][...] = part + refs[4][...] if len(refs) > 5 else part


def last_weight_kernel(*refs):
    *operand_refs, earlier_ref, out_ref, sum_ref, sems = refs
    rows, grads = weight_operands(*operand_refs)
    bands, height, _ = sum_ref.shape
    copies = []
    for i in range(bands):
        band = slice(i * height, (i + 1) * height)
        sum_ref[i] = tn_dot(rows[:, band], grads) + earlier_ref[band]
        copies.append(pltpu.make_async_copy(sum_ref.at[i], out_ref.at[pl.ds(i * height, height)], sems.at[i]))
        copies[-1].start()
    for copy in copies:
        copy.wait()


def call(kernel, out_shape, specs, scratch=(), place=VMEM):
    return pl.pallas_call(
        kernel,
        out_shape=out_shape,
        in_specs=specs,
        out_specs=jax.tree.map(lambda _: place, out_shape),
        scratch_shapes=list(scratch),
        compiler_params=pltpu.CompilerParams(vmem_limit_bytes=32 * 1024 * 1024),
    )


def shards(images, weight):
    groups = lax.axis_size("rep")
    owners = lax.axis_size("dp")
    own, views, depth = images.shape
    block = weight.shape[1]
    width = 2 * block
    features = block * owners
    count = own * owners
    half = count // 2
    lot = 2 * own
    outer = owners // QUAD
    scale = loss_scale / groups
    position = lax.axis_index("dp")
    me = position.reshape(1)
    struct = jax.ShapeDtypeStruct

    def over_rep(array):
        return [
            lax.ppermute(array, "rep", [(i, (i + shift) % groups) for i in range(groups)])
            for shift in range(1, groups)
        ]

    def matmul(rows, matrix):
        return jnp.dot(rows, matrix, preferred_element_type=F32)

    given = swap(images, "dp", CORE)
    mine = call(pick_kernel, struct((own, depth), BF16), [SMEM, VMEM])(me, images)
    given, mine, sent = lax.optimization_barrier((given, mine, weight))
    weight_core = swap(sent, "dp", CORE)
    mine = call(pair_kernel, struct((lot, depth), BF16), [SMEM] + [VMEM] * 2)(me, mine, given)
    column = [swap(mine, "dp", high * QUAD) for high in range(1, outer)]
    wide = jnp.concatenate([weight, weight_core], axis=1)
    column, wide = lax.optimization_barrier((column, wide))
    column = lax.optimization_barrier(jnp.concatenate([mine] + column, axis=0))
    across = swap(column, "dp", ACROSS)
    near = matmul(column, wide)
    near, across = lax.optimization_barrier((near, across))
    far = matmul(across, wide)

    c, packed = call(
        functools.partial(gram_kernel, own),
        (struct((count, width), BF16), struct((half + EXTRA, count), F32)),
        [SMEM] + [VMEM] * 2,
        [pltpu.VMEM((owners, own, width), F32)],
    )(me, near, far)

    top = owners // 2
    along, beside, corner = (swap(packed, "dp", bits) for bits in (ACROSS, top, ACROSS | top))
    wide_t = call(turn_kernel, struct((width, depth), BF16), [VMEM])(wide)
    along, beside, corner, wide_t = lax.optimization_barrier((along, beside, corner, wide_t))
    packed = (packed + along) + (beside + corner)
    packed, near_late, far_late, rows = lax.optimization_barrier(
        (packed, near, far, jnp.concatenate([column, across], axis=0))
    )
    rows_core = swap(rows, "dp", CORE)
    base = call(
        functools.partial(base_kernel, scale, features), struct((count, width), F32), [VMEM] * 2
    )(near_late, far_late)
    base, sent = lax.optimization_barrier((base, rows))
    rows_others = over_rep(sent)
    other = matmul(rows_core, wide)
    bit = QUAD
    while bit < top:
        received = swap(packed, "dp", bit)
        received, other, base = lax.optimization_barrier((received, other, base))
        packed = packed + received
        bit *= 2

    grad, send = call(
        functools.partial(grads_kernel, own, scale, features),
        (struct((count, width), BF16), struct((half, depth), BF16)),
        [SMEM] + [VMEM] * 7,
        [pltpu.VMEM((owners, own, count), F32)],
    )(me, packed, c, near, far, other, base, wide_t)

    def weight_part(*operands):
        return call(weight_kernel, struct((depth, block), F32), [VMEM] * len(operands))(*operands)

    received = swap(send, "dp", ACROSS)
    keep = matmul(grad[:half], wide_t)
    keep, grad = lax.optimization_barrier((keep, grad))
    grad_others = over_rep(grad)
    grad_core = swap(grad[:, block:], "dp", CORE)
    keep = (keep + received.astype(F32)).reshape(outer, lot, depth)
    received = [
        swap(keep[high].astype(BF16), "dp", high * QUAD) for high in range(1, outer)
    ]
    grad, grad_others = lax.optimization_barrier((grad, grad_others))
    weight_grad = weight_part(rows, rows_core, grad, grad_core)
    received, weight_grad = lax.optimization_barrier((received, weight_grad))
    total = keep[0]
    for array in received:
        total = total + array.astype(F32)
    view_other = swap(total[own:], "dp", CORE)
    height = min(depth, 256)
    for left, (theirs, theirs_grad) in enumerate(zip(rows_others, grad_others), 2 - groups):
        operands = [
            theirs, swap(theirs, "dp", CORE),
            theirs_grad, swap(theirs_grad[:, block:], "dp", CORE), weight_grad,
        ]
        if left < 0:
            weight_grad = weight_part(*operands)
        else:
            weight_grad = call(
                last_weight_kernel, struct((depth, block), F32), [VMEM] * 5,
                [
                    pltpu.VMEM((depth // height, height, block), F32),
                    pltpu.SemaphoreType.DMA((depth // height,)),
                ],
                pl.BlockSpec(memory_space=pl.ANY),
            )(*operands)
    view_other, weight_grad = lax.optimization_barrier((view_other, weight_grad))
    image_grad = call(join_kernel, struct((own, views, depth), F32), [SMEM] + [VMEM] * 2)(
        me, total[:own], view_other
    )
    return (image_grad, weight_grad)


def solution(mesh):
    return jax.shard_map(
        shards,
        mesh=mesh,
        in_specs=(P(("rep", "dp"), None, None), P(None, "dp")),
        out_specs=(P(("rep", "dp"), None, None), P(None, "dp")),
        check_vma=False,
    )
```

```python
import functools

import jax
import jax.numpy as jnp
from jax import lax
from jax.experimental import pallas as pl
from jax.experimental.pallas import tpu as pltpu
from jax.sharding import PartitionSpec as P

invariance_weight = 25.0
variance_weight = 25.0
covariance_weight = 1.0
loss_scale = 8192.0
epsilon_var = 0.0001

F32 = jnp.float32
BF16 = jnp.bfloat16
VMEM = pl.BlockSpec(memory_space=pltpu.VMEM)
SMEM = pl.BlockSpec(memory_space=pltpu.SMEM)
CORE, ACROSS, QUAD = 1, 2, 4
EXTRA = 8


def swap(block, axis, bits):
    return lax.ppermute(block, axis, [(i, i ^ bits) for i in range(lax.axis_size(axis))])


def centre(z):
    return z - jnp.mean(z, axis=0, keepdims=True)


def nt_dot(a, b):
    return lax.dot_general(a, b, (((1,), (1,)), ((), ())), preferred_element_type=F32)


def half_masks(half, count):
    row = lax.broadcasted_iota(jnp.int32, (half, count), 0)
    lane = lax.broadcasted_iota(jnp.int32, (half, count), 1)
    return (lane < half) & (row < lane), row == lane, lane < half


def whole(near_ref, far_ref):
    return jnp.concatenate([near_ref[...], far_ref[...]], axis=0)


def pick_kernel(me_ref, images_ref, rows_ref):
    images = images_ref[...]
    rows_ref[...] = jnp.where(me_ref[0] % 2 == 1, images[:, 1, :], images[:, 0, :])


def pair_kernel(me_ref, rows_ref, images_ref, both_ref):
    images = images_ref[...]
    rows = jnp.where(me_ref[0] % 2 == 1, images[:, 1, :], images[:, 0, :])
    both_ref[...] = jnp.concatenate([rows_ref[...], rows], axis=0)


def turn_kernel(wide_ref, turned_ref):
    turned_ref[...] = jnp.swapaxes(wide_ref[...], 0, 1)


def gram_kernel(own, me_ref, near_ref, far_ref, c_ref, packed_ref, sorted_ref):
    me = me_ref[0]
    count, width = c_ref.shape
    devices = count // own
    outer = devices // QUAD
    half = count // 2
    centred = centre(whole(near_ref, far_ref)).reshape(devices, own, width)
    for slot in range(devices):
        rel = (slot // 2 % outer) * QUAD + (slot // 2 // outer) * 2 + slot % 2
        sorted_ref[rel ^ me] = centred[slot]
    c = sorted_ref[...].reshape(count, width).astype(BF16)
    c_ref[...] = c
    gram = nt_dot(c, c)
    upper, diagonal, _ = half_masks(half, count)
    turned = pltpu.roll(gram[half:], half, 1)
    packed_ref[:half] = jnp.where(upper, turned, gram[:half])
    second = jnp.sum(jnp.where(diagonal, turned, 0.0), axis=0, keepdims=True)
    packed_ref[half:] = jnp.broadcast_to(second, (EXTRA, count))


def unpack(packed_ref):
    count = packed_ref.shape[1]
    half = count // 2
    upper, diagonal, left = half_masks(half, count)
    top = packed_ref[:half]
    second = packed_ref[half:half + 1]
    mirror = jnp.swapaxes(jnp.concatenate([top, jnp.zeros_like(top)], axis=0), 0, 1)
    first = jnp.where(upper, mirror[:half], top)
    last = jnp.where(diagonal, second, jnp.where(upper, top, mirror[:half]))
    last = jnp.where(left, mirror[half:], pltpu.roll(last, half, 1))
    return first, last


def base_kernel(scale, features, near_ref, far_ref, base_ref):
    count = base_ref.shape[0]
    coeff = scale * 4.0 * covariance_weight / (features * (count - 1))
    centred = centre(whole(near_ref, far_ref))
    variance = jnp.sum(centred * centred, axis=0, keepdims=True) / (count - 1)
    spread = jnp.sqrt(variance + epsilon_var)
    wide = centred.astype(BF16).astype(F32)
    diag_cov = jnp.sum(wide * wide, axis=0, keepdims=True) / (count - 1)
    var_coeff = jnp.where(
        spread < 1.0, -scale * variance_weight / (features * (count - 1)) / spread, 0.0
    )
    base_ref[...] = var_coeff * centred - coeff * diag_cov * wide


def grads_kernel(own, scale, features, me_ref, packed_ref, c_ref, near_ref, far_ref, other_ref,
                 base_ref, w_ref, grad_ref, send_ref, gram_ref):
    me = me_ref[0]
    count, width = c_ref.shape
    devices = count // own
    half = count // 2
    first, last = unpack(packed_ref)
    gram_ref[:devices // 2] = first.reshape(devices // 2, own, count)
    gram_ref[devices // 2:] = last.reshape(devices // 2, own, count)
    order = [
        high * QUAD + across + core
        for across in (0, ACROSS) for high in range(devices // QUAD) for core in (0, CORE)
    ]
    rest = jnp.concatenate([gram_ref[rel ^ me] for rel in order], axis=0)
    through = 0.0
    for _ in range(2):
        piece = rest.astype(BF16)
        rest = rest - piece.astype(F32)
        through = through + jnp.dot(piece, c_ref[...], preferred_element_type=F32)
    coeff = scale * 4.0 * covariance_weight / (features * (count - 1))
    other = other_ref[...].reshape(devices // 2, 2, own, width)
    other = jnp.concatenate([other[:, 1:], other[:, :1]], axis=1).reshape(count, width)
    gap = whole(near_ref, far_ref) - other
    inv_term = gap * (scale * 2.0 * invariance_weight / (count * features))
    grad = (inv_term + base_ref[...] + through * (coeff / (count - 1))).astype(BF16)
    grad_ref[...] = grad
    send_ref[...] = jnp.dot(grad[count // 2:], w_ref[...], preferred_element_type=F32).astype(BF16)


def join_kernel(me_ref, own_ref, other_ref, out_ref):
    second = me_ref[0] % 2 == 1
    own, other = own_ref[...], other_ref[...]
    out_ref[:, 0, :] = jnp.where(second, other, own)
    out_ref[:, 1, :] = jnp.where(second, own, other)


def weight_operands(rows_ref, rows_core_ref, grad_ref, grad_core_ref):
    block = grad_core_ref.shape[1]
    rows = jnp.concatenate([rows_ref[...], rows_core_ref[...]], axis=0)
    return rows, jnp.concatenate([grad_ref[:, :block], grad_core_ref[...]], axis=0)


def tn_dot(a, b):
    return lax.dot_general(a, b, (((0,), (0,)), ((), ())), preferred_element_type=F32)


def weight_kernel(*refs):
    part = tn_dot(*weight_operands(*refs[:4]))
    refs[-1][...] = part + refs[4][...] if len(refs) > 5 else part


def last_weight_kernel(*refs):
    *operand_refs, earlier_ref, out_ref, sum_ref, sems = refs
    rows, grads = weight_operands(*operand_refs)
    bands, height, _ = sum_ref.shape
    copies = []
    for i in range(bands):
        band = slice(i * height, (i + 1) * height)
        sum_ref[i] = tn_dot(rows[:, band], grads) + earlier_ref[band]
        copies.append(pltpu.make_async_copy(sum_ref.at[i], out_ref.at[pl.ds(i * height, height)], sems.at[i]))
        copies[-1].start()
    for copy in copies:
        copy.wait()


def call(kernel, out_shape, specs, scratch=(), place=VMEM):
    return pl.pallas_call(
        kernel,
        out_shape=out_shape,
        in_specs=specs,
        out_specs=jax.tree.map(lambda _: place, out_shape),
        scratch_shapes=list(scratch),
        compiler_params=pltpu.CompilerParams(vmem_limit_bytes=32 * 1024 * 1024),
    )


def shards(images, weight):
    groups = lax.axis_size("rep")
    owners = lax.axis_size("dp")
    own, views, depth = images.shape
    block = weight.shape[1]
    width = 2 * block
    features = block * owners
    count = own * owners
    half = count // 2
    lot = 2 * own
    outer = owners // QUAD
    scale = loss_scale / groups
    position = lax.axis_index("dp")
    me = position.reshape(1)
    struct = jax.ShapeDtypeStruct

    def over_rep(array):
        return [
            lax.ppermute(array, "rep", [(i, (i + shift) % groups) for i in range(groups)])
            for shift in range(1, groups)
        ]

    def matmul(rows, matrix):
        return jnp.dot(rows, matrix, preferred_element_type=F32)

    given = swap(images, "dp", CORE)
    mine = call(pick_kernel, struct((own, depth), BF16), [SMEM, VMEM])(me, images)
    given, mine, sent = lax.optimization_barrier((given, mine, weight))
    weight_core = swap(sent, "dp", CORE)
    mine = call(pair_kernel, struct((lot, depth), BF16), [SMEM] + [VMEM] * 2)(me, mine, given)
    column = [swap(mine, "dp", high * QUAD) for high in range(1, outer)]
    wide = jnp.concatenate([weight, weight_core], axis=1)
    column, wide = lax.optimization_barrier((column[::-1], wide))
    column = column[::-1]
    column = lax.optimization_barrier(jnp.concatenate([mine] + column, axis=0))
    across = swap(column, "dp", ACROSS)
    near = matmul(column, wide)
    wide_t = call(turn_kernel, struct((width, depth), BF16), [VMEM])(wide)
    wide_t, sent = lax.optimization_barrier((wide_t, column))
    near_others = over_rep(sent)
    near, across = lax.optimization_barrier((near, across))
    far = matmul(across, wide)

    c, packed = call(
        functools.partial(gram_kernel, own),
        (struct((count, width), BF16), struct((half + EXTRA, count), F32)),
        [SMEM] + [VMEM] * 2,
        [pltpu.VMEM((owners, own, width), F32)],
    )(me, near, far)

    top = owners // 2
    along, beside, corner = (swap(packed, "dp", bits) for bits in (ACROSS, top, ACROSS | top))
    corner, beside, along, wide_t = lax.optimization_barrier((corner, beside, along, wide_t))
    along, near_others = lax.optimization_barrier((along, near_others))
    packed = (packed + along) + (beside + corner)
    packed, near_late, far_late, rows = lax.optimization_barrier(
        (packed, near, far, jnp.concatenate([column, across], axis=0))
    )
    rows_core = swap(rows, "dp", CORE)
    base = call(
        functools.partial(base_kernel, scale, features), struct((count, width), F32), [VMEM] * 2
    )(near_late, far_late)
    base, sent = lax.optimization_barrier((base, across))
    rows_others = [
        jnp.concatenate(parts, axis=0) for parts in zip(near_others, over_rep(sent))
    ]
    other = matmul(rows_core, wide)
    bit = QUAD
    while bit < top:
        received = swap(packed, "dp", bit)
        received, other, base = lax.optimization_barrier((received, other, base))
        packed = packed + received
        bit *= 2

    grad, send = call(
        functools.partial(grads_kernel, own, scale, features),
        (struct((count, width), BF16), struct((half, depth), BF16)),
        [SMEM] + [VMEM] * 7,
        [pltpu.VMEM((owners, own, count), F32)],
    )(me, packed, c, near, far, other, base, wide_t)

    def weight_part(*operands):
        return call(weight_kernel, struct((depth, block), F32), [VMEM] * len(operands))(*operands)

    received = swap(send, "dp", ACROSS)
    keep = matmul(grad[:half], wide_t)
    grad_core = swap(grad[:, block:], "dp", CORE)
    keep, grad = lax.optimization_barrier((keep, grad))
    grad = grad[:, :block]
    grad_others, grad_core_others = over_rep(grad), over_rep(grad_core)
    keep = (keep + received.astype(F32)).reshape(outer, lot, depth)
    received = [
        swap(keep[high].astype(BF16), "dp", high * QUAD) for high in range(outer - 1, 0, -1)
    ]
    grad, grad_others, grad_core_others = lax.optimization_barrier(
        (grad, grad_others, grad_core_others)
    )
    weight_grad = weight_part(rows, rows_core, grad, grad_core)
    received, weight_grad = lax.optimization_barrier((received, weight_grad))
    total = keep[0]
    for array in received:
        total = total + array.astype(F32)
    view_other = swap(total[own:], "dp", CORE)
    height = min(depth, 256)
    for left, (theirs, theirs_grad) in enumerate(zip(rows_others, grad_others), 2 - groups):
        operands = [
            theirs, swap(theirs, "dp", CORE),
            theirs_grad, grad_core_others.pop(0), weight_grad,
        ]
        if left < 0:
            weight_grad = weight_part(*operands)
        else:
            weight_grad = call(
                last_weight_kernel, struct((depth, block), F32), [VMEM] * 5,
                [
                    pltpu.VMEM((depth // height, height, block), F32),
                    pltpu.SemaphoreType.DMA((depth // height,)),
                ],
                pl.BlockSpec(memory_space=pl.ANY),
            )(*operands)
    view_other, weight_grad = lax.optimization_barrier((view_other, weight_grad))
    image_grad = call(join_kernel, struct((own, views, depth), F32), [SMEM] + [VMEM] * 2)(
        me, total[:own], view_other
    )
    return (image_grad, weight_grad)


def solution(mesh):
    return jax.shard_map(
        shards,
        mesh=mesh,
        in_specs=(P(("rep", "dp"), None, None), P(None, "dp")),
        out_specs=(P(("rep", "dp"), None, None), P(None, "dp")),
        check_vma=False,
    )
```

```python
import functools

import jax
import jax.numpy as jnp
from jax import lax
from jax.experimental import pallas as pl
from jax.experimental.pallas import tpu as pltpu
from jax.sharding import PartitionSpec as P

invariance_weight = 25.0
variance_weight = 25.0
covariance_weight = 1.0
loss_scale = 8192.0
epsilon_var = 0.0001

F32 = jnp.float32
BF16 = jnp.bfloat16
VMEM = pl.BlockSpec(memory_space=pltpu.VMEM)
SMEM = pl.BlockSpec(memory_space=pltpu.SMEM)
CORE, ACROSS, QUAD = 1, 2, 4
EXTRA = 8


def swap(block, axis, bits):
    return lax.ppermute(block, axis, [(i, i ^ bits) for i in range(lax.axis_size(axis))])


def centre(z):
    return z - jnp.mean(z, axis=0, keepdims=True)


def nt_dot(a, b):
    return lax.dot_general(a, b, (((1,), (1,)), ((), ())), preferred_element_type=F32)


def half_masks(half, count):
    row = lax.broadcasted_iota(jnp.int32, (half, count), 0)
    lane = lax.broadcasted_iota(jnp.int32, (half, count), 1)
    return (lane < half) & (row < lane), row == lane, lane < half


def whole(near_ref, far_ref):
    return jnp.concatenate([near_ref[...], far_ref[...]], axis=0)


def pick_kernel(me_ref, images_ref, rows_ref):
    images = images_ref[...]
    rows_ref[...] = jnp.where(me_ref[0] % 2 == 1, images[:, 1, :], images[:, 0, :])


def pair_kernel(me_ref, rows_ref, images_ref, both_ref):
    images = images_ref[...]
    rows = jnp.where(me_ref[0] % 2 == 1, images[:, 1, :], images[:, 0, :])
    both_ref[...] = jnp.concatenate([rows_ref[...], rows], axis=0)


def turn_kernel(wide_ref, turned_ref):
    turned_ref[...] = jnp.swapaxes(wide_ref[...], 0, 1)


def gram_kernel(own, me_ref, near_ref, far_ref, c_ref, packed_ref, sorted_ref):
    me = me_ref[0]
    count, width = c_ref.shape
    devices = count // own
    outer = devices // QUAD
    half = count // 2
    centred = centre(whole(near_ref, far_ref)).reshape(devices, own, width)
    for slot in range(devices):
        rel = (slot // 2 % outer) * QUAD + (slot // 2 // outer) * 2 + slot % 2
        sorted_ref[rel ^ me] = centred[slot]
    c = sorted_ref[...].reshape(count, width).astype(BF16)
    c_ref[...] = c
    gram = nt_dot(c, c)
    upper, diagonal, _ = half_masks(half, count)
    turned = pltpu.roll(gram[half:], half, 1)
    packed_ref[:half] = jnp.where(upper, turned, gram[:half])
    second = jnp.sum(jnp.where(diagonal, turned, 0.0), axis=0, keepdims=True)
    packed_ref[half:] = jnp.broadcast_to(second, (EXTRA, count))


def unpack(packed_ref):
    count = packed_ref.shape[1]
    half = count // 2
    upper, diagonal, left = half_masks(half, count)
    top = packed_ref[:half]
    second = packed_ref[half:half + 1]
    mirror = jnp.swapaxes(jnp.concatenate([top, jnp.zeros_like(top)], axis=0), 0, 1)
    first = jnp.where(upper, mirror[:half], top)
    last = jnp.where(diagonal, second, jnp.where(upper, top, mirror[:half]))
    last = jnp.where(left, mirror[half:], pltpu.roll(last, half, 1))
    return first, last


def base_kernel(scale, features, near_ref, far_ref, base_ref):
    count = base_ref.shape[0]
    coeff = scale * 4.0 * covariance_weight / (features * (count - 1))
    centred = centre(whole(near_ref, far_ref))
    variance = jnp.sum(centred * centred, axis=0, keepdims=True) / (count - 1)
    spread = jnp.sqrt(variance + epsilon_var)
    wide = centred.astype(BF16).astype(F32)
    diag_cov = jnp.sum(wide * wide, axis=0, keepdims=True) / (count - 1)
    var_coeff = jnp.where(
        spread < 1.0, -scale * variance_weight / (features * (count - 1)) / spread, 0.0
    )
    base_ref[...] = var_coeff * centred - coeff * diag_cov * wide


def grads_kernel(own, scale, features, me_ref, packed_ref, c_ref, near_ref, far_ref, other_ref,
                 base_ref, w_ref, grad_ref, send_ref, gram_ref):
    me = me_ref[0]
    count, width = c_ref.shape
    devices = count // own
    half = count // 2
    first, last = unpack(packed_ref)
    gram_ref[:devices // 2] = first.reshape(devices // 2, own, count)
    gram_ref[devices // 2:] = last.reshape(devices // 2, own, count)
    order = [
        high * QUAD + across + core
        for across in (0, ACROSS) for high in range(devices // QUAD) for core in (0, CORE)
    ]
    rest = jnp.concatenate([gram_ref[rel ^ me] for rel in order], axis=0)
    through = 0.0
    for _ in range(2):
        piece = rest.astype(BF16)
        rest = rest - piece.astype(F32)
        through = through + jnp.dot(piece, c_ref[...], preferred_element_type=F32)
    coeff = scale * 4.0 * covariance_weight / (features * (count - 1))
    other = other_ref[...].reshape(devices // 2, 2, own, width)
    other = jnp.concatenate([other[:, 1:], other[:, :1]], axis=1).reshape(count, width)
    gap = whole(near_ref, far_ref) - other
    inv_term = gap * (scale * 2.0 * invariance_weight / (count * features))
    grad = (inv_term + base_ref[...] + through * (coeff / (count - 1))).astype(BF16)
    grad_ref[...] = grad
    send_ref[...] = jnp.dot(grad[count // 2:], w_ref[...], preferred_element_type=F32).astype(BF16)


def join_kernel(me_ref, own_ref, other_ref, out_ref):
    second = me_ref[0] % 2 == 1
    own, other = own_ref[...], other_ref[...]
    out_ref[:, 0, :] = jnp.where(second, other, own)
    out_ref[:, 1, :] = jnp.where(second, own, other)


def weight_operands(rows_ref, rows_core_ref, grad_ref, grad_core_ref):
    block = grad_core_ref.shape[1]
    rows = jnp.concatenate([rows_ref[...], rows_core_ref[...]], axis=0)
    return rows, jnp.concatenate([grad_ref[:, :block], grad_core_ref[...]], axis=0)


def tn_dot(a, b):
    return lax.dot_general(a, b, (((0,), (0,)), ((), ())), preferred_element_type=F32)


def weight_kernel(*refs):
    part = tn_dot(*weight_operands(*refs[:4]))
    refs[-1][...] = part + refs[4][...] if len(refs) > 5 else part


def last_weight_kernel(*refs):
    *operand_refs, earlier_ref, out_ref, sum_ref, sems = refs
    rows, grads = weight_operands(*operand_refs)
    bands, height, _ = sum_ref.shape
    copies = []
    for i in range(bands):
        band = slice(i * height, (i + 1) * height)
        sum_ref[i] = tn_dot(rows[:, band], grads) + earlier_ref[band]
        copies.append(pltpu.make_async_copy(sum_ref.at[i], out_ref.at[pl.ds(i * height, height)], sems.at[i]))
        copies[-1].start()
    for copy in copies:
        copy.wait()


def call(kernel, out_shape, specs, scratch=(), place=VMEM):
    return pl.pallas_call(
        kernel,
        out_shape=out_shape,
        in_specs=specs,
        out_specs=jax.tree.map(lambda _: place, out_shape),
        scratch_shapes=list(scratch),
        compiler_params=pltpu.CompilerParams(vmem_limit_bytes=32 * 1024 * 1024),
    )


def shards(images, weight):
    groups = lax.axis_size("rep")
    owners = lax.axis_size("dp")
    own, views, depth = images.shape
    block = weight.shape[1]
    width = 2 * block
    features = block * owners
    count = own * owners
    half = count // 2
    lot = 2 * own
    outer = owners // QUAD
    scale = loss_scale / groups
    position = lax.axis_index("dp")
    me = position.reshape(1)
    struct = jax.ShapeDtypeStruct

    def over_rep(array):
        return [
            lax.ppermute(array, "rep", [(i, (i + shift) % groups) for i in range(groups)])
            for shift in range(1, groups)
        ]

    def matmul(rows, matrix):
        return jnp.dot(rows, matrix, preferred_element_type=F32)

    given = swap(images, "dp", CORE)
    mine = call(pick_kernel, struct((own, depth), BF16), [SMEM, VMEM])(me, images)
    given, mine, sent = lax.optimization_barrier((given, mine, weight))
    weight_core = swap(sent, "dp", CORE)
    mine = call(pair_kernel, struct((lot, depth), BF16), [SMEM] + [VMEM] * 2)(me, mine, given)
    column = [swap(mine, "dp", high * QUAD) for high in range(1, outer)]
    wide = jnp.concatenate([weight, weight_core], axis=1)
    column, wide = lax.optimization_barrier((column[::-1], wide))
    column = column[::-1]
    column = lax.optimization_barrier(jnp.concatenate([mine] + column, axis=0))
    across = swap(column, "dp", ACROSS)
    near = matmul(column, wide)
    wide_t = call(turn_kernel, struct((width, depth), BF16), [VMEM])(wide)
    wide_t, sent = lax.optimization_barrier((wide_t, column))
    near_others = over_rep(sent)
    near, across = lax.optimization_barrier((near, across))
    far = matmul(across, wide)

    c, packed = call(
        functools.partial(gram_kernel, own),
        (struct((count, width), BF16), struct((half + EXTRA, count), F32)),
        [SMEM] + [VMEM] * 2,
        [pltpu.VMEM((owners, own, width), F32)],
    )(me, near, far)

    top = owners // 2
    along, beside, corner = (swap(packed, "dp", bits) for bits in (ACROSS, top, ACROSS | top))
    corner, beside, along, wide_t = lax.optimization_barrier((corner, beside, along, wide_t))
    along, near_others = lax.optimization_barrier((along, near_others))
    packed = (packed + along) + (beside + corner)
    packed, near_late, far_late, rows = lax.optimization_barrier(
        (packed, near, far, jnp.concatenate([column, across], axis=0))
    )
    rows_core = swap(rows, "dp", CORE)
    base = call(
        functools.partial(base_kernel, scale, features), struct((count, width), F32), [VMEM] * 2
    )(near_late, far_late)
    base, sent = lax.optimization_barrier((base, across))
    far_others = over_rep(sent)
    other = matmul(rows_core, wide)
    bit = QUAD
    while bit < top:
        received = swap(packed, "dp", bit)
        received, other, base = lax.optimization_barrier((received, other, base))
        packed = packed + received
        bit *= 2

    grad, send = call(
        functools.partial(grads_kernel, own, scale, features),
        (struct((count, width), BF16), struct((half, depth), BF16)),
        [SMEM] + [VMEM] * 7,
        [pltpu.VMEM((owners, own, count), F32)],
    )(me, packed, c, near, far, other, base, wide_t)

    def weight_part(*operands):
        return call(weight_kernel, struct((depth, block), F32), [VMEM] * len(operands))(*operands)

    received = swap(send, "dp", ACROSS)
    keep = matmul(grad[:half], wide_t)
    grad_core = swap(grad[:, block:], "dp", CORE)
    keep, grad = lax.optimization_barrier((keep, grad))
    grad = grad[:, :block]
    grad_others, grad_core_others = over_rep(grad), over_rep(grad_core)
    keep = keep + received.astype(F32)
    keep, far_others = lax.optimization_barrier((keep, far_others))
    rows_others = [jnp.concatenate(pair, axis=0) for pair in zip(near_others, far_others)]
    keep = keep.reshape(outer, lot, depth)
    received = [
        swap(keep[high].astype(BF16), "dp", high * QUAD) for high in range(outer - 1, 0, -1)
    ]
    grad, grad_others, grad_core_others = lax.optimization_barrier(
        (grad, grad_others, grad_core_others)
    )
    weight_grad = weight_part(rows, rows_core, grad, grad_core)
    height = min(depth, 256)
    for left, (theirs, theirs_grad) in enumerate(zip(rows_others, grad_others), 2 - groups):
        operands = [
            theirs, swap(theirs, "dp", CORE),
            theirs_grad, grad_core_others.pop(0), weight_grad,
        ]
        if left < 0:
            weight_grad = weight_part(*operands)
        else:
            weight_grad = call(
                last_weight_kernel, struct((depth, block), F32), [VMEM] * 5,
                [
                    pltpu.VMEM((depth // height, height, block), F32),
                    pltpu.SemaphoreType.DMA((depth // height,)),
                ],
                pl.BlockSpec(memory_space=pl.ANY),
            )(*operands)
    received, weight_grad = lax.optimization_barrier((received, weight_grad))
    total = keep[0]
    for array in received:
        total = total + array.astype(F32)
    view_other = swap(total[own:], "dp", CORE)
    image_grad = call(join_kernel, struct((own, views, depth), F32), [SMEM] + [VMEM] * 2)(
        me, total[:own], view_other
    )
    return (image_grad, weight_grad)


def solution(mesh):
    return jax.shard_map(
        shards,
        mesh=mesh,
        in_specs=(P(("rep", "dp"), None, None), P(None, "dp")),
        out_specs=(P(("rep", "dp"), None, None), P(None, "dp")),
        check_vma=False,
    )
```

```python
import functools

import jax
import jax.numpy as jnp
from jax import lax
from jax.experimental import pallas as pl
from jax.experimental.pallas import tpu as pltpu
from jax.sharding import PartitionSpec as P

invariance_weight = 25.0
variance_weight = 25.0
covariance_weight = 1.0
loss_scale = 8192.0
epsilon_var = 0.0001

F32 = jnp.float32
BF16 = jnp.bfloat16
VMEM = pl.BlockSpec(memory_space=pltpu.VMEM)
SMEM = pl.BlockSpec(memory_space=pltpu.SMEM)
CORE, ACROSS, QUAD = 1, 2, 4
EXTRA = 8


def swap(block, axis, bits):
    return lax.ppermute(block, axis, [(i, i ^ bits) for i in range(lax.axis_size(axis))])


def centre(z):
    return z - jnp.mean(z, axis=0, keepdims=True)


def nt_dot(a, b):
    return lax.dot_general(a, b, (((1,), (1,)), ((), ())), preferred_element_type=F32)


def half_masks(half, count):
    row = lax.broadcasted_iota(jnp.int32, (half, count), 0)
    lane = lax.broadcasted_iota(jnp.int32, (half, count), 1)
    return (lane < half) & (row < lane), row == lane, lane < half


def whole(near_ref, far_ref):
    return jnp.concatenate([near_ref[...], far_ref[...]], axis=0)


def pick(me_ref, images_ref):
    images = images_ref[...].astype(F32)
    return jnp.where(me_ref[0] % 2 == 1, images[:, 1, :], images[:, 0, :])


def pick_kernel(me_ref, images_ref, rows_ref):
    rows_ref[...] = pick(me_ref, images_ref)


def pair_kernel(me_ref, rows_ref, images_ref, both_ref):
    rows = pick(me_ref, images_ref)
    both_ref[...] = jnp.concatenate([rows_ref[...], rows], axis=0).astype(BF16)


def turn_kernel(wide_ref, turned_ref):
    turned_ref[...] = jnp.swapaxes(wide_ref[...], 0, 1)


def gram_kernel(own, me_ref, near_ref, far_ref, c_ref, packed_ref, sorted_ref):
    me = me_ref[0]
    count, width = c_ref.shape
    devices = count // own
    outer = devices // QUAD
    half = count // 2
    centred = centre(whole(near_ref, far_ref)).reshape(devices, own, width)
    for slot in range(devices):
        rel = (slot // 2 % outer) * QUAD + (slot // 2 // outer) * 2 + slot % 2
        sorted_ref[rel ^ me] = centred[slot]
    c = sorted_ref[...].reshape(count, width).astype(BF16)
    c_ref[...] = c
    gram = nt_dot(c, c)
    upper, diagonal, _ = half_masks(half, count)
    turned = pltpu.roll(gram[half:], half, 1)
    packed_ref[:half] = jnp.where(upper, turned, gram[:half])
    second = jnp.sum(jnp.where(diagonal, turned, 0.0), axis=0, keepdims=True)
    packed_ref[half:] = jnp.broadcast_to(second, (EXTRA, count))


def unpack(packed_ref):
    count = packed_ref.shape[1]
    half = count // 2
    upper, diagonal, left = half_masks(half, count)
    top = packed_ref[:half]
    second = packed_ref[half:half + 1]
    mirror = jnp.swapaxes(jnp.concatenate([top, jnp.zeros_like(top)], axis=0), 0, 1)
    first = jnp.where(upper, mirror[:half], top)
    last = jnp.where(diagonal, second, jnp.where(upper, top, mirror[:half]))
    last = jnp.where(left, mirror[half:], pltpu.roll(last, half, 1))
    return first, last


def base_kernel(scale, features, near_ref, far_ref, base_ref):
    count = base_ref.shape[0]
    coeff = scale * 4.0 * covariance_weight / (features * (count - 1))
    centred = centre(whole(near_ref, far_ref))
    variance = jnp.sum(centred * centred, axis=0, keepdims=True) / (count - 1)
    spread = jnp.sqrt(variance + epsilon_var)
    wide = centred.astype(BF16).astype(F32)
    diag_cov = jnp.sum(wide * wide, axis=0, keepdims=True) / (count - 1)
    var_coeff = jnp.where(
        spread < 1.0, -scale * variance_weight / (features * (count - 1)) / spread, 0.0
    )
    base_ref[...] = var_coeff * centred - coeff * diag_cov * wide


def grads_kernel(own, scale, features, me_ref, packed_ref, c_ref, near_ref, far_ref, other_ref,
                 base_ref, w_ref, grad_ref, send_ref, gram_ref):
    me = me_ref[0]
    count, width = c_ref.shape
    devices = count // own
    half = count // 2
    first, last = unpack(packed_ref)
    gram_ref[:devices // 2] = first.reshape(devices // 2, own, count)
    gram_ref[devices // 2:] = last.reshape(devices // 2, own, count)
    order = [
        high * QUAD + across + core
        for across in (0, ACROSS) for high in range(devices // QUAD) for core in (0, CORE)
    ]
    rest = jnp.concatenate([gram_ref[rel ^ me] for rel in order], axis=0)
    through = 0.0
    for _ in range(2):
        piece = rest.astype(BF16)
        rest = rest - piece.astype(F32)
        through = through + jnp.dot(piece, c_ref[...], preferred_element_type=F32)
    coeff = scale * 4.0 * covariance_weight / (features * (count - 1))
    other = other_ref[...].reshape(devices // 2, 2, own, width)
    other = jnp.concatenate([other[:, 1:], other[:, :1]], axis=1).reshape(count, width)
    gap = whole(near_ref, far_ref) - other
    inv_term = gap * (scale * 2.0 * invariance_weight / (count * features))
    grad = (inv_term + base_ref[...] + through * (coeff / (count - 1))).astype(BF16)
    grad_ref[...] = grad
    send_ref[...] = jnp.dot(grad[count // 2:], w_ref[...], preferred_element_type=F32).astype(BF16)


def join_kernel(me_ref, own_ref, other_ref, out_ref):
    second = me_ref[0] % 2 == 1
    own, other = own_ref[...], other_ref[...]
    out_ref[:, 0, :] = jnp.where(second, other, own)
    out_ref[:, 1, :] = jnp.where(second, own, other)


def weight_operands(rows_ref, rows_core_ref, grad_ref, grad_core_ref):
    block = grad_core_ref.shape[1]
    rows = jnp.concatenate([rows_ref[...], rows_core_ref[...]], axis=0)
    return rows, jnp.concatenate([grad_ref[:, :block], grad_core_ref[...]], axis=0)


def tn_dot(a, b):
    return lax.dot_general(a, b, (((0,), (0,)), ((), ())), preferred_element_type=F32)


def weight_kernel(*refs):
    part = tn_dot(*weight_operands(*refs[:4]))
    refs[-1][...] = part + refs[4][...] if len(refs) > 5 else part


def last_weight_kernel(*refs):
    *operand_refs, earlier_ref, out_ref, sum_ref, sems = refs
    rows, grads = weight_operands(*operand_refs)
    bands, height, _ = sum_ref.shape
    copies = []
    for i in range(bands):
        band = slice(i * height, (i + 1) * height)
        sum_ref[i] = tn_dot(rows[:, band], grads) + earlier_ref[band]
        copies.append(pltpu.make_async_copy(sum_ref.at[i], out_ref.at[pl.ds(i * height, height)], sems.at[i]))
        copies[-1].start()
    for copy in copies:
        copy.wait()


def call(kernel, out_shape, specs, scratch=(), place=VMEM):
    return pl.pallas_call(
        kernel,
        out_shape=out_shape,
        in_specs=specs,
        out_specs=jax.tree.map(lambda _: place, out_shape),
        scratch_shapes=list(scratch),
        compiler_params=pltpu.CompilerParams(vmem_limit_bytes=32 * 1024 * 1024),
    )


def shards(images, weight):
    groups = lax.axis_size("rep")
    owners = lax.axis_size("dp")
    own, views, depth = images.shape
    block = weight.shape[1]
    width = 2 * block
    features = block * owners
    count = own * owners
    half = count // 2
    lot = 2 * own
    outer = owners // QUAD
    scale = loss_scale / groups
    position = lax.axis_index("dp")
    me = position.reshape(1)
    struct = jax.ShapeDtypeStruct

    def over_rep(array):
        return [
            lax.ppermute(array, "rep", [(i, (i + shift) % groups) for i in range(groups)])
            for shift in range(1, groups)
        ]

    def matmul(rows, matrix):
        return jnp.dot(rows, matrix, preferred_element_type=F32)

    given = swap(images, "dp", CORE)
    mine = call(pick_kernel, struct((own, depth), F32), [SMEM, VMEM])(me, images)
    given, mine, sent = lax.optimization_barrier((given, mine, weight))
    weight_core = swap(sent, "dp", CORE)
    mine = call(pair_kernel, struct((lot, depth), BF16), [SMEM] + [VMEM] * 2)(me, mine, given)
    column = [swap(mine, "dp", high * QUAD) for high in range(1, outer)]
    wide = jnp.concatenate([weight, weight_core], axis=1)
    column, wide = lax.optimization_barrier((column[::-1], wide))
    column = column[::-1]
    column = lax.optimization_barrier(jnp.concatenate([mine] + column, axis=0))
    across = swap(column, "dp", ACROSS)
    near = matmul(column, wide)
    wide_t = call(turn_kernel, struct((width, depth), BF16), [VMEM])(wide)
    wide_t, sent = lax.optimization_barrier((wide_t, column))
    near_others = over_rep(sent)
    near, across = lax.optimization_barrier((near, across))
    far = matmul(across, wide)

    c, packed = call(
        functools.partial(gram_kernel, own),
        (struct((count, width), BF16), struct((half + EXTRA, count), F32)),
        [SMEM] + [VMEM] * 2,
        [pltpu.VMEM((owners, own, width), F32)],
    )(me, near, far)

    top = owners // 2
    along, beside, corner = (swap(packed, "dp", bits) for bits in (ACROSS, top, ACROSS | top))
    corner, beside, along, wide_t = lax.optimization_barrier((corner, beside, along, wide_t))
    along, near_others = lax.optimization_barrier((along, near_others))
    packed = (packed + along) + (beside + corner)
    packed, near_late, far_late, rows = lax.optimization_barrier(
        (packed, near, far, jnp.concatenate([column, across], axis=0))
    )
    rows_core = swap(rows, "dp", CORE)
    base = call(
        functools.partial(base_kernel, scale, features), struct((count, width), F32), [VMEM] * 2
    )(near_late, far_late)
    base, sent = lax.optimization_barrier((base, across))
    far_others = over_rep(sent)
    other = matmul(rows_core, wide)
    bit = QUAD
    while bit < top:
        received = swap(packed, "dp", bit)
        received, other, base = lax.optimization_barrier((received, other, base))
        packed = packed + received
        bit *= 2

    grad, send = call(
        functools.partial(grads_kernel, own, scale, features),
        (struct((count, width), BF16), struct((half, depth), BF16)),
        [SMEM] + [VMEM] * 7,
        [pltpu.VMEM((owners, own, count), F32)],
    )(me, packed, c, near, far, other, base, wide_t)

    def weight_part(*operands):
        return call(weight_kernel, struct((depth, block), F32), [VMEM] * len(operands))(*operands)

    received = swap(send, "dp", ACROSS)
    keep = matmul(grad[:half], wide_t)
    grad_core = swap(grad[:, block:], "dp", CORE)
    keep, grad = lax.optimization_barrier((keep, grad))
    grad = grad[:, :block]
    grad_others, grad_core_others = over_rep(grad), over_rep(grad_core)
    keep = keep + received.astype(F32)
    keep, far_others = lax.optimization_barrier((keep, far_others))
    rows_others = [jnp.concatenate(pair, axis=0) for pair in zip(near_others, far_others)]
    keep = keep.reshape(outer, lot, depth)
    received = [
        swap(keep[high].astype(BF16), "dp", high * QUAD) for high in range(outer - 1, 0, -1)
    ]
    grad, grad_others, grad_core_others = lax.optimization_barrier(
        (grad, grad_others, grad_core_others)
    )
    weight_grad = weight_part(rows, rows_core, grad, grad_core)
    height = min(depth, 256)
    for left, (theirs, theirs_grad) in enumerate(zip(rows_others, grad_others), 2 - groups):
        operands = [
            theirs, swap(theirs, "dp", CORE),
            theirs_grad, grad_core_others.pop(0), weight_grad,
        ]
        if left < 0:
            weight_grad = weight_part(*operands)
        else:
            weight_grad = call(
                last_weight_kernel, struct((depth, block), F32), [VMEM] * 5,
                [
                    pltpu.VMEM((depth // height, height, block), F32),
                    pltpu.SemaphoreType.DMA((depth // height,)),
                ],
                pl.BlockSpec(memory_space=pl.ANY),
            )(*operands)
    received, weight_grad = lax.optimization_barrier((received, weight_grad))
    total = keep[0]
    for array in received:
        total = total + array.astype(F32)
    view_other = swap(total[own:], "dp", CORE)
    image_grad = call(join_kernel, struct((own, views, depth), F32), [SMEM] + [VMEM] * 2)(
        me, total[:own], view_other
    )
    return (image_grad, weight_grad)


def solution(mesh):
    return jax.shard_map(
        shards,
        mesh=mesh,
        in_specs=(P(("rep", "dp"), None, None), P(None, "dp")),
        out_specs=(P(("rep", "dp"), None, None), P(None, "dp")),
        check_vma=False,
    )
```

```python
import functools

import jax
import jax.numpy as jnp
from jax import lax
from jax.experimental import pallas as pl
from jax.experimental.pallas import tpu as pltpu
from jax.sharding import PartitionSpec as P

invariance_weight = 25.0
variance_weight = 25.0
covariance_weight = 1.0
loss_scale = 8192.0
epsilon_var = 0.0001

F32 = jnp.float32
BF16 = jnp.bfloat16
VMEM = pl.BlockSpec(memory_space=pltpu.VMEM)
SMEM = pl.BlockSpec(memory_space=pltpu.SMEM)
CORE, ACROSS, QUAD = 1, 2, 4
EXTRA = 8


def swap(block, axis, bits):
    return lax.ppermute(block, axis, [(i, i ^ bits) for i in range(lax.axis_size(axis))])


def centre(z):
    return z - jnp.mean(z, axis=0, keepdims=True)


def nt_dot(a, b):
    return lax.dot_general(a, b, (((1,), (1,)), ((), ())), preferred_element_type=F32)


def half_masks(half, count):
    row = lax.broadcasted_iota(jnp.int32, (half, count), 0)
    lane = lax.broadcasted_iota(jnp.int32, (half, count), 1)
    return (lane < half) & (row < lane), row == lane, lane < half


def whole(near_ref, far_ref):
    return jnp.concatenate([near_ref[...], far_ref[...]], axis=0)


def pick(me_ref, images_ref):
    images = images_ref[...].astype(F32)
    return jnp.where(me_ref[0] % 2 == 1, images[:, 1, :], images[:, 0, :])


def pick_kernel(me_ref, images_ref, rows_ref):
    rows_ref[...] = pick(me_ref, images_ref)


def pair_kernel(me_ref, rows_ref, images_ref, both_ref):
    rows = pick(me_ref, images_ref)
    both_ref[...] = jnp.concatenate([rows_ref[...], rows], axis=0).astype(BF16)


def turn_kernel(wide_ref, turned_ref):
    turned_ref[...] = jnp.swapaxes(wide_ref[...], 0, 1)


def gram_kernel(own, me_ref, near_ref, far_ref, c_ref, packed_ref, sorted_ref):
    me = me_ref[0]
    count, width = c_ref.shape
    devices = count // own
    outer = devices // QUAD
    half = count // 2
    centred = centre(whole(near_ref, far_ref)).reshape(devices, own, width)
    for slot in range(devices):
        rel = (slot // 2 % outer) * QUAD + (slot // 2 // outer) * 2 + slot % 2
        sorted_ref[rel ^ me] = centred[slot]
    c = sorted_ref[...].reshape(count, width).astype(BF16)
    c_ref[...] = c
    gram = nt_dot(c, c)
    upper, diagonal, _ = half_masks(half, count)
    turned = pltpu.roll(gram[half:], half, 1)
    packed_ref[:half] = jnp.where(upper, turned, gram[:half])
    second = jnp.sum(jnp.where(diagonal, turned, 0.0), axis=0, keepdims=True)
    packed_ref[half:] = jnp.broadcast_to(second, (EXTRA, count))


def unpack(packed_ref):
    count = packed_ref.shape[1]
    half = count // 2
    upper, diagonal, left = half_masks(half, count)
    top = packed_ref[:half]
    second = packed_ref[half:half + 1]
    mirror = jnp.swapaxes(jnp.concatenate([top, jnp.zeros_like(top)], axis=0), 0, 1)
    first = jnp.where(upper, mirror[:half], top)
    last = jnp.where(diagonal, second, jnp.where(upper, top, mirror[:half]))
    last = jnp.where(left, mirror[half:], pltpu.roll(last, half, 1))
    return first, last


def base_kernel(scale, features, near_ref, far_ref, base_ref):
    count = base_ref.shape[0]
    coeff = scale * 4.0 * covariance_weight / (features * (count - 1))
    centred = centre(whole(near_ref, far_ref))
    variance = jnp.sum(centred * centred, axis=0, keepdims=True) / (count - 1)
    spread = jnp.sqrt(variance + epsilon_var)
    wide = centred.astype(BF16).astype(F32)
    diag_cov = jnp.sum(wide * wide, axis=0, keepdims=True) / (count - 1)
    var_coeff = jnp.where(
        spread < 1.0, -scale * variance_weight / (features * (count - 1)) / spread, 0.0
    )
    base_ref[...] = var_coeff * centred - coeff * diag_cov * wide


def grads_kernel(side, scale, features, me_ref, packed_ref, c_ref, z_ref, other_ref, base_ref,
                 w_ref, grad_ref, part_ref, gram_ref):
    me = me_ref[0]
    count = c_ref.shape[0]
    devices, own, _ = gram_ref.shape
    half, width = z_ref.shape
    first, last = unpack(packed_ref)
    gram_ref[:devices // 2] = first.reshape(devices // 2, own, count)
    gram_ref[devices // 2:] = last.reshape(devices // 2, own, count)
    order = [
        high * QUAD + side * ACROSS + core
        for high in range(devices // QUAD) for core in (0, CORE)
    ]
    rest = jnp.concatenate([gram_ref[rel ^ me] for rel in order], axis=0)
    through = 0.0
    for _ in range(2):
        piece = rest.astype(BF16)
        rest = rest - piece.astype(F32)
        through = through + jnp.dot(piece, c_ref[...], preferred_element_type=F32)
    coeff = scale * 4.0 * covariance_weight / (features * (count - 1))
    rows = slice(side * half, (side + 1) * half)
    other = other_ref[rows].reshape(half // (2 * own), 2, own, width)
    other = jnp.concatenate([other[:, 1:], other[:, :1]], axis=1).reshape(half, width)
    inv_term = (z_ref[...] - other) * (scale * 2.0 * invariance_weight / (count * features))
    grad = (inv_term + base_ref[rows] + through * (coeff / (count - 1))).astype(BF16)
    grad_ref[...] = grad
    part = jnp.dot(grad, w_ref[...], preferred_element_type=F32)
    part_ref[...] = part.astype(part_ref.dtype)


def join_kernel(me_ref, own_ref, other_ref, out_ref):
    second = me_ref[0] % 2 == 1
    own, other = own_ref[...], other_ref[...]
    out_ref[:, 0, :] = jnp.where(second, other, own)
    out_ref[:, 1, :] = jnp.where(second, own, other)


def weight_operands(rows_ref, rows_core_ref, grad_ref, grad_core_ref):
    block = grad_core_ref.shape[1]
    rows = jnp.concatenate([rows_ref[...], rows_core_ref[...]], axis=0)
    return rows, jnp.concatenate([grad_ref[:, :block], grad_core_ref[...]], axis=0)


def tn_dot(a, b):
    return lax.dot_general(a, b, (((0,), (0,)), ((), ())), preferred_element_type=F32)


def weight_kernel(*refs):
    part = tn_dot(*weight_operands(*refs[:4]))
    refs[-1][...] = part + refs[4][...] if len(refs) > 5 else part


def last_weight_kernel(*refs):
    *operand_refs, earlier_ref, out_ref, sum_ref, sems = refs
    rows, grads = weight_operands(*operand_refs)
    bands, height, _ = sum_ref.shape
    copies = []
    for i in range(bands):
        band = slice(i * height, (i + 1) * height)
        sum_ref[i] = tn_dot(rows[:, band], grads) + earlier_ref[band]
        copies.append(pltpu.make_async_copy(sum_ref.at[i], out_ref.at[pl.ds(i * height, height)], sems.at[i]))
        copies[-1].start()
    for copy in copies:
        copy.wait()


def call(kernel, out_shape, specs, scratch=(), place=VMEM):
    return pl.pallas_call(
        kernel,
        out_shape=out_shape,
        in_specs=specs,
        out_specs=jax.tree.map(lambda _: place, out_shape),
        scratch_shapes=list(scratch),
        compiler_params=pltpu.CompilerParams(vmem_limit_bytes=32 * 1024 * 1024),
    )


def shards(images, weight):
    groups = lax.axis_size("rep")
    owners = lax.axis_size("dp")
    own, views, depth = images.shape
    block = weight.shape[1]
    width = 2 * block
    features = block * owners
    count = own * owners
    half = count // 2
    lot = 2 * own
    outer = owners // QUAD
    scale = loss_scale / groups
    position = lax.axis_index("dp")
    me = position.reshape(1)
    struct = jax.ShapeDtypeStruct

    def over_rep(array):
        return [
            lax.ppermute(array, "rep", [(i, (i + shift) % groups) for i in range(groups)])
            for shift in range(1, groups)
        ]

    def matmul(rows, matrix):
        return jnp.dot(rows, matrix, preferred_element_type=F32)

    given = swap(images, "dp", CORE)
    mine = call(pick_kernel, struct((own, depth), F32), [SMEM, VMEM])(me, images)
    given, mine, sent = lax.optimization_barrier((given, mine, weight))
    weight_core = swap(sent, "dp", CORE)
    mine = call(pair_kernel, struct((lot, depth), BF16), [SMEM] + [VMEM] * 2)(me, mine, given)
    column = [swap(mine, "dp", high * QUAD) for high in range(1, outer)]
    wide = jnp.concatenate([weight, weight_core], axis=1)
    column, wide = lax.optimization_barrier((column[::-1], wide))
    column = column[::-1]
    column = lax.optimization_barrier(jnp.concatenate([mine] + column, axis=0))
    across = swap(column, "dp", ACROSS)
    near = matmul(column, wide)
    wide_t = call(turn_kernel, struct((width, depth), BF16), [VMEM])(wide)
    wide_t, sent = lax.optimization_barrier((wide_t, column))
    near_others = over_rep(sent)
    near, across = lax.optimization_barrier((near, across))
    far = matmul(across, wide)

    c, packed = call(
        functools.partial(gram_kernel, own),
        (struct((count, width), BF16), struct((half + EXTRA, count), F32)),
        [SMEM] + [VMEM] * 2,
        [pltpu.VMEM((owners, own, width), F32)],
    )(me, near, far)

    top = owners // 2
    along, beside, corner = (swap(packed, "dp", bits) for bits in (ACROSS, top, ACROSS | top))
    corner, beside, along, wide_t = lax.optimization_barrier((corner, beside, along, wide_t))
    along, near_others = lax.optimization_barrier((along, near_others))
    packed = (packed + along) + (beside + corner)
    packed, near_late, far_late, rows = lax.optimization_barrier(
        (packed, near, far, jnp.concatenate([column, across], axis=0))
    )
    rows_core = swap(rows, "dp", CORE)
    base = call(
        functools.partial(base_kernel, scale, features), struct((count, width), F32), [VMEM] * 2
    )(near_late, far_late)
    base, sent = lax.optimization_barrier((base, across))
    far_others = over_rep(sent)
    other = matmul(rows_core, wide)
    bit = QUAD
    while bit < top:
        received = swap(packed, "dp", bit)
        received, other, base = lax.optimization_barrier((received, other, base))
        packed = packed + received
        bit *= 2

    def grads(side, z, kind):
        return call(
            functools.partial(grads_kernel, side, scale, features),
            (struct((half, width), BF16), struct((half, depth), kind)),
            [SMEM] + [VMEM] * 6,
            [pltpu.VMEM((owners, own, count), F32)],
        )(me, packed, c, z, other, base, wide_t)

    grad_far, send = grads(1, far, BF16)

    def weight_part(*operands):
        return call(weight_kernel, struct((depth, block), F32), [VMEM] * len(operands))(*operands)

    received = swap(send, "dp", ACROSS)
    _, late = lax.optimization_barrier((send, near))
    grad_near, keep = grads(0, late, F32)
    grad = jnp.concatenate([grad_near, grad_far], axis=0)
    grad_core = swap(grad[:, block:], "dp", CORE)
    keep, grad = lax.optimization_barrier((keep, grad))
    grad = grad[:, :block]
    grad_others, grad_core_others = over_rep(grad), over_rep(grad_core)
    keep = keep + received.astype(F32)
    keep, far_others = lax.optimization_barrier((keep, far_others))
    rows_others = [jnp.concatenate(pair, axis=0) for pair in zip(near_others, far_others)]
    keep = keep.reshape(outer, lot, depth)
    received = [
        swap(keep[high].astype(BF16), "dp", high * QUAD) for high in range(outer - 1, 0, -1)
    ]
    grad, grad_others, grad_core_others = lax.optimization_barrier(
        (grad, grad_others, grad_core_others)
    )
    weight_grad = weight_part(rows, rows_core, grad, grad_core)
    height = min(depth, 256)
    for left, (theirs, theirs_grad) in enumerate(zip(rows_others, grad_others), 2 - groups):
        operands = [
            theirs, swap(theirs, "dp", CORE),
            theirs_grad, grad_core_others.pop(0), weight_grad,
        ]
        if left < 0:
            weight_grad = weight_part(*operands)
        else:
            weight_grad = call(
                last_weight_kernel, struct((depth, block), F32), [VMEM] * 5,
                [
                    pltpu.VMEM((depth // height, height, block), F32),
                    pltpu.SemaphoreType.DMA((depth // height,)),
                ],
                pl.BlockSpec(memory_space=pl.ANY),
            )(*operands)
    received, weight_grad = lax.optimization_barrier((received, weight_grad))
    total = keep[0]
    for array in received:
        total = total + array.astype(F32)
    view_other = swap(total[own:], "dp", CORE)
    image_grad = call(join_kernel, struct((own, views, depth), F32), [SMEM] + [VMEM] * 2)(
        me, total[:own], view_other
    )
    return (image_grad, weight_grad)


def solution(mesh):
    return jax.shard_map(
        shards,
        mesh=mesh,
        in_specs=(P(("rep", "dp"), None, None), P(None, "dp")),
        out_specs=(P(("rep", "dp"), None, None), P(None, "dp")),
        check_vma=False,
    )
```

```python
import functools

import jax
import jax.numpy as jnp
from jax import lax
from jax.experimental import pallas as pl
from jax.experimental.pallas import tpu as pltpu
from jax.sharding import PartitionSpec as P

invariance_weight = 25.0
variance_weight = 25.0
covariance_weight = 1.0
loss_scale = 8192.0
epsilon_var = 0.0001

F32 = jnp.float32
BF16 = jnp.bfloat16
VMEM = pl.BlockSpec(memory_space=pltpu.VMEM)
SMEM = pl.BlockSpec(memory_space=pltpu.SMEM)
CORE, ACROSS, QUAD = 1, 2, 4
EXTRA = 8


def swap(block, axis, bits):
    return lax.ppermute(block, axis, [(i, i ^ bits) for i in range(lax.axis_size(axis))])


def centre(z):
    return z - jnp.mean(z, axis=0, keepdims=True)


def nt_dot(a, b):
    return lax.dot_general(a, b, (((1,), (1,)), ((), ())), preferred_element_type=F32)


def half_masks(half, count):
    row = lax.broadcasted_iota(jnp.int32, (half, count), 0)
    lane = lax.broadcasted_iota(jnp.int32, (half, count), 1)
    return (lane < half) & (row < lane), row == lane, lane < half


def whole(near_ref, far_ref):
    return jnp.concatenate([near_ref[...], far_ref[...]], axis=0)


def pick(me_ref, images_ref):
    images = images_ref[...].astype(F32)
    return jnp.where(me_ref[0] % 2 == 1, images[:, 1, :], images[:, 0, :])


def pick_kernel(me_ref, images_ref, rows_ref):
    rows_ref[...] = pick(me_ref, images_ref)


def pair_kernel(me_ref, rows_ref, images_ref, both_ref):
    rows = pick(me_ref, images_ref)
    both_ref[...] = jnp.concatenate([rows_ref[...], rows], axis=0).astype(BF16)


def turn_kernel(wide_ref, turned_ref):
    turned_ref[...] = jnp.swapaxes(wide_ref[...], 0, 1)


def gram_kernel(own, me_ref, near_ref, far_ref, c_ref, packed_ref, sorted_ref):
    me = me_ref[0]
    count, width = c_ref.shape
    devices = count // own
    outer = devices // QUAD
    half = count // 2
    centred = centre(whole(near_ref, far_ref)).reshape(devices, own, width)
    for slot in range(devices):
        rel = (slot // 2 % outer) * QUAD + (slot // 2 // outer) * 2 + slot % 2
        sorted_ref[rel ^ me] = centred[slot]
    c = sorted_ref[...].reshape(count, width).astype(BF16)
    c_ref[...] = c
    gram = nt_dot(c, c)
    upper, diagonal, _ = half_masks(half, count)
    turned = pltpu.roll(gram[half:], half, 1)
    packed_ref[:half] = jnp.where(upper, turned, gram[:half])
    second = jnp.sum(jnp.where(diagonal, turned, 0.0), axis=0, keepdims=True)
    packed_ref[half:] = jnp.broadcast_to(second, (EXTRA, count))


def unpack(packed_ref):
    count = packed_ref.shape[1]
    half = count // 2
    upper, diagonal, left = half_masks(half, count)
    top = packed_ref[:half]
    second = packed_ref[half:half + 1]
    mirror = jnp.swapaxes(jnp.concatenate([top, jnp.zeros_like(top)], axis=0), 0, 1)
    first = jnp.where(upper, mirror[:half], top)
    last = jnp.where(diagonal, second, jnp.where(upper, top, mirror[:half]))
    last = jnp.where(left, mirror[half:], pltpu.roll(last, half, 1))
    return first, last


def base_kernel(scale, features, near_ref, far_ref, base_ref):
    count = base_ref.shape[0]
    coeff = scale * 4.0 * covariance_weight / (features * (count - 1))
    centred = centre(whole(near_ref, far_ref))
    variance = jnp.sum(centred * centred, axis=0, keepdims=True) / (count - 1)
    spread = jnp.sqrt(variance + epsilon_var)
    wide = centred.astype(BF16).astype(F32)
    diag_cov = jnp.sum(wide * wide, axis=0, keepdims=True) / (count - 1)
    var_coeff = jnp.where(
        spread < 1.0, -scale * variance_weight / (features * (count - 1)) / spread, 0.0
    )
    base_ref[...] = var_coeff * centred - coeff * diag_cov * wide


def grads_kernel(side, scale, features, me_ref, packed_ref, c_ref, z_ref, other_ref, base_ref,
                 w_ref, grad_ref, part_ref, gram_ref):
    me = me_ref[0]
    count = c_ref.shape[0]
    devices, own, _ = gram_ref.shape
    half, width = z_ref.shape
    first, last = unpack(packed_ref)
    gram_ref[:devices // 2] = first.reshape(devices // 2, own, count)
    gram_ref[devices // 2:] = last.reshape(devices // 2, own, count)
    order = [
        high * QUAD + side * ACROSS + core
        for high in range(devices // QUAD) for core in (0, CORE)
    ]
    rest = jnp.concatenate([gram_ref[rel ^ me] for rel in order], axis=0)
    through = 0.0
    for _ in range(2):
        piece = rest.astype(BF16)
        rest = rest - piece.astype(F32)
        through = through + jnp.dot(piece, c_ref[...], preferred_element_type=F32)
    coeff = scale * 4.0 * covariance_weight / (features * (count - 1))
    rows = slice(side * half, (side + 1) * half)
    other = other_ref[rows].reshape(half // (2 * own), 2, own, width)
    other = jnp.concatenate([other[:, 1:], other[:, :1]], axis=1).reshape(half, width)
    inv_term = (z_ref[...] - other) * (scale * 2.0 * invariance_weight / (count * features))
    grad = (inv_term + base_ref[rows] + through * (coeff / (count - 1))).astype(BF16)
    grad_ref[...] = grad
    part = jnp.dot(grad, w_ref[...], preferred_element_type=F32)
    part_ref[...] = part.astype(part_ref.dtype)


def join_kernel(me_ref, own_ref, other_ref, out_ref):
    second = me_ref[0] % 2 == 1
    own, other = own_ref[...], other_ref[...]
    out_ref[:, 0, :] = jnp.where(second, other, own)
    out_ref[:, 1, :] = jnp.where(second, own, other)


def weight_operands(rows_ref, rows_core_ref, grad_ref, grad_core_ref):
    block = grad_core_ref.shape[1]
    rows = jnp.concatenate([rows_ref[...], rows_core_ref[...]], axis=0)
    return rows, jnp.concatenate([grad_ref[:, :block], grad_core_ref[...]], axis=0)


def tn_dot(a, b):
    return lax.dot_general(a, b, (((0,), (0,)), ((), ())), preferred_element_type=F32)


def weight_kernel(*refs):
    part = tn_dot(*weight_operands(*refs[:4]))
    refs[-1][...] = part + refs[4][...] if len(refs) > 5 else part


def last_weight_kernel(*refs):
    *operand_refs, earlier_ref, out_ref, sum_ref, sems = refs
    rows, grads = weight_operands(*operand_refs)
    bands, height, _ = sum_ref.shape
    copies = []
    for i in range(bands):
        band = slice(i * height, (i + 1) * height)
        sum_ref[i] = tn_dot(rows[:, band], grads) + earlier_ref[band]
        copies.append(pltpu.make_async_copy(sum_ref.at[i], out_ref.at[pl.ds(i * height, height)], sems.at[i]))
        copies[-1].start()
    for copy in copies:
        copy.wait()


def call(kernel, out_shape, specs, scratch=(), place=VMEM):
    return pl.pallas_call(
        kernel,
        out_shape=out_shape,
        in_specs=specs,
        out_specs=jax.tree.map(lambda _: place, out_shape),
        scratch_shapes=list(scratch),
        compiler_params=pltpu.CompilerParams(vmem_limit_bytes=32 * 1024 * 1024),
    )


def shards(images, weight):
    groups = lax.axis_size("rep")
    owners = lax.axis_size("dp")
    own, views, depth = images.shape
    block = weight.shape[1]
    width = 2 * block
    features = block * owners
    count = own * owners
    half = count // 2
    lot = 2 * own
    outer = owners // QUAD
    scale = loss_scale / groups
    position = lax.axis_index("dp")
    me = position.reshape(1)
    struct = jax.ShapeDtypeStruct

    def over_rep(array):
        return [
            lax.ppermute(array, "rep", [(i, (i + shift) % groups) for i in range(groups)])
            for shift in range(1, groups)
        ]

    def matmul(rows, matrix):
        return jnp.dot(rows, matrix, preferred_element_type=F32)

    given = swap(images, "dp", CORE)
    mine = call(pick_kernel, struct((own, depth), F32), [SMEM, VMEM])(me, images)
    given, mine, sent = lax.optimization_barrier((given, mine, weight))
    weight_core = swap(sent, "dp", CORE)
    mine = call(pair_kernel, struct((lot, depth), BF16), [SMEM] + [VMEM] * 2)(me, mine, given)
    column = [swap(mine, "dp", high * QUAD) for high in range(1, outer)]
    wide = jnp.concatenate([weight, weight_core], axis=1)
    column, wide = lax.optimization_barrier((column[::-1], wide))
    column = column[::-1]
    column = lax.optimization_barrier(jnp.concatenate([mine] + column, axis=0))
    across = swap(column, "dp", ACROSS)
    near = matmul(column, wide)
    wide_t = call(turn_kernel, struct((width, depth), BF16), [VMEM])(wide)
    wide_t, sent = lax.optimization_barrier((wide_t, column))
    near_others = over_rep(sent)
    near, across = lax.optimization_barrier((near, across))
    far = matmul(across, wide)

    c, packed = call(
        functools.partial(gram_kernel, own),
        (struct((count, width), BF16), struct((half + EXTRA, count), F32)),
        [SMEM] + [VMEM] * 2,
        [pltpu.VMEM((owners, own, width), F32)],
    )(me, near, far)

    along = swap(packed, "dp", ACROSS)
    along, wide_t, near_others = lax.optimization_barrier((along, wide_t, near_others))
    packed = packed + along
    packed, near_late, far_late, rows = lax.optimization_barrier(
        (packed, near, far, jnp.concatenate([column, across], axis=0))
    )
    rows_core = swap(rows, "dp", CORE)
    base = call(
        functools.partial(base_kernel, scale, features), struct((count, width), F32), [VMEM] * 2
    )(near_late, far_late)
    base, sent = lax.optimization_barrier((base, across))
    far_others = over_rep(sent)
    other = matmul(rows_core, wide)
    received = [swap(packed, "dp", high * QUAD) for high in range(outer - 1, 0, -1)]
    received, other, base = lax.optimization_barrier((received, other, base))
    packed = (packed + received[-1]) + functools.reduce(jnp.add, received[:-1])

    def grads(side, z, kind):
        return call(
            functools.partial(grads_kernel, side, scale, features),
            (struct((half, width), BF16), struct((half, depth), kind)),
            [SMEM] + [VMEM] * 6,
            [pltpu.VMEM((owners, own, count), F32)],
        )(me, packed, c, z, other, base, wide_t)

    grad_far, send = grads(1, far, BF16)

    def weight_part(*operands):
        return call(weight_kernel, struct((depth, block), F32), [VMEM] * len(operands))(*operands)

    received = swap(send, "dp", ACROSS)
    _, late = lax.optimization_barrier((send, near))
    grad_near, keep = grads(0, late, F32)
    grad = jnp.concatenate([grad_near, grad_far], axis=0)
    grad_core = swap(grad[:, block:], "dp", CORE)
    keep, grad = lax.optimization_barrier((keep, grad))
    grad = grad[:, :block]
    grad_others, grad_core_others = over_rep(grad), over_rep(grad_core)
    keep = keep + received.astype(F32)
    keep, far_others = lax.optimization_barrier((keep, far_others))
    rows_others = [jnp.concatenate(pair, axis=0) for pair in zip(near_others, far_others)]
    keep = keep.reshape(outer, lot, depth)
    received = [
        swap(keep[high].astype(BF16), "dp", high * QUAD) for high in range(outer - 1, 0, -1)
    ]
    grad, grad_others, grad_core_others = lax.optimization_barrier(
        (grad, grad_others, grad_core_others)
    )
    weight_grad = weight_part(rows, rows_core, grad, grad_core)
    height = min(depth, 256)
    for left, (theirs, theirs_grad) in enumerate(zip(rows_others, grad_others), 2 - groups):
        operands = [
            theirs, swap(theirs, "dp", CORE),
            theirs_grad, grad_core_others.pop(0), weight_grad,
        ]
        if left < 0:
            weight_grad = weight_part(*operands)
        else:
            weight_grad = call(
                last_weight_kernel, struct((depth, block), F32), [VMEM] * 5,
                [
                    pltpu.VMEM((depth // height, height, block), F32),
                    pltpu.SemaphoreType.DMA((depth // height,)),
                ],
                pl.BlockSpec(memory_space=pl.ANY),
            )(*operands)
    received, weight_grad = lax.optimization_barrier((received, weight_grad))
    total = keep[0]
    for array in received:
        total = total + array.astype(F32)
    view_other = swap(total[own:], "dp", CORE)
    image_grad = call(join_kernel, struct((own, views, depth), F32), [SMEM] + [VMEM] * 2)(
        me, total[:own], view_other
    )
    return (image_grad, weight_grad)


def solution(mesh):
    return jax.shard_map(
        shards,
        mesh=mesh,
        in_specs=(P(("rep", "dp"), None, None), P(None, "dp")),
        out_specs=(P(("rep", "dp"), None, None), P(None, "dp")),
        check_vma=False,
    )
```

```python
import functools

import jax
import jax.numpy as jnp
from jax import lax
from jax.experimental import pallas as pl
from jax.experimental.pallas import tpu as pltpu
from jax.sharding import PartitionSpec as P

invariance_weight = 25.0
variance_weight = 25.0
covariance_weight = 1.0
loss_scale = 8192.0
epsilon_var = 0.0001

F32 = jnp.float32
BF16 = jnp.bfloat16
VMEM = pl.BlockSpec(memory_space=pltpu.VMEM)
SMEM = pl.BlockSpec(memory_space=pltpu.SMEM)
CORE, ACROSS, QUAD = 1, 2, 4
EXTRA = 8


def swap(block, axis, bits):
    return lax.ppermute(block, axis, [(i, i ^ bits) for i in range(lax.axis_size(axis))])


def centre(z):
    return z - jnp.mean(z, axis=0, keepdims=True)


def nt_dot(a, b):
    return lax.dot_general(a, b, (((1,), (1,)), ((), ())), preferred_element_type=F32)


def half_masks(half, count):
    row = lax.broadcasted_iota(jnp.int32, (half, count), 0)
    lane = lax.broadcasted_iota(jnp.int32, (half, count), 1)
    return (lane < half) & (row < lane), row == lane, lane < half


def whole(near_ref, far_ref):
    return jnp.concatenate([near_ref[...], far_ref[...]], axis=0)


def pick(me_ref, images_ref):
    images = images_ref[...].astype(F32)
    return jnp.where(me_ref[0] % 2 == 1, images[:, 1, :], images[:, 0, :])


def pick_kernel(me_ref, images_ref, rows_ref):
    rows_ref[...] = pick(me_ref, images_ref)


def pair_kernel(me_ref, rows_ref, images_ref, both_ref):
    rows = pick(me_ref, images_ref)
    both_ref[...] = jnp.concatenate([rows_ref[...], rows], axis=0).astype(BF16)


def turn_kernel(wide_ref, turned_ref):
    turned_ref[...] = jnp.swapaxes(wide_ref[...], 0, 1)


def gram_kernel(own, me_ref, near_ref, far_ref, c_ref, packed_ref, sorted_ref):
    me = me_ref[0]
    count, width = c_ref.shape
    devices = count // own
    outer = devices // QUAD
    half = count // 2
    centred = centre(whole(near_ref, far_ref)).reshape(devices, own, width)
    for slot in range(devices):
        rel = (slot // 2 % outer) * QUAD + (slot // 2 // outer) * 2 + slot % 2
        sorted_ref[rel ^ me] = centred[slot]
    c = sorted_ref[...].reshape(count, width).astype(BF16)
    c_ref[...] = c
    gram = nt_dot(c, c)
    upper, diagonal, _ = half_masks(half, count)
    turned = pltpu.roll(gram[half:], half, 1)
    packed_ref[:half] = jnp.where(upper, turned, gram[:half])
    second = jnp.sum(jnp.where(diagonal, turned, 0.0), axis=0, keepdims=True)
    packed_ref[half:] = jnp.broadcast_to(second, (EXTRA, count))


def unpack(packed_ref):
    count = packed_ref.shape[1]
    half = count // 2
    upper, diagonal, left = half_masks(half, count)
    top = packed_ref[:half]
    second = packed_ref[half:half + 1]
    mirror = jnp.swapaxes(jnp.concatenate([top, jnp.zeros_like(top)], axis=0), 0, 1)
    first = jnp.where(upper, mirror[:half], top)
    last = jnp.where(diagonal, second, jnp.where(upper, top, mirror[:half]))
    last = jnp.where(left, mirror[half:], pltpu.roll(last, half, 1))
    return first, last


def base_kernel(scale, features, near_ref, far_ref, base_ref):
    count = base_ref.shape[0]
    coeff = scale * 4.0 * covariance_weight / (features * (count - 1))
    centred = centre(whole(near_ref, far_ref))
    variance = jnp.sum(centred * centred, axis=0, keepdims=True) / (count - 1)
    spread = jnp.sqrt(variance + epsilon_var)
    wide = centred.astype(BF16).astype(F32)
    diag_cov = jnp.sum(wide * wide, axis=0, keepdims=True) / (count - 1)
    var_coeff = jnp.where(
        spread < 1.0, -scale * variance_weight / (features * (count - 1)) / spread, 0.0
    )
    base_ref[...] = var_coeff * centred - coeff * diag_cov * wide


def grads_kernel(side, scale, features, me_ref, packed_ref, c_ref, z_ref, other_ref, base_ref,
                 w_ref, grad_ref, part_ref, gram_ref):
    me = me_ref[0]
    count = c_ref.shape[0]
    devices, own, _ = gram_ref.shape
    half, width = z_ref.shape
    first, last = unpack(packed_ref)
    gram_ref[:devices // 2] = first.reshape(devices // 2, own, count)
    gram_ref[devices // 2:] = last.reshape(devices // 2, own, count)
    order = [
        high * QUAD + side * ACROSS + core
        for high in range(devices // QUAD) for core in (0, CORE)
    ]
    rest = jnp.concatenate([gram_ref[rel ^ me] for rel in order], axis=0)
    through = 0.0
    for _ in range(2):
        piece = rest.astype(BF16)
        rest = rest - piece.astype(F32)
        through = through + jnp.dot(piece, c_ref[...], preferred_element_type=F32)
    coeff = scale * 4.0 * covariance_weight / (features * (count - 1))
    rows = slice(side * half, (side + 1) * half)
    other = other_ref[rows].reshape(half // (2 * own), 2, own, width)
    other = jnp.concatenate([other[:, 1:], other[:, :1]], axis=1).reshape(half, width)
    inv_term = (z_ref[...] - other) * (scale * 2.0 * invariance_weight / (count * features))
    grad = (inv_term + base_ref[rows] + through * (coeff / (count - 1))).astype(BF16)
    grad_ref[...] = grad
    part = jnp.dot(grad, w_ref[...], preferred_element_type=F32)
    part_ref[...] = part.astype(part_ref.dtype)


def join_kernel(me_ref, own_ref, other_ref, out_ref):
    second = me_ref[0] % 2 == 1
    own, other = own_ref[...], other_ref[...]
    out_ref[:, 0, :] = jnp.where(second, other, own)
    out_ref[:, 1, :] = jnp.where(second, own, other)


def weight_operands(rows_ref, rows_core_ref, grad_ref, grad_core_ref):
    block = grad_core_ref.shape[1]
    rows = jnp.concatenate([rows_ref[...], rows_core_ref[...]], axis=0)
    return rows, jnp.concatenate([grad_ref[:, :block], grad_core_ref[...]], axis=0)


def tn_dot(a, b):
    return lax.dot_general(a, b, (((0,), (0,)), ((), ())), preferred_element_type=F32)


def weight_kernel(*refs):
    part = tn_dot(*weight_operands(*refs[:4]))
    refs[-1][...] = part + refs[4][...] if len(refs) > 5 else part


def last_weight_kernel(*refs):
    *operand_refs, earlier_ref, out_ref, sum_ref, sems = refs
    rows, grads = weight_operands(*operand_refs)
    bands, height, _ = sum_ref.shape
    copies = []
    for i in range(bands):
        band = slice(i * height, (i + 1) * height)
        sum_ref[i] = tn_dot(rows[:, band], grads) + earlier_ref[band]
        copies.append(pltpu.make_async_copy(sum_ref.at[i], out_ref.at[pl.ds(i * height, height)], sems.at[i]))
        copies[-1].start()
    for copy in copies:
        copy.wait()


def call(kernel, out_shape, specs, scratch=(), place=VMEM):
    return pl.pallas_call(
        kernel,
        out_shape=out_shape,
        in_specs=specs,
        out_specs=jax.tree.map(lambda _: place, out_shape),
        scratch_shapes=list(scratch),
        compiler_params=pltpu.CompilerParams(vmem_limit_bytes=32 * 1024 * 1024),
    )


def shards(images, weight):
    groups = lax.axis_size("rep")
    owners = lax.axis_size("dp")
    own, views, depth = images.shape
    block = weight.shape[1]
    width = 2 * block
    features = block * owners
    count = own * owners
    half = count // 2
    lot = 2 * own
    outer = owners // QUAD
    scale = loss_scale / groups
    position = lax.axis_index("dp")
    me = position.reshape(1)
    struct = jax.ShapeDtypeStruct

    def over_rep(array):
        return [
            lax.ppermute(array, "rep", [(i, (i + shift) % groups) for i in range(groups)])
            for shift in range(1, groups)
        ]

    def matmul(rows, matrix):
        return jnp.dot(rows, matrix, preferred_element_type=F32)

    given = swap(images, "dp", CORE)
    mine = call(pick_kernel, struct((own, depth), F32), [SMEM, VMEM])(me, images)
    given, mine, sent = lax.optimization_barrier((given, mine, weight))
    weight_core = swap(sent, "dp", CORE)
    mine = call(pair_kernel, struct((lot, depth), BF16), [SMEM] + [VMEM] * 2)(me, mine, given)
    column = [swap(mine, "dp", high * QUAD) for high in range(1, outer)]
    wide = jnp.concatenate([weight, weight_core], axis=1)
    column, wide = lax.optimization_barrier((column[::-1], wide))
    column = column[::-1]
    column = lax.optimization_barrier(jnp.concatenate([mine] + column, axis=0))
    across = swap(column, "dp", ACROSS)
    near = matmul(column, wide)
    wide_t = call(turn_kernel, struct((width, depth), BF16), [VMEM])(wide)
    wide_t, sent = lax.optimization_barrier((wide_t, column))
    near_others = over_rep(sent)
    near, across = lax.optimization_barrier((near, across))
    far = matmul(across, wide)

    c, packed = call(
        functools.partial(gram_kernel, own),
        (struct((count, width), BF16), struct((half + EXTRA, count), F32)),
        [SMEM] + [VMEM] * 2,
        [pltpu.VMEM((owners, own, width), F32)],
    )(me, near, far)

    along = swap(packed, "dp", ACROSS)
    along, wide_t, near_others = lax.optimization_barrier((along, wide_t, near_others))
    packed = packed + along
    packed, near_late, far_late, rows = lax.optimization_barrier(
        (packed, near, far, jnp.concatenate([column, across], axis=0))
    )
    rows_core = swap(rows, "dp", CORE)
    base = call(
        functools.partial(base_kernel, scale, features), struct((count, width), F32), [VMEM] * 2
    )(near_late, far_late)
    base, sent = lax.optimization_barrier((base, across))
    far_others = over_rep(sent)
    other = matmul(rows_core, wide)
    received = [swap(packed, "dp", high * QUAD) for high in range(1, outer)]
    received, other, base = lax.optimization_barrier((received, other, base))
    packed = (packed + received[0]) + functools.reduce(jnp.add, received[1:])

    def grads(side, z, kind):
        return call(
            functools.partial(grads_kernel, side, scale, features),
            (struct((half, width), BF16), struct((half, depth), kind)),
            [SMEM] + [VMEM] * 6,
            [pltpu.VMEM((owners, own, count), F32)],
        )(me, packed, c, z, other, base, wide_t)

    grad_far, send = grads(1, far, BF16)

    def weight_part(*operands):
        return call(weight_kernel, struct((depth, block), F32), [VMEM] * len(operands))(*operands)

    received = swap(send, "dp", ACROSS)
    _, late = lax.optimization_barrier((send, near))
    grad_near, keep = grads(0, late, F32)
    grad = jnp.concatenate([grad_near, grad_far], axis=0)
    grad_core = swap(grad[:, block:], "dp", CORE)
    keep, grad = lax.optimization_barrier((keep, grad))
    grad = grad[:, :block]
    grad_others, grad_core_others = over_rep(grad), over_rep(grad_core)
    keep = keep + received.astype(F32)
    keep, far_others = lax.optimization_barrier((keep, far_others))
    rows_others = [jnp.concatenate(pair, axis=0) for pair in zip(near_others, far_others)]
    keep = keep.reshape(outer, lot, depth)
    received = [
        swap(keep[high].astype(BF16), "dp", high * QUAD) for high in range(outer - 1, 0, -1)
    ]
    grad, grad_others, grad_core_others = lax.optimization_barrier(
        (grad, grad_others, grad_core_others)
    )
    weight_grad = weight_part(rows, rows_core, grad, grad_core)
    height = min(depth, 256)
    for left, (theirs, theirs_grad) in enumerate(zip(rows_others, grad_others), 2 - groups):
        operands = [
            theirs, swap(theirs, "dp", CORE),
            theirs_grad, grad_core_others.pop(0), weight_grad,
        ]
        if left < 0:
            weight_grad = weight_part(*operands)
        else:
            weight_grad = call(
                last_weight_kernel, struct((depth, block), F32), [VMEM] * 5,
                [
                    pltpu.VMEM((depth // height, height, block), F32),
                    pltpu.SemaphoreType.DMA((depth // height,)),
                ],
                pl.BlockSpec(memory_space=pl.ANY),
            )(*operands)
    received, weight_grad = lax.optimization_barrier((received, weight_grad))
    total = keep[0]
    for array in received:
        total = total + array.astype(F32)
    view_other = swap(total[own:], "dp", CORE)
    image_grad = call(join_kernel, struct((own, views, depth), F32), [SMEM] + [VMEM] * 2)(
        me, total[:own], view_other
    )
    return (image_grad, weight_grad)


def solution(mesh):
    return jax.shard_map(
        shards,
        mesh=mesh,
        in_specs=(P(("rep", "dp"), None, None), P(None, "dp")),
        out_specs=(P(("rep", "dp"), None, None), P(None, "dp")),
        check_vma=False,
    )
```

```python
import functools

import jax
import jax.numpy as jnp
from jax import lax
from jax.experimental import pallas as pl
from jax.experimental.pallas import tpu as pltpu
from jax.sharding import PartitionSpec as P

invariance_weight = 25.0
variance_weight = 25.0
covariance_weight = 1.0
loss_scale = 8192.0
epsilon_var = 0.0001

F32 = jnp.float32
BF16 = jnp.bfloat16
VMEM = pl.BlockSpec(memory_space=pltpu.VMEM)
SMEM = pl.BlockSpec(memory_space=pltpu.SMEM)
CORE, ACROSS, QUAD = 1, 2, 4
EXTRA = 8


def swap(block, axis, bits):
    return lax.ppermute(block, axis, [(i, i ^ bits) for i in range(lax.axis_size(axis))])


def centre(z):
    return z - jnp.mean(z, axis=0, keepdims=True)


def nt_dot(a, b):
    return lax.dot_general(a, b, (((1,), (1,)), ((), ())), preferred_element_type=F32)


def half_masks(half, count):
    row = lax.broadcasted_iota(jnp.int32, (half, count), 0)
    lane = lax.broadcasted_iota(jnp.int32, (half, count), 1)
    return (lane < half) & (row < lane), row == lane, lane < half


def whole(near_ref, far_ref):
    return jnp.concatenate([near_ref[...], far_ref[...]], axis=0)


def pick(me_ref, images_ref):
    images = images_ref[...].astype(F32)
    return jnp.where(me_ref[0] % 2 == 1, images[:, 1, :], images[:, 0, :])


def pick_kernel(me_ref, images_ref, rows_ref):
    rows_ref[...] = pick(me_ref, images_ref)


def pair_kernel(me_ref, rows_ref, images_ref, both_ref):
    rows = pick(me_ref, images_ref)
    both_ref[...] = jnp.concatenate([rows_ref[...], rows], axis=0).astype(BF16)


def turn_kernel(wide_ref, turned_ref):
    turned_ref[...] = jnp.swapaxes(wide_ref[...], 0, 1)


def gram_kernel(own, me_ref, near_ref, far_ref, c_ref, packed_ref, sorted_ref):
    me = me_ref[0]
    count, width = c_ref.shape
    devices = count // own
    outer = devices // QUAD
    half = count // 2
    centred = centre(whole(near_ref, far_ref)).reshape(devices, own, width)
    for slot in range(devices):
        rel = (slot // 2 % outer) * QUAD + (slot // 2 // outer) * 2 + slot % 2
        sorted_ref[rel ^ me] = centred[slot]
    c = sorted_ref[...].reshape(count, width).astype(BF16)
    c_ref[...] = c
    gram = nt_dot(c, c)
    upper, diagonal, _ = half_masks(half, count)
    turned = pltpu.roll(gram[half:], half, 1)
    packed_ref[:half] = jnp.where(upper, turned, gram[:half])
    second = jnp.sum(jnp.where(diagonal, turned, 0.0), axis=0, keepdims=True)
    packed_ref[half:] = jnp.broadcast_to(second, (EXTRA, count))


def unpack(packed_ref):
    count = packed_ref.shape[1]
    half = count // 2
    upper, diagonal, left = half_masks(half, count)
    top = packed_ref[:half]
    second = packed_ref[half:half + 1]
    mirror = jnp.swapaxes(jnp.concatenate([top, jnp.zeros_like(top)], axis=0), 0, 1)
    first = jnp.where(upper, mirror[:half], top)
    last = jnp.where(diagonal, second, jnp.where(upper, top, mirror[:half]))
    last = jnp.where(left, mirror[half:], pltpu.roll(last, half, 1))
    return first, last


def base_kernel(scale, features, near_ref, far_ref, base_ref):
    count = base_ref.shape[0]
    coeff = scale * 4.0 * covariance_weight / (features * (count - 1))
    centred = centre(whole(near_ref, far_ref))
    variance = jnp.sum(centred * centred, axis=0, keepdims=True) / (count - 1)
    spread = jnp.sqrt(variance + epsilon_var)
    wide = centred.astype(BF16).astype(F32)
    diag_cov = jnp.sum(wide * wide, axis=0, keepdims=True) / (count - 1)
    var_coeff = jnp.where(
        spread < 1.0, -scale * variance_weight / (features * (count - 1)) / spread, 0.0
    )
    base_ref[...] = var_coeff * centred - coeff * diag_cov * wide


def grads_kernel(side, scale, features, me_ref, packed_ref, c_ref, z_ref, other_ref, base_ref,
                 w_ref, grad_ref, part_ref, gram_ref):
    me = me_ref[0]
    count = c_ref.shape[0]
    devices, own, _ = gram_ref.shape
    half, width = z_ref.shape
    first, last = unpack(packed_ref)
    gram_ref[:devices // 2] = first.reshape(devices // 2, own, count)
    gram_ref[devices // 2:] = last.reshape(devices // 2, own, count)
    order = [
        high * QUAD + side * ACROSS + core
        for high in range(devices // QUAD) for core in (0, CORE)
    ]
    rest = jnp.concatenate([gram_ref[rel ^ me] for rel in order], axis=0)
    through = 0.0
    for _ in range(2):
        piece = rest.astype(BF16)
        rest = rest - piece.astype(F32)
        through = through + jnp.dot(piece, c_ref[...], preferred_element_type=F32)
    coeff = scale * 4.0 * covariance_weight / (features * (count - 1))
    rows = slice(side * half, (side + 1) * half)
    other = other_ref[rows].reshape(half // (2 * own), 2, own, width)
    other = jnp.concatenate([other[:, 1:], other[:, :1]], axis=1).reshape(half, width)
    inv_term = (z_ref[...] - other) * (scale * 2.0 * invariance_weight / (count * features))
    grad = (inv_term + base_ref[rows] + through * (coeff / (count - 1))).astype(BF16)
    grad_ref[...] = grad
    part = jnp.dot(grad, w_ref[...], preferred_element_type=F32)
    part_ref[...] = part.astype(part_ref.dtype)


def join_kernel(me_ref, own_ref, other_ref, out_ref):
    second = me_ref[0] % 2 == 1
    own, other = own_ref[...], other_ref[...]
    out_ref[:, 0, :] = jnp.where(second, other, own)
    out_ref[:, 1, :] = jnp.where(second, own, other)


def weight_operands(rows_ref, rows_core_ref, grad_ref, grad_core_ref):
    block = grad_core_ref.shape[1]
    rows = jnp.concatenate([rows_ref[...], rows_core_ref[...]], axis=0)
    return rows, jnp.concatenate([grad_ref[:, :block], grad_core_ref[...]], axis=0)


def tn_dot(a, b):
    return lax.dot_general(a, b, (((0,), (0,)), ((), ())), preferred_element_type=F32)


def weight_kernel(*refs):
    part = tn_dot(*weight_operands(*refs[:4]))
    refs[-1][...] = part + refs[4][...] if len(refs) > 5 else part


def last_weight_kernel(*refs):
    *operand_refs, earlier_ref, out_ref, sum_ref, sems = refs
    rows, grads = weight_operands(*operand_refs)
    bands, height, _ = sum_ref.shape
    copies = []
    for i in range(bands):
        band = slice(i * height, (i + 1) * height)
        sum_ref[i] = tn_dot(rows[:, band], grads) + earlier_ref[band]
        copies.append(pltpu.make_async_copy(sum_ref.at[i], out_ref.at[pl.ds(i * height, height)], sems.at[i]))
        copies[-1].start()
    for copy in copies:
        copy.wait()


def call(kernel, out_shape, specs, scratch=(), place=VMEM):
    return pl.pallas_call(
        kernel,
        out_shape=out_shape,
        in_specs=specs,
        out_specs=jax.tree.map(lambda _: place, out_shape),
        scratch_shapes=list(scratch),
        compiler_params=pltpu.CompilerParams(vmem_limit_bytes=32 * 1024 * 1024),
    )


def shards(images, weight):
    groups = lax.axis_size("rep")
    owners = lax.axis_size("dp")
    own, views, depth = images.shape
    block = weight.shape[1]
    width = 2 * block
    features = block * owners
    count = own * owners
    half = count // 2
    lot = 2 * own
    outer = owners // QUAD
    scale = loss_scale / groups
    position = lax.axis_index("dp")
    me = position.reshape(1)
    struct = jax.ShapeDtypeStruct

    def over_rep(array):
        return [
            lax.ppermute(array, "rep", [(i, (i + shift) % groups) for i in range(groups)])
            for shift in range(1, groups)
        ]

    def matmul(rows, matrix):
        return jnp.dot(rows, matrix, preferred_element_type=F32)

    given = swap(images, "dp", CORE)
    mine = call(pick_kernel, struct((own, depth), F32), [SMEM, VMEM])(me, images)
    given, mine, sent = lax.optimization_barrier((given, mine, weight))
    weight_core = swap(sent, "dp", CORE)
    mine = call(pair_kernel, struct((lot, depth), BF16), [SMEM] + [VMEM] * 2)(me, mine, given)
    column = [swap(mine, "dp", high * QUAD) for high in range(1, outer)]
    wide = jnp.concatenate([weight, weight_core], axis=1)
    column, wide = lax.optimization_barrier((column[::-1], wide))
    column = column[::-1]
    column = lax.optimization_barrier(jnp.concatenate([mine] + column, axis=0))
    across = swap(column, "dp", ACROSS)
    near = matmul(column, wide)
    wide_t = call(turn_kernel, struct((width, depth), BF16), [VMEM])(wide)
    wide_t, sent = lax.optimization_barrier((wide_t, column))
    near_others = over_rep(sent)
    near, across = lax.optimization_barrier((near, across))
    far = matmul(across, wide)

    c, packed = call(
        functools.partial(gram_kernel, own),
        (struct((count, width), BF16), struct((half + EXTRA, count), F32)),
        [SMEM] + [VMEM] * 2,
        [pltpu.VMEM((owners, own, width), F32)],
    )(me, near, far)

    top = owners // 2
    along, beside, corner = (swap(packed, "dp", bits) for bits in (ACROSS, top, ACROSS | top))
    corner, beside, along, wide_t = lax.optimization_barrier((corner, beside, along, wide_t))
    along, near_others = lax.optimization_barrier((along, near_others))
    packed = (packed + along) + (beside + corner)
    packed, near_late, far_late, rows = lax.optimization_barrier(
        (packed, near, far, jnp.concatenate([column, across], axis=0))
    )
    rows_core = swap(rows, "dp", CORE)
    base = call(
        functools.partial(base_kernel, scale, features), struct((count, width), F32), [VMEM] * 2
    )(near_late, far_late)
    base, sent = lax.optimization_barrier((base, across))
    far_others = over_rep(sent)
    other = matmul(rows_core, wide)
    bit = QUAD
    while bit < top:
        received = swap(packed, "dp", bit)
        received, other, base = lax.optimization_barrier((received, other, base))
        packed = packed + received
        bit *= 2

    def grads(side, z, kind):
        return call(
            functools.partial(grads_kernel, side, scale, features),
            (struct((half, width), BF16), struct((half, depth), kind)),
            [SMEM] + [VMEM] * 6,
            [pltpu.VMEM((owners, own, count), F32)],
        )(me, packed, c, z, other, base, wide_t)

    grad_far, send = grads(1, far, BF16)

    def weight_part(*operands):
        return call(weight_kernel, struct((depth, block), F32), [VMEM] * len(operands))(*operands)

    received = swap(send, "dp", ACROSS)
    _, late = lax.optimization_barrier((send, near))
    grad_near, keep = grads(0, late, F32)
    grad = jnp.concatenate([grad_near, grad_far], axis=0)
    grad_core = swap(grad[:, block:], "dp", CORE)
    keep, grad = lax.optimization_barrier((keep, grad))
    grad = grad[:, :block]
    grad_others, grad_core_others = over_rep(grad), over_rep(grad_core)
    keep = keep + received.astype(F32)
    keep, far_others = lax.optimization_barrier((keep, far_others))
    rows_others = [jnp.concatenate(pair, axis=0) for pair in zip(near_others, far_others)]
    keep = keep.reshape(outer, lot, depth)
    received = [
        swap(keep[high].astype(BF16), "dp", high * QUAD) for high in range(outer - 1, 0, -1)
    ]
    grad, grad_others, grad_core_others = lax.optimization_barrier(
        (grad, grad_others, grad_core_others)
    )
    weight_grad = weight_part(rows, rows_core, grad, grad_core)
    height = min(depth, 128)
    for left, (theirs, theirs_grad) in enumerate(zip(rows_others, grad_others), 2 - groups):
        operands = [
            theirs, swap(theirs, "dp", CORE),
            theirs_grad, grad_core_others.pop(0), weight_grad,
        ]
        if left < 0:
            weight_grad = weight_part(*operands)
        else:
            weight_grad = call(
                last_weight_kernel, struct((depth, block), F32), [VMEM] * 5,
                [
                    pltpu.VMEM((depth // height, height, block), F32),
                    pltpu.SemaphoreType.DMA((depth // height,)),
                ],
                pl.BlockSpec(memory_space=pl.ANY),
            )(*operands)
    received, weight_grad = lax.optimization_barrier((received, weight_grad))
    total = keep[0]
    for array in received:
        total = total + array.astype(F32)
    view_other = swap(total[own:], "dp", CORE)
    image_grad = call(join_kernel, struct((own, views, depth), F32), [SMEM] + [VMEM] * 2)(
        me, total[:own], view_other
    )
    return (image_grad, weight_grad)


def solution(mesh):
    return jax.shard_map(
        shards,
        mesh=mesh,
        in_specs=(P(("rep", "dp"), None, None), P(None, "dp")),
        out_specs=(P(("rep", "dp"), None, None), P(None, "dp")),
        check_vma=False,
    )
```
